32 devices in a mesh: fsdp: 2 (over y), ctx: 16 (over z, x, core).
Axes of the slice: x: 2, y: 2, z: 4, core: 2. Of those that a mesh axis runs over, the one named last changes fastest.
Arguments:
- tokens: bfloat16 [3, 2, 2048, 768], P(None, 'fsdp', 'ctx'), may hold values from -6 to 6
- cotangent: bfloat16 [3, 2, 2048, 768], P(None, 'fsdp', 'ctx'), may hold values from -6 to 6
- segment_ids: int32 [3, 2, 2048], P(None, 'fsdp', 'ctx'), may hold values from 0 to 15, never falling along the last dimension, each value on 1 to 1024 neighbouring positions
- q_weight: bfloat16 [192, 768], P('fsdp'), may hold values from -0.4375 to 0.4375
- key_weight: bfloat16 [192, 768], P('fsdp'), may hold values from -0.4375 to 0.4375
- value_weight: bfloat16 [192, 768], P('fsdp'), may hold values from -0.4375 to 0.4375
- q_bias: bfloat16 [768], P('fsdp'), may hold values from -4 to 4
- value_bias: bfloat16 [768], P('fsdp'), may hold values from -1.5 to 1.5
- out_weight: bfloat16 [768, 768], P('fsdp'), may hold values from -1.25 to 1.25
- out_bias: bfloat16 [768], P('fsdp'), may hold values from -1.5 to 1.5
- norm1_gain: bfloat16 [768], P('fsdp'), may hold values from 0.5 to 1.5
- norm1_bias: bfloat16 [768], P('fsdp'), may hold values from -1.5 to 1.5
- inter_weight: bfloat16 [192, 3072], P('fsdp'), may hold values from -0.4375 to 0.4375
- inter_bias: bfloat16 [3072], P('fsdp'), may hold values from -1.5 to 1.5
- ffo_weight: bfloat16 [768, 768], P('fsdp'), may hold values from -0.21875 to 0.21875
- ffo_bias: bfloat16 [768], P('fsdp'), may hold values from -1.5 to 1.5
- norm2_gain: bfloat16 [768], P('fsdp'), may hold values from 0.5 to 1.5
- norm2_bias: bfloat16 [768], P('fsdp'), may hold values from -1.5 to 1.5
Outputs:
- out: bfloat16 [3, 2, 2048, 768], P(None, 'fsdp', 'ctx')
- tokens_grad: bfloat16 [3, 2, 2048, 768], P(None, 'fsdp', 'ctx')
- q_weight_grad: float32 [192, 768], P('fsdp')
- key_weight_grad: float32 [192, 768], P('fsdp')
- value_weight_grad: float32 [192, 768], P('fsdp')
- q_bias_grad: float32 [768], P('fsdp')
- value_bias_grad: float32 [768], P('fsdp')
- out_weight_grad: float32 [768, 768], P('fsdp')
- out_bias_grad: float32 [768], P('fsdp')
- norm1_gain_grad: float32 [768], P('fsdp')
- norm1_bias_grad: float32 [768], P('fsdp')
- inter_weight_grad: float32 [192, 3072], P('fsdp')
- inter_bias_grad: float32 [3072], P('fsdp')
- ffo_weight_grad: float32 [768, 768], P('fsdp')
- ffo_bias_grad: float32 [768], P('fsdp')
- norm2_gain_grad: float32 [768], P('fsdp')
- norm2_bias_grad: float32 [768], P('fsdp')
The draws below stay inside these ranges and needn't reach their ends.
Inputs may be any that keep to these rules, and one draw needn't show every extreme that they name: `segment_ids`: within each sequence the segment numbers never fall; each of the 16 numbers is used, every document has 1 to 1024 tokens, and one has exactly 1024.
All inputs are finite; a program needn't handle non-finite values.
Results may differ from the reference program's by a relative error of at most 0.024.
Values may be sent and summed in bfloat16 or wider, within the bound.
A program may use at most 192 MiB of HBM per device.

```python
import math
import jax
import jax.numpy as jnp
import numpy as np
from jax import lax

D = 768
HEADS = 12
HEAD = 64
FF = 3072
GROUPS = 4
GIN = 192
FGIN = 768
MICRO = 3
SPM = 1
TOK_CTX = 128
SEQ = 2048
SEQS_MB = 2
DOCS = 16
LONGEST = 1024
N_FSDP = 2
N_CTX = 16


def draw_tokens(key, part):
    full_shape = (MICRO, SPM * N_FSDP, TOK_CTX * N_CTX, D)
    return jnp.clip(jax.random.normal(key, full_shape, jnp.float32), -6.0, 6.0).astype(jnp.bfloat16)


def block_scale(stream_key, dims, shards, smallest, high):
    level, own = 1.0, jax.random.fold_in(stream_key, 6)
    for axis_at, blocks in shards:
        draws = jnp.exp(jax.random.uniform(jax.random.fold_in(own, axis_at), (blocks,), jnp.float32, smallest / len(shards), high / len(shards)))
        level = level * jnp.repeat(draws, dims[axis_at] // blocks).reshape([-1 if axis == axis_at else 1 for axis in range(len(dims))])
    return level


def split_up(number_of, total, limit, skew):
    portions = [(1 << 20) // math.isqrt(rank ** skew) + 1 for rank in range(2, number_of + 1)]
    spare, counts = total - limit - (number_of - 1), [1] * (number_of - 1)
    while spare > 0:
        movable = [i for i in range(number_of - 1) if counts[i] < limit]
        whole, budget = sum([portions[i] for i in movable]), spare
        for i in movable:
            more = min(limit - counts[i], max(1, budget * portions[i] // whole), spare)
            counts[i] = counts[i] + more
            spare = spare - more
    return np.array([limit] + counts)


def uneven_parts(stream_key, number_of, total, bound, lean):
    if number_of == 2:
        one = jax.random.randint(stream_key, (), max(1, total - bound), min(bound, total - 1) + 1)
        return jnp.stack([one, total - one])
    sizes = jnp.asarray(split_up(number_of, total, bound, lean), jnp.int32)
    couples = (number_of - 1) // 2
    donor, taker = sizes[1:1 + 2 * couples:2], sizes[2:2 + 2 * couples:2]
    slack = jnp.minimum(donor - 1, bound - taker)
    shifted = jax.random.randint(jax.random.fold_in(stream_key, 1), (couples,), 0, 1 << 20) % (slack + 1)
    sizes = sizes.at[1:1 + 2 * couples:2].set(donor - shifted).at[2:2 + 2 * couples:2].set(taker + shifted)
    return sizes[jax.random.permutation(jax.random.fold_in(stream_key, 2), number_of)]


def gaussian(key, extent, spread, reach, cuts=(), dtype=jnp.bfloat16):
    level = block_scale(key, extent, cuts, -0.22, 0.18) if cuts else 1.0
    entries = jax.random.normal(key, extent, jnp.float32) * spread * level
    return jnp.minimum(jnp.maximum(entries, -reach), reach).astype(dtype)


def setup_inputs(seed: int = 0) -> dict:
    splits = jax.random.split(jax.random.key(seed), 19)
    return {
        "tokens": draw_tokens(jax.random.fold_in(splits[18], 71), 0),
        "cotangent": gaussian(splits[1], (MICRO, SEQS_MB, SEQ, D), 1.0, 6.0, ((1, 2), (2, 16))),
        "segment_ids": jax.vmap(lambda own: jnp.searchsorted(jnp.cumsum(uneven_parts(own, DOCS, SEQ, LONGEST, 2)), jnp.arange(SEQ), side="right"))(jax.random.split(splits[2], MICRO * SEQS_MB)).reshape((MICRO, SEQS_MB, SEQ)).astype(jnp.int32),
        "q_weight": gaussian(splits[3], (GIN, D), GIN ** -0.5, 0.4375, ((0, 2),)),
        "key_weight": gaussian(splits[4], (GIN, D), GIN ** -0.5, 0.4375, ((0, 2),)),
        "value_weight": gaussian(splits[5], (GIN, D), GIN ** -0.5, 0.4375, ((0, 2),)),
        "q_bias": gaussian(splits[6], (D,), 0.3, 4.0, ((0, 2),)),
        "value_bias": gaussian(splits[7], (D,), 0.1, 1.5, ((0, 2),)),
        "out_weight": gaussian(splits[8], (D, D), (max(D // 32, 1)) ** -0.5, 1.25, ((0, 2),)),
        "out_bias": gaussian(splits[9], (D,), 0.1, 1.5, ((0, 2),)),
        "norm1_gain": jnp.clip(1.0 + 0.1 * jax.random.normal(splits[10], (D,), jnp.float32), 0.5, 1.5).astype(jnp.bfloat16),
        "norm1_bias": gaussian(splits[11], (D,), 0.1, 1.5, ((0, 2),)),
        "inter_weight": gaussian(splits[12], (GIN, FF), GIN ** -0.5, 0.4375, ((0, 2),)),
        "inter_bias": gaussian(splits[13], (FF,), 0.1, 1.5, ((0, 2),)),
        "ffo_weight": gaussian(splits[14], (FGIN, D), FGIN ** -0.5, 0.21875, ((0, 2),)),
        "ffo_bias": gaussian(splits[15], (D,), 0.1, 1.5, ((0, 2),)),
        "norm2_gain": jnp.clip(1.0 + 0.1 * jax.random.normal(splits[16], (D,), jnp.float32), 0.5, 1.5).astype(jnp.bfloat16),
        "norm2_bias": gaussian(splits[17], (D,), 0.1, 1.5, ((0, 2),)),
    }


NORM_EPS = 1e-12
MASKED = -1000000000.0

@jax.custom_vjp
def low(v):
    return lax.optimization_barrier(v.astype(jnp.bfloat16)).astype(jnp.float32)

@jax.custom_vjp
def low_back(v):
    return v

def low_keep(v):
    return (low(v), None)

def low_pass(kept, grad):
    return (grad,)

def back_keep(v):
    return (v, None)

def back_low(kept, grad):
    return (low(grad),)
low.defvjp(low_keep, low_pass)
low_back.defvjp(back_keep, back_low)

def group_proj(inputs, weight, groups):
    row_count = inputs.shape[0]
    width_in = inputs.shape[1] // groups
    width_out = weight.shape[1] // groups
    shaped = inputs.reshape(row_count, groups, width_in)
    kernel = weight.reshape(width_in, groups, width_out)
    result = jnp.einsum('rgi,igo->rgo', shaped, kernel, precision=lax.Precision.HIGHEST)
    return result.reshape(row_count, groups * width_out)

def layer_norm(residual, norm_gain, norm_shift):
    average = lax.optimization_barrier(jnp.mean(residual, axis=-1, keepdims=True))
    centred = residual - average
    inverse_root = lax.rsqrt(lax.optimization_barrier(jnp.mean(centred * centred, axis=-1, keepdims=True)) + NORM_EPS)
    return centred * inverse_root * norm_gain + norm_shift

def gelu_exact(values):
    return 0.5 * values * (1.0 + lax.erf(values * math.sqrt(0.5)))

def attention(query_heads, key_heads, value_heads, anchors, segments):
    seq_len = query_heads.shape[0]
    block_len = math.gcd(seq_len, 512)
    block_count = seq_len // block_len
    score_scale = HEAD ** (-0.5)

    def one_block(block_in):
        query_block, anchor_block, segment_block = block_in
        scores = low_back(jnp.einsum('qhd,khd->hqk', query_block, key_heads, precision=lax.Precision.HIGHEST) * score_scale)
        same_doc = segment_block[None, :, None] == segments[None, None, :]
        exp_weights = jnp.exp(jnp.where(same_doc, scores - jnp.transpose(anchor_block)[:, :, None], MASKED))
        totals = low_back(lax.optimization_barrier(jnp.sum(exp_weights, axis=-1)))
        weighted = low_back(jnp.einsum('hqk,khd->qhd', low(exp_weights), value_heads, precision=lax.Precision.HIGHEST))
        return weighted / jnp.transpose(totals)[:, :, None]
    blocks = lax.map(jax.checkpoint(one_block), (query_heads.reshape(block_count, block_len, HEADS, HEAD), anchors.reshape(block_count, block_len, HEADS), segments.reshape(block_count, block_len)))
    return blocks.reshape(seq_len, HEADS * HEAD)

def encoder_layer(inputs, segments, params):
    w_query, w_key, w_value, b_query, b_value, w_out, b_out, gain_one, shift_one, w_inter, b_inter, w_second, b_second, gain_two, shift_two = params
    seq_len = inputs.shape[0]
    queries = low_back(low(group_proj(inputs, w_query, GROUPS) + b_query))
    key_rows = low_back(low(group_proj(inputs, w_key, GROUPS)))
    value_rows = low_back(low(group_proj(inputs, w_value, GROUPS) + b_value))
    query_heads = queries.reshape(seq_len, HEADS, HEAD)
    key_heads = key_rows.reshape(seq_len, HEADS, HEAD)
    value_heads = value_rows.reshape(seq_len, HEADS, HEAD)
    anchors = low(lax.optimization_barrier(jnp.sum(query_heads * key_heads, axis=-1)) * HEAD ** (-0.5))
    context = low(attention(query_heads, key_heads, value_heads, anchors, segments))
    attn_out = low_back(group_proj(context, w_out, 1) + b_out)
    normed_one = layer_norm(attn_out + inputs, gain_one, shift_one)
    hidden_pre = low_back(group_proj(low(normed_one), w_inter, GROUPS) + b_inter)
    hidden = low(gelu_exact(hidden_pre))
    branch = low_back(group_proj(hidden, w_second, GROUPS) + b_second)
    return layer_norm(branch + normed_one, gain_two, shift_two)

def reference(tokens, cotangent, segment_ids, q_weight, key_weight, value_weight, q_bias, value_bias, out_weight, out_bias, norm1_gain, norm1_bias, inter_weight, inter_bias, ffo_weight, ffo_bias, norm2_gain, norm2_bias):
    params = tuple((weight.astype(jnp.float32) for weight in (q_weight, key_weight, value_weight, q_bias, value_bias, out_weight, out_bias, norm1_gain, norm1_bias, inter_weight, inter_bias, ffo_weight, ffo_bias, norm2_gain, norm2_bias)))
    seq_len = tokens.shape[2]
    model_width = tokens.shape[3]
    flat_tokens = tokens.reshape(-1, seq_len, model_width).astype(jnp.float32)
    flat_cotangent = cotangent.reshape(-1, seq_len, model_width).astype(jnp.float32)
    flat_segments = segment_ids.reshape(-1, seq_len).astype(jnp.int32)

    def one_sequence(grad_sums, seq_in):
        seq_tokens, seq_upstream, seq_segments = seq_in

        def apply_layer(layer_in, param_set):
            return encoder_layer(layer_in, seq_segments, param_set)
        result, pull_back = jax.vjp(apply_layer, seq_tokens, params)
        d_tokens, d_params = pull_back(seq_upstream)
        grad_sums = jax.tree.map(jnp.add, grad_sums, d_params)
        return (grad_sums, (result.astype(jnp.bfloat16), d_tokens.astype(jnp.bfloat16)))
    start_sums = tuple((jnp.zeros_like(weight) for weight in params))
    grad_total, (outputs, token_grads) = lax.scan(one_sequence, start_sums, (flat_tokens, flat_cotangent, flat_segments))
    return (outputs.reshape(tokens.shape), token_grads.reshape(tokens.shape), grad_total[0], grad_total[1], grad_total[2], grad_total[3], grad_total[4], grad_total[5], grad_total[6], grad_total[7], grad_total[8], grad_total[9], grad_total[10], grad_total[11], grad_total[12], grad_total[13], grad_total[14])
```

```python
import math

import jax
import jax.numpy as jnp
from jax import lax
from jax.experimental import pallas as pl
from jax.experimental.pallas import tpu as pltpu
from jax.sharding import PartitionSpec as P

MESH = pl.DeviceIdType.MESH
MICRO = 3


def place(n, g, m):
    return g * (n // 4) + m + (g % 2)


def owners(n):
    return [place(n, g, m) for m in range(MICRO) for g in range(4)]


def unit_of(c, n):
    g = c // (n // 4)
    m = c - g * (n // 4) - lax.rem(g, 2)
    return g, m, (m >= 0) & (m < MICRO)


def greet(f, c, n):
    bar = pltpu.get_barrier_semaphore()
    for d in range(1, n):
        pl.semaphore_signal(bar, inc=1, device_id=(f, lax.rem(c + d, n)), device_id_type=MESH)
    pl.semaphore_wait(bar, n - 1)


def to_units(n, src, dst, ssem, rsem, lsem):
    f, c = lax.axis_index("fsdp"), lax.axis_index("ctx")
    own = owners(n)
    mine = unit_of(c, n)[2]
    def copy(u):
        return pltpu.make_async_remote_copy(src_ref=src.at[u], dst_ref=dst.at[c], send_sem=ssem.at[u], recv_sem=rsem.at[c],
                                            device_id=(f, own[u]), device_id_type=MESH)
    for u in range(12):
        @pl.when(c != own[u])
        def _():
            copy(u).start()
        @pl.when(c == own[u])
        def _():
            pltpu.make_async_copy(src.at[u], dst.at[c], lsem).start()
    @pl.when(mine)
    def _():
        pltpu.make_async_copy(src.at[0], dst.at[c], lsem).wait()
        for s in range(n):
            @pl.when(c != s)
            def _():
                pltpu.make_async_remote_copy(src_ref=src.at[0], dst_ref=dst.at[s], send_sem=ssem.at[0], recv_sem=rsem.at[s], device_id=(f, s), device_id_type=MESH).wait_recv()
    for u in range(12):
        @pl.when(c != own[u])
        def _():
            copy(u).wait_send()


def to_rows(n, src, dst, ssem, rsem, lsem):
    f, c = lax.axis_index("fsdp"), lax.axis_index("ctx")
    own = owners(n)
    g, m, mine = unit_of(c, n)
    u = m * 4 + g
    def copy(d):
        t = lax.rem(c + d, n)
        return pltpu.make_async_remote_copy(src_ref=src.at[t], dst_ref=dst.at[u], send_sem=ssem.at[d], recv_sem=rsem.at[u],
                                            device_id=(f, t), device_id_type=MESH)
    @pl.when(mine)
    def _():
        for d in range(1, n):
            copy(d).start()
        pltpu.make_async_copy(src.at[c], dst.at[u], lsem).start()
    for k in range(12):
        @pl.when(c != own[k])
        def _():
            pltpu.make_async_remote_copy(src_ref=src.at[0], dst_ref=dst.at[k], send_sem=ssem.at[0], recv_sem=rsem.at[k], device_id=(f, own[k]), device_id_type=MESH).wait_recv()
    @pl.when(mine)
    def _():
        pltpu.make_async_copy(src.at[c], dst.at[u], lsem).wait()
        for d in range(1, n):
            copy(d).wait_send()

BF, F32 = jnp.bfloat16, jnp.float32
HEAD, GW = 64, 192
CH = 208
XA = 240
BIG = 1e9
NN = (((1,), (0,)), ((), ()))
NT = (((1,), (1,)), ((), ()))
TN = (((0,), (0,)), ((), ()))

def mm(a, b, dims=NN):
    return lax.dot_general(a, b, dims, preferred_element_type=F32)

def iota(shape, axis):
    return lax.broadcasted_iota(jnp.int32, shape, axis)

def select_group(n, wf_ref, bf_ref, w_ref, b_ref):
    g = lax.axis_index("ctx") // (n // 4)
    for k in range(4):
        @pl.when(g == k)
        def _():
            w_ref[...] = wf_ref[:, :, k * GW:k * GW + GW]
            b_ref[...] = bf_ref[:, k * GW:k * GW + GW]


def build_weights(w_ref, b_ref, wa_ref, wat_ref):
    for s in range(3):
        for h in range(3):
            w = w_ref[s, :, h * 64:h * 64 + 64].astype(F32)
            top = jnp.concatenate([w * (0.125 if s == 0 else 1.0), jnp.zeros((GW, 64), F32)], axis=1)
            r, c = iota((48, 128), 0), iota((48, 128), 1)
            same = (c - 64 == r)
            lanes = (c >= 64) & (c < 96) & (r < 32)
            one = (r == 32)
            zero = jnp.zeros((48, 128), F32)
            if s == 0:
                bias = jnp.concatenate([b_ref[0:1, h * 64:h * 64 + 64].astype(F32) * 0.125, jnp.zeros((1, 64), F32)], axis=1)
                low = jnp.where(lanes & same, 1.0, zero) + jnp.where(one, bias, zero)
            elif s == 1:
                low = jnp.where(lanes & ~same, -BIG, zero) + jnp.where(one & (c == 96), 1.0, zero)
            else:
                bias = jnp.concatenate([b_ref[1:2, h * 64:h * 64 + 64].astype(F32), jnp.zeros((1, 64), F32)], axis=1)
                low = jnp.where(one, bias, zero) + jnp.where(one & (c == 64), 1.0, zero)
            full = jnp.concatenate([top, low], axis=0)
            wa_ref[s, :, h * 128:h * 128 + 128] = full.astype(BF)
            wat_ref[s, h * 128:h * 128 + 128, :] = jnp.transpose(full).astype(BF)

def bounds(xt_ref, nb, seg_ref, lohi_ref):
    for b in range(nb):
        seg_ref[b:b + 1, :] = xt_ref[b, GW:GW + 16, :].astype(F32)[0:1, :]
    seg = seg_ref[0:nb, :]
    full = jnp.concatenate([seg, jnp.full((128 - nb, 128), 1e6, F32)], axis=0)
    t = jnp.transpose(full)
    minrow, maxrow = t[0:1, :], t[127:128, :]
    mincol, maxcol = seg[:, 0:1], seg[:, 127:128]
    lo = jnp.sum((maxcol < minrow).astype(F32), axis=0, keepdims=True)
    hi = (nb - 1) - jnp.sum((mincol > maxrow).astype(F32), axis=0, keepdims=True)
    r = iota((8, 128), 0)
    lohi_ref[...] = jnp.where(r == 0, lo, hi).astype(jnp.int32)

def prep(xt_ref, nb, wa_ref, wat_ref, qt_ref, ka_ref, vt_ref, xn_ref=None, qn_ref=None, kt_ref=None, va_ref=None):
    def block(i, carry):
        x = jnp.concatenate([xt_ref[2 * i], xt_ref[2 * i + 1]], axis=1)
        seg = x[GW:GW + 16].astype(F32)[0:1].astype(jnp.int32)
        r = iota((48, 256), 0)
        aug = jnp.where((r == seg) & (r < 32) | (r == 32), 1.0, 0.0).astype(BF)
        xa = jnp.concatenate([x[0:GW], aug], axis=0)
        xn = jnp.transpose(xa)
        qt = mm(wat_ref[0], xa).astype(BF)
        kt = mm(wat_ref[1], xa).astype(BF)
        kn = mm(xn, wa_ref[1]).astype(BF)
        if vt_ref is not None:
            vt = mm(wat_ref[2], xa).astype(BF)
        if qn_ref is not None:
            qn = mm(xn, wa_ref[0]).astype(BF)
            vn = mm(xn, wa_ref[2]).astype(BF)
        for h in range(3):
            o = h * 128
            qt_ref[h, i] = qt[o:o + 128]
            anchor = jnp.sum(qt[o:o + 64].astype(F32) * kt[o:o + 64].astype(F32), axis=0, keepdims=True)
            qt_ref[h, i, 96:112] = jnp.where(iota((16, 256), 0) == 0, -anchor, 0.0).astype(BF)
            ka_ref[h, i] = kn[:, o:o + 128]
            if vt_ref is not None:
                vt_ref[h, i] = vt[o:o + 80]
            if qn_ref is not None:
                qn_ref[h, i] = qn[:, o:o + 128]
                kt_ref[h, i] = kt[o:o + 64]
                va_ref[h, i] = vn[:, o:o + 128]
        return carry
    lax.fori_loop(0, nb // 2, block, 0)

def fwd_kernel(nb, xt_ref, wf_ref, bf_ref, ctx_ref, cf_ref, l_ref, lohi_ref, w_ref, b_ref, wa_ref, wat_ref, qt_ref, ka_ref, vt_ref, seg_ref, acc_ref, lohi_v, lohi_s, sem):
    @pl.when(unit_of(lax.axis_index("ctx"), nb)[2])
    def _():
        select_group(nb, wf_ref, bf_ref, w_ref, b_ref)
        sb = nb // 2
        bounds(xt_ref, nb, seg_ref, lohi_v)
        cp = pltpu.make_async_copy(lohi_v, lohi_s, sem)
        cp.start()
        lohi_ref[...] = lohi_v[...]
        build_weights(w_ref, b_ref, wa_ref, wat_ref)
        prep(xt_ref, nb, wa_ref, wat_ref, qt_ref, ka_ref, vt_ref)
        cp.wait()
        def qblock(i, carry):
            lo, hi = lohi_s[0, 2 * i] // 2, lohi_s[1, 2 * i + 1] // 2
            acc_ref[...] = jnp.zeros_like(acc_ref)
            def kblock(j, c):
                s = [mm(ka_ref[h, j], qt_ref[h, i]) for h in range(3)]
                e = [jnp.exp(x).astype(BF) for x in s]
                o = [mm(vt_ref[h, j], e[h]) for h in range(3)]
                for h in range(3):
                    acc_ref[h] += o[h]
                return c
            lax.fori_loop(lo, hi + 1, kblock, 0)
            for h in range(3):
                a = acc_ref[h]
                l = a[64:65]
                c = a[0:64] / l
                cf_ref[i, h * 64:h * 64 + 64, :] = c
                l_ref[i, h:h + 1, :] = l
                cb = c.astype(BF)
                ctx_ref[2 * i, h * 64:h * 64 + 64, :] = cb[:, 0:128]
                ctx_ref[2 * i + 1, h * 64:h * 64 + 64, :] = cb[:, 128:256]
            return carry
        lax.fori_loop(0, sb, qblock, 0)


def attn_fwd(xt, w, b):
    nb = xt.shape[0]
    sb = nb // 2
    return pl.pallas_call(
        lambda *a: fwd_kernel(nb, *a),
        out_shape=(jax.ShapeDtypeStruct((nb, GW, 128), BF), jax.ShapeDtypeStruct((sb, GW, 256), F32),
                   jax.ShapeDtypeStruct((sb, 8, 256), F32), jax.ShapeDtypeStruct((8, 128), jnp.int32)),
        scratch_shapes=[pltpu.VMEM((3, GW, GW), BF), pltpu.VMEM((8, GW), BF), pltpu.VMEM((3, XA, 384), BF), pltpu.VMEM((3, 384, XA), BF), pltpu.VMEM((3, sb, 128, 256), BF), pltpu.VMEM((3, sb, 256, 128), BF),
                        pltpu.VMEM((3, sb, 80, 256), BF), pltpu.VMEM((max(nb, 8), 128), F32), pltpu.VMEM((3, 80, 256), F32),
                        pltpu.VMEM((8, 128), jnp.int32), pltpu.SMEM((8, 128), jnp.int32), pltpu.SemaphoreType.DMA],
        compiler_params=pltpu.CompilerParams(vmem_limit_bytes=60 * 2**20))(xt, w, b)

def bwd_kernel(nb, xt_ref, wf_ref, bf_ref, dc_ref, cf_ref, l_ref, lohi_s, dx_ref, gw_ref, gb_ref,
               w_ref, b_ref, wa_ref, wat_ref, qt_ref, ka_ref, qn_ref, kt_ref, va_ref, dnt_ref, dnn_ref, dq_ref, dqt_ref, dkv_ref, gacc_ref, gbacc_ref):
    gw_ref[...] = jnp.zeros_like(gw_ref)
    gb_ref[...] = jnp.zeros_like(gb_ref)
    @pl.when(unit_of(lax.axis_index("ctx"), nb)[2])
    def _():
        select_group(nb, wf_ref, bf_ref, w_ref, b_ref)
        sb = nb // 2
        build_weights(w_ref, b_ref, wa_ref, wat_ref)
        prep(xt_ref, nb, wa_ref, wat_ref, qt_ref, ka_ref, None, True, qn_ref, kt_ref, va_ref)
        dkv_ref[...] = jnp.zeros_like(dkv_ref)
        def pre(i, carry):
            d = jnp.concatenate([dc_ref[2 * i], dc_ref[2 * i + 1]], axis=1).astype(F32)
            for h in range(3):
                dh = d[h * 64:h * 64 + 64]
                inv = 1.0 / l_ref[i, h:h + 1, :]
                delta = jnp.sum(dh * cf_ref[i, h * 64:h * 64 + 64, :], axis=0, keepdims=True) * inv
                dn = dh * inv
                full = jnp.concatenate([dn, jnp.where(iota((64, 256), 0) == 0, -delta, 0.0)], axis=0)
                dnt_ref[h, i] = full.astype(BF)
                dnn_ref[h, i] = jnp.transpose(full).astype(BF)
            return carry
        lax.fori_loop(0, sb, pre, 0)
        def qblock(i, carry):
            lo, hi = lohi_s[0, 2 * i] // 2, lohi_s[1, 2 * i + 1] // 2
            dq_ref[...] = jnp.zeros_like(dq_ref)
            def kblock(j, c):
                s = [mm(ka_ref[h, j], qt_ref[h, i]) for h in range(3)]
                dp = [mm(va_ref[h, j], dnt_ref[h, i]) for h in range(3)]
                e = [jnp.exp(x) for x in s]
                eb = [x.astype(BF) for x in e]
                ds = [(e[h] * dp[h]).astype(BF) for h in range(3)]
                q = [mm(kt_ref[h, j], ds[h]) for h in range(3)]
                k = [mm(ds[h], qn_ref[h, i])[:, 0:64] for h in range(3)]
                v = [mm(eb[h], dnn_ref[h, i])[:, 0:64] for h in range(3)]
                for h in range(3):
                    dq_ref[h] += q[h]
                    dkv_ref[h, j, :, 0:64] += k[h]
                    dkv_ref[h, j, :, 64:128] += v[h]
                return c
            lax.fori_loop(lo, hi + 1, kblock, 0)
            dqt_ref[i] = (dq_ref[...].reshape(GW, 256) * 0.125).astype(BF)
            return carry
        lax.fori_loop(0, sb, qblock, 0)
        def post(i, carry):
            xt = jnp.concatenate([xt_ref[2 * i], xt_ref[2 * i + 1]], axis=1)[0:GW]
            dqt = dqt_ref[i]
            dk = jnp.concatenate([dkv_ref[h, i, :, 0:64] for h in range(3)], axis=1).astype(BF)
            dv = jnp.concatenate([dkv_ref[h, i, :, 64:128] for h in range(3)], axis=1).astype(BF)
            dx = mm(w_ref[0], dqt) + mm(w_ref[1], dk, NT) + mm(w_ref[2], dv, NT)
            dxb = dx.astype(BF)
            dx_ref[2 * i] = dxb[:, 0:128]
            dx_ref[2 * i + 1] = dxb[:, 128:256]
            gacc_ref[0] += mm(xt, dqt, NT)
            gacc_ref[1] += mm(xt, dk)
            gacc_ref[2] += mm(xt, dv)
            dqn = jnp.transpose(dqt.astype(F32))
            gbacc_ref[0:1] += jnp.sum(dqn, axis=0, keepdims=True)
            gbacc_ref[1:2] += jnp.sum(dv.astype(F32), axis=0, keepdims=True)
            return carry
        gacc_ref[...] = jnp.zeros_like(gacc_ref)
        gbacc_ref[...] = jnp.zeros_like(gbacc_ref)
        lax.fori_loop(0, sb, post, 0)
        g = lax.axis_index("ctx") // (nb // 4)
        for k in range(4):
            @pl.when(g == k)
            def _():
                gw_ref[:, :, k * GW:k * GW + GW] = gacc_ref[...].astype(BF)
                gb_ref[:, k * GW:k * GW + GW] = gbacc_ref[...]


def attn_bwd(xt, w, b, dc, cf, l, lohi):
    nb = xt.shape[0]
    sb = nb // 2
    return pl.pallas_call(
        lambda *a: bwd_kernel(nb, *a),
        out_shape=(jax.ShapeDtypeStruct((nb, GW, 128), BF), jax.ShapeDtypeStruct((3, GW, 768), BF), jax.ShapeDtypeStruct((8, 768), F32)),
        in_specs=[pl.BlockSpec(memory_space=pltpu.VMEM)] * 6 + [pl.BlockSpec(memory_space=pltpu.SMEM)],
        scratch_shapes=[pltpu.VMEM((3, GW, GW), BF), pltpu.VMEM((8, GW), BF), pltpu.VMEM((3, XA, 384), BF), pltpu.VMEM((3, 384, XA), BF), pltpu.VMEM((3, sb, 128, 256), BF), pltpu.VMEM((3, sb, 256, 128), BF),
                        pltpu.VMEM((3, sb, 256, 128), BF), pltpu.VMEM((3, sb, 64, 256), BF), pltpu.VMEM((3, sb, 256, 128), BF),
                        pltpu.VMEM((3, sb, 128, 256), BF), pltpu.VMEM((3, sb, 256, 128), BF), pltpu.VMEM((3, 64, 256), F32),
                        pltpu.VMEM((sb, GW, 256), BF), pltpu.VMEM((3, sb, 256, 128), F32), pltpu.VMEM((3, GW, GW), F32), pltpu.VMEM((8, GW), F32)],
        compiler_params=pltpu.CompilerParams(vmem_limit_bytes=60 * 2**20))(xt, w, b, dc, cf, l, lohi)


D, FF = 768, 3072
EPS = 1e-12
WIN = (0, 128, 384, 512)
OFF = (0, 64, 0, 64)
RS2 = math.sqrt(0.5)
IPI = 1.0 / math.sqrt(2.0 * math.pi)
CK = 32

def rowmean(x):
    return jnp.sum(x, axis=-1, keepdims=True) * (1.0 / D)

def dense_body(rows, tok, cot, ctxt, wout, wint, wffo, vec, out, d1, dct, ga, gi, gf, gv,
               ctx, attn, n1, n1b, wip, wfp, gp, hid, br, d2, db, dpre, dn, da, st):
    nm = rows // 128
    v = lambda i: vec[i:i + 1, :]
    for j in range(4):
        o = OFF[j]
        wip[j] = jnp.zeros((256, D), BF)
        wip[j, o:o + 192, :] = wint[:, j * D:(j + 1) * D]
        lane = iota((D, 256), 1)
        w = wffo[:, WIN[j]:WIN[j] + 256]
        wfp[j] = jnp.where((lane >= o) & (lane < o + 192), w.astype(F32), 0.0).astype(BF)
    for m in range(nm):
        ctx[m * 128:(m + 1) * 128, :] = jnp.transpose(ctxt[m])
    attn[...] = mm(ctx[...], wout[...])
    def ln1(t, c):
        s = pl.ds(pl.multiple_of(t * CK, CK), CK)
        r = attn[s, :] + v(0) + tok[s, :].astype(F32)
        cen = r - rowmean(r)
        rstd = lax.rsqrt(rowmean(cen * cen) + EPS)
        xh = cen * rstd
        attn[s, :] = xh
        st[s, :] = jnp.broadcast_to(rstd, (CK, 128))
        n = xh * v(1) + v(2)
        n1[s, :] = n
        n1b[s, :] = n.astype(BF)
        br[s, :] = n + v(3)
        return c
    lax.fori_loop(0, rows // CK, ln1, 0)
    for j in range(4):
        for m in range(nm):
            s = slice(m * 128, (m + 1) * 128)
            u = mm(n1b[s, WIN[j]:WIN[j] + 256], wip[j]) + v(8 + j)
            half = 0.5 + 0.5 * lax.erf(u * RS2)
            hid[j, s, :] = (u * half).astype(BF)
            gp[j, s, :] = half + u * (jnp.exp(u * u * -0.5) * IPI)
        br[:, WIN[j]:WIN[j] + 256] += mm(hid[j], wfp[j])
    gv[...] = jnp.zeros_like(gv)
    def ln2(t, c):
        s = pl.ds(pl.multiple_of(t * CK, CK), CK)
        r = br[s, :]
        cen = r - rowmean(r)
        rstd = lax.rsqrt(rowmean(cen * cen) + EPS)
        xh = cen * rstd
        out[s, :] = (xh * v(4) + v(5)).astype(BF)
        ct = cot[s, :].astype(F32)
        u = ct * v(4)
        dd = rstd * (u - rowmean(u) - xh * rowmean(u * xh))
        d2[s, :] = dd
        ddb = dd.astype(BF)
        db[s, :] = ddb
        gv[4:5, :] += jnp.sum(ct * xh, axis=0, keepdims=True)
        gv[5:6, :] += jnp.sum(ct, axis=0, keepdims=True)
        gv[3:4, :] += jnp.sum(ddb.astype(F32), axis=0, keepdims=True)
        return c
    lax.fori_loop(0, rows // CK, ln2, 0)
    dn[...] = d2[...]
    for j in range(4):
        for m in range(nm):
            s = slice(m * 128, (m + 1) * 128)
            dh = mm(db[s, WIN[j]:WIN[j] + 256], wfp[j], NT)
            dp = (dh * gp[j, s, :]).astype(BF)
            dpre[j, s, :] = dp
            gv[8 + j:9 + j, :] += jnp.sum(dp.astype(F32), axis=0, keepdims=True)
        dn[:, WIN[j]:WIN[j] + 256] += mm(dpre[j], wip[j], NT)
    def lnb(t, c):
        s = pl.ds(pl.multiple_of(t * CK, CK), CK)
        g = dn[s, :]
        xh = attn[s, :]
        u = g * v(1)
        dd = st[s, 0:1] * (u - rowmean(u) - xh * rowmean(u * xh))
        d1[s, :] = dd
        ddb = dd.astype(BF)
        da[s, :] = ddb
        gv[1:2, :] += jnp.sum(g * xh, axis=0, keepdims=True)
        gv[2:3, :] += jnp.sum(g, axis=0, keepdims=True)
        gv[0:1, :] += jnp.sum(ddb.astype(F32), axis=0, keepdims=True)
        return c
    lax.fori_loop(0, rows // CK, lnb, 0)
    dc = mm(wout[...], da[...], NT).astype(BF)
    for m in range(nm):
        dct[m] = dc[:, m * 128:(m + 1) * 128]
    ct = jnp.concatenate([ctxt[m] for m in range(nm)], axis=1)
    ga[...] = mm(ct, da[...]).astype(BF)
    nt = jnp.transpose(n1b[...])
    dbt = jnp.transpose(db[...])
    for j in range(4):
        o = WIN[j] + OFF[j]
        gi[:, j * D:(j + 1) * D] = mm(nt[o:o + 192, :], dpre[j]).astype(BF)
        gf[j * 192:(j + 1) * 192, :] = mm(dbt[o:o + 192, :], hid[j]).astype(BF)

def scratch(rows):
    return [pltpu.VMEM((rows, D), BF), pltpu.VMEM((rows, D), F32), pltpu.VMEM((rows, D), F32), pltpu.VMEM((rows, D), BF),
            pltpu.VMEM((4, 256, D), BF), pltpu.VMEM((4, D, 256), BF), pltpu.VMEM((4, rows, D), F32), pltpu.VMEM((4, rows, D), BF),
            pltpu.VMEM((rows, D), F32), pltpu.VMEM((rows, D), F32), pltpu.VMEM((rows, D), BF), pltpu.VMEM((4, rows, D), BF),
            pltpu.VMEM((rows, D), F32), pltpu.VMEM((rows, D), BF), pltpu.VMEM((rows, 128), F32)]

def dense(tok, cot, ctxt, wout, wint, wffo, vec):
    rows = tok.shape[0]
    nm = rows // 128
    S = jax.ShapeDtypeStruct
    return pl.pallas_call(
        lambda *a: dense_body(rows, *a),
        out_shape=(S((rows, D), BF), S((rows, D), F32), S((nm, D, 128), BF), S((D, D), BF), S((192, FF), BF), S((D, D), BF), S((16, D), F32)),
        scratch_shapes=scratch(rows),
        compiler_params=pltpu.CompilerParams(vmem_limit_bytes=60 * 2**20))(tok, cot, ctxt, wout, wint, wffo, vec)


def tokens_kernel(n, tok, seg, xt, buf, ssem, rsem, lsem):
    f, c = lax.axis_index("fsdp"), lax.axis_index("ctx")
    for m in range(MICRO):
        t = jnp.transpose(tok[m])
        sg = jnp.broadcast_to(seg[m:m + 1, :].astype(F32), (16, 128)).astype(BF)
        for g in range(4):
            buf[m * 4 + g, 0:GW, :] = t[g * GW:g * GW + GW]
            buf[m * 4 + g, GW:CH, :] = sg
    greet(f, c, n)
    to_units(n, buf, xt, ssem, rsem, lsem)


def rows_kernel(n, src, dst, ssem, rsem, lsem):
    greet(lax.axis_index("fsdp"), lax.axis_index("ctx"), n)
    to_rows(n, src, dst, ssem, rsem, lsem)


def units_kernel(n, src, dst, ssem, rsem, lsem):
    greet(lax.axis_index("fsdp"), lax.axis_index("ctx"), n)
    to_units(n, src, dst, ssem, rsem, lsem)


def final_kernel(n, src, d1, grad, buf, ssem, rsem, lsem):
    greet(lax.axis_index("fsdp"), lax.axis_index("ctx"), n)
    to_rows(n, src, buf, ssem, rsem, lsem)
    for m in range(MICRO):
        x = jnp.concatenate([buf[m * 4 + g] for g in range(4)], axis=0).astype(F32)
        grad[m] = (jnp.transpose(x) + d1[m]).astype(BF)


DMA = pltpu.SemaphoreType.DMA


def remote(kernel, n, cid, outs, args, scratch=()):
    vm = pl.BlockSpec(memory_space=pltpu.VMEM)
    return pl.pallas_call(
        lambda *a: kernel(n, *a), out_shape=outs, in_specs=[vm] * len(args),
        out_specs=jax.tree.map(lambda _: vm, outs),
        scratch_shapes=list(scratch) + [DMA((n,)), DMA((n,)), DMA],
        compiler_params=pltpu.CompilerParams(collective_id=cid, has_side_effects=True, vmem_limit_bytes=60 * 2**20))(*args)


def local(tokens, cotangent, segment_ids, q_weight, key_weight, value_weight, q_bias, value_bias, out_weight, out_bias,
          norm1_gain, norm1_bias, inter_weight, inter_bias, ffo_weight, ffo_bias, norm2_gain, norm2_bias):
    n, nf = lax.axis_size("ctx"), lax.axis_size("fsdp")
    S = jax.ShapeDtypeStruct
    rows = MICRO * 128
    tok = tokens.reshape(MICRO, 128, D)
    gather = lambda a, ax: lax.all_gather(a, "fsdp", axis=ax, tiled=True)
    wqkv = gather(jnp.stack([q_weight, key_weight, value_weight]), 1)
    wout, wint, wffo = gather(out_weight, 0), gather(inter_weight, 0), gather(ffo_weight, 0)
    dl = q_bias.shape[0]
    pack = jnp.concatenate([jnp.stack([out_bias, norm1_gain, norm1_bias, ffo_bias, norm2_gain, norm2_bias, q_bias, value_bias]),
                            inter_bias.reshape(4, dl)], axis=0)
    allv = lax.all_gather(pack, "fsdp", axis=0)
    top = jnp.swapaxes(allv[:, 0:8], 0, 1).reshape(8, D)
    low = allv[:, 8:12].reshape(4, D)
    vec = jnp.concatenate([top, low, jnp.zeros((4, D), BF)], axis=0).astype(F32)
    bqv = jnp.concatenate([top[6:8], jnp.zeros((6, D), BF)], axis=0)
    xt = remote(tokens_kernel, n, 0, S((n, CH, 128), BF), (tok, segment_ids.reshape(MICRO, 128)), [pltpu.VMEM((12, CH, 128), BF)])
    ctx, cf, l, lohi = attn_fwd(xt, wqkv, bqv)
    ctxt = remote(rows_kernel, n, 1, S((12, GW, 128), BF), (ctx,))
    out, d1, dct, ga, gi, gf, gv = dense(tok.reshape(rows, D), cotangent.reshape(rows, D), ctxt.reshape(MICRO, D, 128), wout, wint, wffo, vec)
    dc = remote(units_kernel, n, 2, S((n, GW, 128), BF), (dct.reshape(12, GW, 128),))
    dx, gw, gb = attn_bwd(xt, wqkv, bqv, dc, cf, l, lohi)
    grad = remote(final_kernel, n, 3, S((MICRO, 128, D), BF), (dx, d1.reshape(MICRO, 128, D)), [pltpu.VMEM((12, GW, 128), BF)])
    scatter = lambda a: lax.psum(lax.psum_scatter(a, "fsdp", scatter_dimension=0, tiled=True), "ctx").astype(F32)
    gvec = lax.psum(jnp.concatenate([gv, gb], axis=0), ("fsdp", "ctx"))
    me = lax.axis_index("fsdp")
    part = lambda i: lax.dynamic_slice(gvec[i], (me * dl,), (dl,))
    gib = lax.dynamic_slice(gvec[8:12].reshape(4 * D), (me * 4 * dl,), (4 * dl,))
    return (out.reshape(tokens.shape), grad.reshape(tokens.shape), scatter(gw[0]), scatter(gw[1]), scatter(gw[2]), part(16), part(17),
            scatter(ga), part(0), part(1), part(2), scatter(gi), gib, scatter(gf.T), part(3), part(4), part(5))


def solution(mesh):
    act, seg, mat, vec = P(None, "fsdp", "ctx", None), P(None, "fsdp", "ctx"), P("fsdp", None), P("fsdp")
    return jax.shard_map(
        local, mesh=mesh,
        in_specs=(act, act, seg, mat, mat, mat, vec, vec, mat, vec, vec, vec, mat, vec, mat, vec, vec, vec),
        out_specs=(act, act, mat, mat, mat, vec, vec, mat, vec, vec, vec, mat, vec, mat, vec, vec, vec),
        check_vma=False)
```

```python
import math

import jax
import jax.numpy as jnp
from jax import lax
from jax.experimental import pallas as pl
from jax.experimental.pallas import tpu as pltpu
from jax.sharding import PartitionSpec as P

MESH = pl.DeviceIdType.MESH
MICRO = 3


def place(n, g, m):
    return g * (n // 4) + m + (g % 2)


def owners(n):
    return [place(n, g, m) for m in range(MICRO) for g in range(4)]


def unit_of(c, n):
    g = c // (n // 4)
    m = c - g * (n // 4) - lax.rem(g, 2)
    return g, m, (m >= 0) & (m < MICRO)


def greet(f, c, n):
    bar = pltpu.get_barrier_semaphore()
    for d in range(1, n):
        pl.semaphore_signal(bar, inc=1, device_id=(f, lax.rem(c + d, n)), device_id_type=MESH)
    pl.semaphore_wait(bar, n - 1)


BF, F32 = jnp.bfloat16, jnp.float32
HEAD, GW = 64, 192
CH = 208
XA = 240
BIG = 1e9
NN = (((1,), (0,)), ((), ()))
NT = (((1,), (1,)), ((), ()))
TN = (((0,), (0,)), ((), ()))

def mm(a, b, dims=NN):
    return lax.dot_general(a, b, dims, preferred_element_type=F32)

def iota(shape, axis):
    return lax.broadcasted_iota(jnp.int32, shape, axis)

def build_weights(w_ref, b_ref, wa_ref, wat_ref):
    for s in range(3):
        for h in range(3):
            w = w_ref[s, :, h * 64:h * 64 + 64].astype(F32)
            top = jnp.concatenate([w * (0.125 if s == 0 else 1.0), jnp.zeros((GW, 64), F32)], axis=1)
            r, c = iota((48, 128), 0), iota((48, 128), 1)
            same = (c - 64 == r)
            lanes = (c >= 64) & (c < 96) & (r < 32)
            one = (r == 32)
            zero = jnp.zeros((48, 128), F32)
            if s == 0:
                bias = jnp.concatenate([b_ref[0:1, h * 64:h * 64 + 64].astype(F32) * 0.125, jnp.zeros((1, 64), F32)], axis=1)
                low = jnp.where(lanes & same, 1.0, zero) + jnp.where(one, bias, zero)
            elif s == 1:
                low = jnp.where(lanes & ~same, -BIG, zero) + jnp.where(one & (c == 96), 1.0, zero)
            else:
                bias = jnp.concatenate([b_ref[1:2, h * 64:h * 64 + 64].astype(F32), jnp.zeros((1, 64), F32)], axis=1)
                low = jnp.where(one, bias, zero) + jnp.where(one & (c == 64), 1.0, zero)
            full = jnp.concatenate([top, low], axis=0)
            wa_ref[s, :, h * 128:h * 128 + 128] = full.astype(BF)
            wat_ref[s, h * 128:h * 128 + 128, :] = jnp.transpose(full).astype(BF)

D, FF = 768, 3072
EPS = 1e-12
WIN = (0, 128, 384, 512)
OFF = (0, 64, 0, 64)
RS2 = math.sqrt(0.5)
IPI = 1.0 / math.sqrt(2.0 * math.pi)
CK = 32

def rowmean(x):
    return jnp.sum(x, axis=-1, keepdims=True) * (1.0 / D)

def tall(ref, m):
    return jnp.concatenate([ref[m * 4 + g] for g in range(4)], axis=0)


def dense_body(rows, tok, cot, ctxt, wout, wint, wffo, vec, out, d1, dct, ga, gi, gf, gv,
               ctx, attn, n1b, wip, wfp, dpre, hid, br, dn, db, st, send):
    da = ctx
    nm = rows // 128
    v = lambda i: vec[i:i + 1, :]
    for j in range(4):
        o = OFF[j]
        wip[j] = jnp.zeros((256, D), BF)
        wip[j, o:o + 192, :] = wint[:, j * D:(j + 1) * D]
        lane = iota((D, 256), 1)
        w = wffo[:, WIN[j]:WIN[j] + 256]
        wfp[j] = jnp.where((lane >= o) & (lane < o + 192), w.astype(F32), 0.0).astype(BF)
    for m in range(nm):
        ctx[m * 128:(m + 1) * 128, :] = jnp.transpose(tall(ctxt, m))
    attn[...] = mm(ctx[...], wout[...])
    def ln1(t, c):
        s = pl.ds(pl.multiple_of(t * CK, CK), CK)
        r = attn[s, :] + v(0) + tok[s, :].astype(F32)
        cen = r - rowmean(r)
        rstd = lax.rsqrt(rowmean(cen * cen) + EPS)
        xh = cen * rstd
        attn[s, :] = xh
        st[s, :] = jnp.broadcast_to(rstd, (CK, 128))
        n = xh * v(1) + v(2)
        n1b[s, :] = n.astype(BF)
        br[s, :] = n + v(3)
        return c
    lax.fori_loop(0, rows // CK, ln1, 0)
    for j in range(4):
        for m in range(nm):
            s = slice(m * 128, (m + 1) * 128)
            u = mm(n1b[s, WIN[j]:WIN[j] + 256], wip[j]) + v(8 + j)
            half = 0.5 + 0.5 * lax.erf(u * RS2)
            hid[j, s, :] = (u * half).astype(BF)
            dpre[j, s, :] = (half + u * (jnp.exp(u * u * -0.5) * IPI)).astype(BF)
        br[:, WIN[j]:WIN[j] + 256] += mm(hid[j], wfp[j])
    gv[...] = jnp.zeros_like(gv)
    def ln2(t, c):
        s = pl.ds(pl.multiple_of(t * CK, CK), CK)
        r = br[s, :]
        cen = r - rowmean(r)
        rstd = lax.rsqrt(rowmean(cen * cen) + EPS)
        xh = cen * rstd
        out[s, :] = (xh * v(4) + v(5)).astype(BF)
        ct = cot[s, :].astype(F32)
        u = ct * v(4)
        dd = rstd * (u - rowmean(u) - xh * rowmean(u * xh))
        dn[s, :] = dd
        ddb = dd.astype(BF)
        db[s, :] = ddb
        gv[4:5, :] += jnp.sum(ct * xh, axis=0, keepdims=True)
        gv[5:6, :] += jnp.sum(ct, axis=0, keepdims=True)
        gv[3:4, :] += jnp.sum(ddb.astype(F32), axis=0, keepdims=True)
        return c
    lax.fori_loop(0, rows // CK, ln2, 0)
    for j in range(4):
        for m in range(nm):
            s = slice(m * 128, (m + 1) * 128)
            dh = mm(db[s, WIN[j]:WIN[j] + 256], wfp[j], NT)
            dp = (dh * dpre[j, s, :].astype(F32)).astype(BF)
            dpre[j, s, :] = dp
            gv[8 + j:9 + j, :] += jnp.sum(dp.astype(F32), axis=0, keepdims=True)
        dn[:, WIN[j]:WIN[j] + 256] += mm(dpre[j], wip[j], NT)
    def lnb(t, c):
        s = pl.ds(pl.multiple_of(t * CK, CK), CK)
        g = dn[s, :]
        xh = attn[s, :]
        u = g * v(1)
        dd = st[s, 0:1] * (u - rowmean(u) - xh * rowmean(u * xh))
        d1[s, :] = dd
        ddb = dd.astype(BF)
        da[s, :] = ddb
        gv[1:2, :] += jnp.sum(g * xh, axis=0, keepdims=True)
        gv[2:3, :] += jnp.sum(g, axis=0, keepdims=True)
        gv[0:1, :] += jnp.sum(ddb.astype(F32), axis=0, keepdims=True)
        return c
    lax.fori_loop(0, rows // CK, lnb, 0)
    dc = mm(wout[...], da[...], NT).astype(BF)
    for m in range(nm):
        for g in range(4):
            dct[m * 4 + g] = dc[g * GW:g * GW + GW, m * 128:(m + 1) * 128]
    send()
    ct = jnp.concatenate([tall(ctxt, m) for m in range(nm)], axis=1)
    ga[...] = mm(ct, da[...]).astype(BF)
    nt = jnp.transpose(n1b[...])
    dbt = jnp.transpose(db[...])
    for j in range(4):
        o = WIN[j] + OFF[j]
        gi[:, j * D:(j + 1) * D] = mm(nt[o:o + 192, :], dpre[j]).astype(BF)
        gf[j * 192:(j + 1) * 192, :] = mm(dbt[o:o + 192, :], hid[j]).astype(BF)

def remote_copy(src, dst, ssem, rsem, f, c):
    return pltpu.make_async_remote_copy(src_ref=src, dst_ref=dst, send_sem=ssem, recv_sem=rsem, device_id=(f, c), device_id_type=MESH)


def tile_at(q, t, half):
    p, mir = lax.rem(q, half // 2), lax.div(q, half // 2)
    b = lax.div(t + half - 1 - p, 2 * half)
    i = p + b * (half - 1 - 2 * p)
    j = t - b * (half + 1 + p)
    last = 2 * half - 1
    return b, i + mir * (last - 2 * i), j + mir * (last - 2 * j)


def rows_at(q, half):
    p, mir = lax.rem(q, half // 2), lax.div(q, half // 2)
    last = 2 * half - 1
    return [i + mir * (last - 2 * i) for i in (p, half - 1 - p)]


def forward_tiles(q, half, qt, ka, vt, acc):
    acc[...] = jnp.zeros_like(acc)
    items = [(h,) + tile_at(q, t, half) for t in range(3 * half + 1) for h in range(3)]
    def front(it):
        h, _, i, j = it
        return mm(ka[h, j], qt[h, i])
    ready = [front(it) for it in items[:3]]
    for t, (h, b, i, j) in enumerate(items):
        if t + 3 < len(items):
            ready.append(front(items[t + 3]))
        e = jnp.exp(ready[t]).astype(BF)
        ready[t] = None
        acc[h, b] += mm(vt[h, j], e)


def backward_tiles(q, half, qt, ka, kt, va, dnt, dq, dk, dv):
    dq[...] = jnp.zeros_like(dq)
    items = [(h,) + tile_at(q, t, half) for t in range(3 * half + 1) for h in range(3)]
    def front(it):
        h, _, i, j = it
        return mm(ka[h, j], qt[h, i]), mm(va[h, j, :, 0:80], dnt[h, i])
    ready = [front(it) for it in items[:2]]
    for t, (h, b, i, j) in enumerate(items):
        if t + 2 < len(items):
            ready.append(front(items[t + 2]))
        s, dp = ready[t]
        ready[t] = None
        e = jnp.exp(s)
        eb = e.astype(BF)
        ds = (e * dp).astype(BF)
        dq[h, b] += mm(kt[h, j], ds)
        dk[h, j] += mm(qt[h, i, 0:64], ds, NT)
        dv[h, j] += mm(dnt[h, i, 0:64], eb, NT)


def prep_block(i, xt, wa, wat, qt, ka, vt, kt, va):
    x = jnp.concatenate([xt[2 * i], xt[2 * i + 1]], axis=1)
    seg = x[GW:GW + 16].astype(F32)[0:1].astype(jnp.int32)
    r = iota((48, 256), 0)
    aug = jnp.where((r == seg) & (r < 32) | (r == 32), 1.0, 0.0).astype(BF)
    xa = jnp.concatenate([x[0:GW], aug], axis=0)
    xn = jnp.transpose(xa)
    q = mm(wat[0], xa).astype(BF)
    k = mm(wat[1], xa).astype(BF)
    v = mm(wat[2], xa).astype(BF)
    kn = mm(xn, wa[1]).astype(BF)
    vn = mm(xn, wa[2]).astype(BF)
    for h in range(3):
        o = h * 128
        qt[h, i] = q[o:o + 128]
        anchor = jnp.sum(q[o:o + 64].astype(F32) * k[o:o + 64].astype(F32), axis=0, keepdims=True)
        qt[h, i, 96:112] = jnp.where(iota((16, 256), 0) == 0, -anchor, 0.0).astype(BF)
        ka[h, i] = kn[:, o:o + 128]
        vt[h, i] = v[o:o + 80]
        kt[h, i] = k[o:o + 64]
        va[h, i] = vn[:, o:o + 128]


def mega(n, tok, seg, cot, wqkv, bqv, wout, wint, wffo, vec,
         out, grad, gw, gb, ga, gi, gf, gv,
         tsend, xt, csend, crecv, dsend, dc, xrecv,
         w, bias, wa, wat, qt, ka, vt, kt, va, cf, lsum, acc, dq, dk, dv, dqt, gacc, gbacc,
         d1, dense_refs, tss, trs, css, crs, dss, drs, xss, xrs, ls):
    f, c = lax.axis_index("fsdp"), lax.axis_index("ctx")
    g, m, mine = unit_of(c, n)
    u = m * 4 + g
    own = owners(n)
    sb, half = n // 2, n // 4
    dnt = vt
    bar = pltpu.get_barrier_semaphore()
    for d in range(1, n):
        pl.semaphore_signal(bar, inc=1, device_id=(f, lax.rem(c + d, n)), device_id_type=MESH)
    for k in range(MICRO):
        t = jnp.transpose(tok[k * 128:k * 128 + 128, :])
        sg = jnp.broadcast_to(seg[k:k + 1, :].astype(F32), (16, 128)).astype(BF)
        for j in range(4):
            tsend[k * 4 + j, 0:GW, :] = t[j * GW:j * GW + GW]
            tsend[k * 4 + j, GW:CH, :] = sg
    pl.semaphore_wait(bar, n - 1)

    def spread(src, dst, ss, rs, start):
        for k in range(12):
            @pl.when(c != own[k])
            def _():
                cp = remote_copy(src.at[k], dst.at[c], ss.at[k], rs.at[c], f, own[k])
                cp.start() if start else cp.wait_send()
            if start:
                @pl.when(c == own[k])
                def _():
                    pltpu.make_async_copy(src.at[k], dst.at[c], rs.at[c]).start()
    def arrived(src, dst, rs, s):
        @pl.when(c != s)
        def _():
            remote_copy(src.at[0], dst.at[s], ls, rs.at[s], f, s).wait_recv()
        @pl.when(c == s)
        def _():
            pltpu.make_async_copy(src.at[0], dst.at[s], rs.at[s]).wait()
    def give(src, dst, ss, rs, t, start):
        @pl.when(c != t)
        def _():
            cp = remote_copy(src.at[t], dst.at[u], ss.at[t], rs.at[u], f, t)
            cp.start() if start else cp.wait_send()
        if start:
            @pl.when(c == t)
            def _():
                pltpu.make_async_copy(src.at[t], dst.at[u], rs.at[u]).start()
    def taken(src, dst, rs):
        for k in range(12):
            @pl.when(c != own[k])
            def _():
                remote_copy(src.at[0], dst.at[k], ls, rs.at[k], f, own[k]).wait_recv()
            @pl.when(c == own[k])
            def _():
                pltpu.make_async_copy(src.at[0], dst.at[k], rs.at[k]).wait()

    spread(tsend, xt, tss, trs, True)

    @pl.when(mine)
    def _():
        for k in range(4):
            @pl.when(g == k)
            def _():
                w[...] = wqkv[:, :, k * GW:k * GW + GW]
                bias[...] = bqv[:, k * GW:k * GW + GW]
        build_weights(w, bias, wa, wat)
        def first(i, carry):
            arrived(tsend, xt, trs, 2 * i)
            arrived(tsend, xt, trs, 2 * i + 1)
            prep_block(i, xt, wa, wat, qt, ka, vt, kt, va)
            return carry
        lax.fori_loop(0, sb, first, 0)
        def step(q, carry):
            forward_tiles(q, half, qt, ka, vt, acc)
            for b, i in enumerate(rows_at(q, half)):
                for h in range(3):
                    a = acc[h, b]
                    x = a[0:64] / a[64:65]
                    cf[i, h * 64:h * 64 + 64, :] = x
                    lsum[i, h:h + 1, :] = a[64:65]
                    xb = x.astype(BF)
                    csend[2 * i, h * 64:h * 64 + 64, :] = xb[:, 0:128]
                    csend[2 * i + 1, h * 64:h * 64 + 64, :] = xb[:, 128:256]
                give(csend, crecv, css, crs, 2 * i, True)
                give(csend, crecv, css, crs, 2 * i + 1, True)
            return carry
        lax.fori_loop(0, half, step, 0)
        dk[...] = jnp.zeros_like(dk)
        dv[...] = jnp.zeros_like(dv)

    taken(csend, crecv, crs)
    def send_dct():
        spread(dsend, dc, dss, drs, True)
    dense_body(MICRO * 128, tok, cot, crecv, wout, wint, wffo, vec, out, d1, dsend, ga, gi, gf, gv, *dense_refs, send=send_dct)

    gw[...] = jnp.zeros_like(gw)
    gb[...] = jnp.zeros_like(gb)

    @pl.when(mine)
    def _():
        def step(q, carry):
            for b, i in enumerate(rows_at(q, half)):
                arrived(dsend, dc, drs, 2 * i)
                arrived(dsend, dc, drs, 2 * i + 1)
                d = jnp.concatenate([dc[2 * i], dc[2 * i + 1]], axis=1).astype(F32)
                for h in range(3):
                    dh = d[h * 64:h * 64 + 64]
                    inv = 1.0 / lsum[i, h:h + 1, :]
                    delta = jnp.sum(dh * cf[i, h * 64:h * 64 + 64, :], axis=0, keepdims=True) * inv
                    dnt[h, i] = jnp.concatenate([dh * inv, jnp.where(iota((16, 256), 0) == 0, -delta, 0.0)], axis=0).astype(BF)
            backward_tiles(q, half, qt, ka, kt, va, dnt, dq, dk, dv)
            for b, i in enumerate(rows_at(q, half)):
                for h in range(3):
                    dqt[i, h * 64:h * 64 + 64, :] = (dq[h, b] * 0.125).astype(BF)
            return carry
        lax.fori_loop(0, half, step, 0)
        for t in range(n):
            give(csend, crecv, css, crs, t, False)
        xsend = csend
        gacc[...] = jnp.zeros_like(gacc)
        gbacc[...] = jnp.zeros_like(gbacc)
        ones = jnp.ones((8, 256), BF)
        def post(i, carry):
            x = jnp.concatenate([xt[2 * i, 0:GW, :], xt[2 * i + 1, 0:GW, :]], axis=1)
            q = dqt[i]
            k = jnp.concatenate([dk[h, i] for h in range(3)], axis=0).astype(BF)
            v = jnp.concatenate([dv[h, i] for h in range(3)], axis=0).astype(BF)
            x2 = (mm(w[0], q) + mm(w[1], k) + mm(w[2], v)).astype(BF)
            xsend[2 * i] = x2[:, 0:128]
            xsend[2 * i + 1] = x2[:, 128:256]
            give(xsend, xrecv, xss, xrs, 2 * i, True)
            give(xsend, xrecv, xss, xrs, 2 * i + 1, True)
            gacc[0] += mm(x, q, NT)
            gacc[1] += mm(x, k, NT)
            gacc[2] += mm(x, v, NT)
            gbacc[0] += mm(ones, q, NT)
            gbacc[1] += mm(ones, v, NT)
            return carry
        lax.fori_loop(0, sb, post, 0)
        for k in range(4):
            @pl.when(g == k)
            def _():
                gw[:, :, k * GW:k * GW + GW] = gacc[...].astype(BF)
                gb[0:1, k * GW:k * GW + GW] = gbacc[0, 0:1]
                gb[1:2, k * GW:k * GW + GW] = gbacc[1, 0:1]

    taken(csend, xrecv, xrs)
    for k in range(MICRO):
        x = jnp.concatenate([xrecv[k * 4 + j] for j in range(4)], axis=0).astype(F32)
        s = slice(k * 128, k * 128 + 128)
        grad[s, :] = (jnp.transpose(x) + d1[s, :]).astype(BF)
    spread(tsend, xt, tss, trs, False)
    spread(dsend, dc, dss, drs, False)
    @pl.when(mine)
    def _():
        for t in range(n):
            give(csend, xrecv, xss, xrs, t, False)

DMA = pltpu.SemaphoreType.DMA


def run_mega(n, tok, seg, cot, wqkv, bqv, wout, wint, wffo, vec):
    S, V = jax.ShapeDtypeStruct, pltpu.VMEM
    rows, sb = MICRO * 128, n // 2
    vm = pl.BlockSpec(memory_space=pltpu.VMEM)
    outs = (S((rows, D), BF), S((rows, D), BF), S((3, GW, D), BF), S((8, D), F32), S((D, D), BF), S((192, FF), BF), S((D, D), BF), S((16, D), F32))
    dense_refs = [V((rows, D), BF), V((rows, D), F32), V((rows, D), BF), V((4, 256, D), BF), V((4, D, 256), BF), V((4, rows, D), BF),
                  V((4, rows, D), BF), V((rows, D), F32), V((rows, D), F32), V((rows, D), BF), V((rows, 128), F32)]
    scratch = [V((12, CH, 128), BF), V((n, CH, 128), BF), V((n, GW, 128), BF), V((12, GW, 128), BF), V((12, GW, 128), BF), V((n, GW, 128), BF),
               V((12, GW, 128), BF),
               V((3, GW, GW), BF), V((8, GW), BF), V((3, XA, 384), BF), V((3, 384, XA), BF), V((3, sb, 128, 256), BF), V((3, sb, 256, 128), BF),
               V((3, sb, 80, 256), BF), V((3, sb, 64, 256), BF), V((3, sb, 256, 128), BF), V((sb, GW, 256), F32), V((sb, 8, 256), F32),
               V((3, 2, 80, 256), F32), V((3, 2, 64, 256), F32), V((3, sb, 64, 256), F32), V((3, sb, 64, 256), F32), V((sb, GW, 256), BF), V((3, GW, GW), F32), V((2, 8, GW), F32),
               V((rows, D), F32), dense_refs] + [DMA((12,)), DMA((n,)), DMA((n,)), DMA((12,)), DMA((12,)), DMA((n,)), DMA((n,)), DMA((12,)), DMA]
    return pl.pallas_call(
        lambda *a: mega(n, *a), out_shape=outs, in_specs=[vm] * 9, out_specs=(vm,) * 8, scratch_shapes=scratch,
        compiler_params=pltpu.CompilerParams(collective_id=0, has_side_effects=True, vmem_limit_bytes=60 * 2**20))(
            tok, seg, cot, wqkv, bqv, wout, wint, wffo, vec)


def local(tokens, cotangent, segment_ids, q_weight, key_weight, value_weight, q_bias, value_bias, out_weight, out_bias,
          norm1_gain, norm1_bias, inter_weight, inter_bias, ffo_weight, ffo_bias, norm2_gain, norm2_bias):
    n, nf = lax.axis_size("ctx"), lax.axis_size("fsdp")
    S = jax.ShapeDtypeStruct
    rows = MICRO * 128
    tok = tokens.reshape(MICRO, 128, D)
    gather = lambda a, ax: lax.all_gather(a, "fsdp", axis=ax, tiled=True)
    wqkv = gather(jnp.stack([q_weight, key_weight, value_weight]), 1)
    wout, wint, wffo = gather(out_weight, 0), gather(inter_weight, 0), gather(ffo_weight, 0)
    dl = q_bias.shape[0]
    pack = jnp.concatenate([jnp.stack([out_bias, norm1_gain, norm1_bias, ffo_bias, norm2_gain, norm2_bias, q_bias, value_bias]),
                            inter_bias.reshape(4, dl)], axis=0)
    allv = lax.all_gather(pack, "fsdp", axis=0)
    top = jnp.swapaxes(allv[:, 0:8], 0, 1).reshape(8, D)
    low = allv[:, 8:12].reshape(4, D)
    vec = jnp.concatenate([top, low, jnp.zeros((4, D), BF)], axis=0).astype(F32)
    bqv = jnp.concatenate([top[6:8], jnp.zeros((6, D), BF)], axis=0)
    out, grad, gw, gb, ga, gi, gf, gv = run_mega(n, tok.reshape(rows, D), segment_ids.reshape(MICRO, 128), cotangent.reshape(rows, D),
                                                 wqkv, bqv, wout, wint, wffo, vec)
    scatter = lambda a: lax.psum(lax.psum_scatter(a, "fsdp", scatter_dimension=0, tiled=True), "ctx").astype(F32)
    gvec = lax.psum(jnp.concatenate([gv, gb], axis=0), ("fsdp", "ctx"))
    me = lax.axis_index("fsdp")
    part = lambda i: lax.dynamic_slice(gvec[i], (me * dl,), (dl,))
    gib = lax.dynamic_slice(gvec[8:12].reshape(4 * D), (me * 4 * dl,), (4 * dl,))
    return (out.reshape(tokens.shape), grad.reshape(tokens.shape), scatter(gw[0]), scatter(gw[1]), scatter(gw[2]), part(16), part(17),
            scatter(ga), part(0), part(1), part(2), scatter(gi), gib, scatter(gf.T), part(3), part(4), part(5))


def solution(mesh):
    act, seg, mat, vec = P(None, "fsdp", "ctx", None), P(None, "fsdp", "ctx"), P("fsdp", None), P("fsdp")
    return jax.shard_map(
        local, mesh=mesh,
        in_specs=(act, act, seg, mat, mat, mat, vec, vec, mat, vec, vec, vec, mat, vec, mat, vec, vec, vec),
        out_specs=(act, act, mat, mat, mat, vec, vec, mat, vec, vec, vec, mat, vec, mat, vec, vec, vec),
        check_vma=False)
```

```python
import math

import jax
import jax.numpy as jnp
from jax import lax
from jax.experimental import pallas as pl
from jax.experimental.pallas import tpu as pltpu
from jax.sharding import PartitionSpec as P

MESH = pl.DeviceIdType.MESH
MICRO = 3


def place(n, g, m):
    return g * (n // 4) + m + (g % 2)


def owners(n):
    return [place(n, g, m) for m in range(MICRO) for g in range(4)]


def unit_of(c, n):
    g = c // (n // 4)
    m = c - g * (n // 4) - lax.rem(g, 2)
    return g, m, (m >= 0) & (m < MICRO)


BF, F32 = jnp.bfloat16, jnp.float32
HEAD, GW = 64, 192
CH = 208
XA = 240
BIG = 1e9
NN = (((1,), (0,)), ((), ()))
NT = (((1,), (1,)), ((), ()))
TN = (((0,), (0,)), ((), ()))

def mm(a, b, dims=NN):
    return lax.dot_general(a, b, dims, preferred_element_type=F32)

def iota(shape, axis):
    return lax.broadcasted_iota(jnp.int32, shape, axis)

def build_weights(w_ref, b_ref, wa_ref, wat_ref):
    for s in range(3):
        for h in range(3):
            w = w_ref[s, :, h * 64:h * 64 + 64].astype(F32)
            top = jnp.concatenate([w * (0.125 if s == 0 else 1.0), jnp.zeros((GW, 64), F32)], axis=1)
            r, c = iota((48, 128), 0), iota((48, 128), 1)
            same = (c - 64 == r)
            lanes = (c >= 64) & (c < 96) & (r < 32)
            one = (r == 32)
            zero = jnp.zeros((48, 128), F32)
            if s == 0:
                bias = jnp.concatenate([b_ref[0:1, h * 64:h * 64 + 64].astype(F32) * 0.125, jnp.zeros((1, 64), F32)], axis=1)
                low = jnp.where(lanes & same, 1.0, zero) + jnp.where(one, bias, zero)
            elif s == 1:
                low = jnp.where(lanes & ~same, -BIG, zero) + jnp.where(one & (c == 96), 1.0, zero)
            else:
                bias = jnp.concatenate([b_ref[1:2, h * 64:h * 64 + 64].astype(F32), jnp.zeros((1, 64), F32)], axis=1)
                low = jnp.where(one, bias, zero) + jnp.where(one & (c == 64), 1.0, zero)
            full = jnp.concatenate([top, low], axis=0)
            wa_ref[s, :, h * 128:h * 128 + 128] = full.astype(BF)
            wat_ref[s, h * 128:h * 128 + 128, :] = jnp.transpose(full).astype(BF)

D, FF = 768, 3072
EPS = 1e-12
WIN = (0, 128, 384, 512)
OFF = (0, 64, 0, 64)
RS2 = math.sqrt(0.5)
IPI = 1.0 / math.sqrt(2.0 * math.pi)
CK = 32

def rowmean(x):
    return jnp.sum(x, axis=-1, keepdims=True) * (1.0 / D)

def tall(ref, m):
    return jnp.concatenate([ref[m * 4 + g] for g in range(4)], axis=0)


def pad_weights(wint, wffo, wip, wfp):
    for j in range(4):
        o = OFF[j]
        wip[j] = jnp.zeros((256, D), BF)
        wip[j, o:o + 192, :] = wint[:, j * D:(j + 1) * D]
        lane = iota((D, 256), 1)
        w = wffo[:, WIN[j]:WIN[j] + 256]
        wfp[j] = jnp.where((lane >= o) & (lane < o + 192), w.astype(F32), 0.0).astype(BF)


def dense_body(rows, x, send, chains):
    tok, cot, ctxt, wout, out, d1, dct, gv = x.tok, x.cot, x.crecv, x.wout, x.out, x.d1, x.dsend, x.gv
    ctx, attn, n1b, wip, wfp, dpre, hid, br, dn, db, st = x.ctx, x.xh, x.n1b, x.wip, x.wfp, x.dpre, x.hid, x.br, x.dn, x.db, x.st
    da = ctx
    nm = rows // 128
    v = lambda i: x.vec[i:i + 1, :]
    for m in range(nm):
        ctx[m * 128:(m + 1) * 128, :] = jnp.transpose(tall(ctxt, m))
    attn[...] = mm(ctx[...], wout[...])
    def ln1(t, c):
        s = pl.ds(pl.multiple_of(t * CK, CK), CK)
        r = attn[s, :] + v(0) + tok[s, :].astype(F32)
        cen = r - rowmean(r)
        rstd = lax.rsqrt(rowmean(cen * cen) + EPS)
        xh = cen * rstd
        attn[s, :] = xh
        st[s, :] = jnp.broadcast_to(rstd, (CK, 128))
        n = xh * v(1) + v(2)
        n1b[s, :] = n.astype(BF)
        br[s, :] = n + v(3)
        return c
    lax.fori_loop(0, rows // CK, ln1, 0)
    for j in range(4):
        for m in range(nm):
            s = slice(m * 128, (m + 1) * 128)
            u = mm(n1b[s, WIN[j]:WIN[j] + 256], wip[j]) + v(8 + j)
            half = 0.5 + 0.5 * lax.erf(u * RS2)
            hid[j, s, :] = (u * half).astype(BF)
            dpre[j, s, :] = (half + u * (jnp.exp(u * u * -0.5) * IPI)).astype(BF)
        br[:, WIN[j]:WIN[j] + 256] += mm(hid[j], wfp[j])
    gv[...] = jnp.zeros_like(gv)
    def ln2(t, c):
        s = pl.ds(pl.multiple_of(t * CK, CK), CK)
        r = br[s, :]
        cen = r - rowmean(r)
        rstd = lax.rsqrt(rowmean(cen * cen) + EPS)
        xh = cen * rstd
        out[s, :] = (xh * v(4) + v(5)).astype(BF)
        ct = cot[s, :].astype(F32)
        u = ct * v(4)
        dd = rstd * (u - rowmean(u) - xh * rowmean(u * xh))
        dn[s, :] = dd
        ddb = dd.astype(BF)
        db[s, :] = ddb
        gv[4:5, :] += jnp.sum(ct * xh, axis=0, keepdims=True)
        gv[5:6, :] += jnp.sum(ct, axis=0, keepdims=True)
        gv[3:4, :] += jnp.sum(ddb.astype(F32), axis=0, keepdims=True)
        return c
    lax.fori_loop(0, rows // CK, ln2, 0)
    for j in range(4):
        for m in range(nm):
            s = slice(m * 128, (m + 1) * 128)
            dh = mm(db[s, WIN[j]:WIN[j] + 256], wfp[j], NT)
            dp = (dh * dpre[j, s, :].astype(F32)).astype(BF)
            dpre[j, s, :] = dp
            gv[8 + j:9 + j, :] += jnp.sum(dp.astype(F32), axis=0, keepdims=True)
        dn[:, WIN[j]:WIN[j] + 256] += mm(dpre[j], wip[j], NT)
    def lnb(t, c):
        s = pl.ds(pl.multiple_of(t * CK, CK), CK)
        g = dn[s, :]
        xh = attn[s, :]
        u = g * v(1)
        dd = st[s, 0:1] * (u - rowmean(u) - xh * rowmean(u * xh))
        d1[s, :] = dd
        ddb = dd.astype(BF)
        da[s, :] = ddb
        gv[1:2, :] += jnp.sum(g * xh, axis=0, keepdims=True)
        gv[2:3, :] += jnp.sum(g, axis=0, keepdims=True)
        gv[0:1, :] += jnp.sum(ddb.astype(F32), axis=0, keepdims=True)
        return c
    lax.fori_loop(0, rows // CK, lnb, 0)
    dc = mm(wout[...], da[...], NT).astype(BF)
    for m in range(nm):
        for g in range(4):
            dct[m * 4 + g] = dc[g * GW:g * GW + GW, m * 128:(m + 1) * 128]
    send()
    ct = jnp.concatenate([tall(ctxt, m) for m in range(nm)], axis=1)
    nt = jnp.transpose(n1b[...])
    dbt = jnp.transpose(db[...])
    if chains is None:
        x.ga[...] = mm(ct, da[...]).astype(BF)
        for j in range(4):
            o = WIN[j] + OFF[j]
            x.gi[:, j * D:(j + 1) * D] = mm(nt[o:o + 192, :], dpre[j]).astype(BF)
            x.gf[j * 192:(j + 1) * 192, :] = mm(dbt[o:o + 192, :], hid[j]).astype(BF)
        return
    for s in range(3):
        val = mm(ct, da[:, s * 256:s * 256 + 256])
        for f in range(2):
            for k in range(2):
                put(x.Ab, f, (2 * s + k) * 384, val[f * 384:f * 384 + 384, k * 128:k * 128 + 128])
    low = iota((16, 128), 0)
    for f in range(2):
        for b in range(16):
            two = []
            for k in (2 * b, 2 * b + 1):
                if k < 18:
                    at = f * 384 + (k % 3) * 128
                    two.append(gv[k // 3:k // 3 + 1, at:at + 128])
                elif k < 30:
                    row, at = 8 + 2 * f + (k - 18) // 6, (k - 18) % 6 * 128
                    two.append(gv[row:row + 1, at:at + 128])
                else:
                    two.append(jnp.zeros((1, 128), F32))
            x.Ab[b // 8, f, (b // 4) % 2, b % 4, 144:160, :] = jnp.where(low == 0, two[0], jnp.where(low == 1, two[1], 0.0)).astype(BF)
    chains["A"].step(0)
    for j in range(4):
        o = WIN[j] + OFF[j]
        val = mm(nt[o:o + 192, :], dpre[j])
        for f in range(2):
            for s in range(6):
                put(x.Bb, f, (j * 6 + s) * 96, val[f * 96:f * 96 + 96, s * 128:s * 128 + 128])
    chains["B"].step(0)
    for j in range(4):
        o = WIN[j] + OFF[j]
        val = mm(dbt[o:o + 192, :], hid[j])
        for f in range(2):
            for s in range(3):
                at = f * 384 + s * 128
                put(x.Cb, f, s * 768 + j * 192, val[:, at:at + 128])
    chains["C"].step(0)


def remote_copy(src, dst, ssem, rsem, f, c):
    return pltpu.make_async_remote_copy(src_ref=src, dst_ref=dst, send_sem=ssem, recv_sem=rsem, device_id=(f, c), device_id_type=MESH)


VECTORS = ("out_bias", "norm1_gain", "norm1_bias", "ffo_bias", "norm2_gain", "norm2_bias", "q_bias", "value_bias")
LEN = {"A": 160, "B": 144, "C": 144}


def pieces(base, rows):
    out, at = [], 0
    while at < rows:
        b, w = divmod(base + at, 144)
        size = min(144 - w, rows - at)
        out.append((b, w, at, size))
        at += size
    return out


def put(ref, f, base, val):
    for b, w, at, size in pieces(base, val.shape[0]):
        ref[b // 8, f, (b // 4) % 2, b % 4, w:w + size, :] = val[at:at + size].astype(BF)


class Chain:
    def __init__(self, order, f, c, refs):
        self.order, self.f, self.c = order, f, c
        self.b, self.c1, self.c2, self.c3, self.c4, self.out, self.ss, self.rs = refs
        self.r, self.x, self.z = lax.rem(c, 2), lax.rem(lax.div(c, 2), 2), lax.div(c, 4)
        self.started = []

    def core(self):
        return self.f, self.c + 1 - 2 * self.r

    def along_x(self):
        return self.f, self.c + 2 - 4 * self.x

    def along_z(self, d):
        return self.f, lax.rem(self.c + 4 * d, 16)

    def copy(self, k, src, dst, to):
        return remote_copy(src, dst, self.ss.at[k], self.rs.at[k], *to)

    def moves(self, k):
        b, r, f, x, z, o = self.b, self.r, self.f, self.x, self.z, self.out
        zs = [(d, lax.rem(z + d, 4)) for d in (1, 2, 3)]
        y = (1 - f, self.c)
        if k == 0:
            return [(0, b.at[1 - r], self.c1, self.core())]
        if k == 6:
            return [(4, o.at[r], o.at[r], self.core())]
        if self.order == "yxz":
            return {1: [(1, b.at[r, 1 - f], self.c2, y)],
                    2: [(2, b.at[r, f, 1 - x], self.c3, self.along_x())],
                    3: [(4 + d, b.at[r, f, x, t], self.c4.at[z], self.along_z(d)) for d, t in zs],
                    4: [(7 + d, o.at[r, x, z], o.at[r, x, z], self.along_z(d)) for d, t in zs],
                    5: [(3, o.at[r, x], o.at[r, x], self.along_x())]}[k]
        return {1: [(4 + d, b.at[r, :, :, t], self.c4.at[z], self.along_z(d)) for d, t in zs],
                2: [(1, b.at[r, 1 - f, :, z], self.c2, y)],
                3: [(2, b.at[r, f, 1 - x, z], self.c3, self.along_x())],
                4: [(3, o.at[r, x, z], o.at[r, x, z], self.along_x())],
                5: [(7 + d, o.at[r, :, z], o.at[r, :, z], self.along_z(d)) for d, t in zs]}[k]

    def start(self, k):
        for mv in self.moves(k):
            self.copy(*mv).start()

    def received(self, k):
        for mv in self.moves(k):
            self.copy(*mv).wait_recv()

    def sent(self):
        for k in range(7):
            for mv in self.moves(k):
                self.copy(*mv).wait_send()

    def add(self, k):
        b, r, f, x, z, o = self.b, self.r, self.f, self.x, self.z, self.out
        up = lambda v: v.astype(F32)
        others = [lax.rem(z + 4 - d, 4) for d in (1, 2, 3)]
        if k == 0:
            def one(t, carry):
                i, j, l = t // 8, lax.rem(t // 4, 2), lax.rem(t, 4)
                b[r, i, j, l] = (up(b[r, i, j, l]) + up(self.c1[i, j, l])).astype(BF)
                return carry
            lax.fori_loop(0, 16, one, 0)
        elif self.order == "yxz" and k == 1:
            def one(t, carry):
                j, l = t // 4, lax.rem(t, 4)
                b[r, f, j, l] = (up(b[r, f, j, l]) + up(self.c2[j, l])).astype(BF)
                return carry
            lax.fori_loop(0, 8, one, 0)
        elif self.order == "yxz" and k == 2:
            for l in range(4):
                b[r, f, x, l] = (up(b[r, f, x, l]) + up(self.c3[l])).astype(BF)
        elif self.order == "yxz" and k == 3:
            o[r, x, z] = (up(b[r, f, x, z]) + sum(up(self.c4[t]) for t in others)).astype(BF)
        elif self.order == "zyx" and k == 1:
            for i in range(2):
                for j in range(2):
                    b[r, i, j, z] = (up(b[r, i, j, z]) + sum(up(self.c4[t, i, j]) for t in others)).astype(BF)
        elif self.order == "zyx" and k == 2:
            for j in range(2):
                b[r, f, j, z] = (up(b[r, f, j, z]) + up(self.c2[j])).astype(BF)
        elif self.order == "zyx" and k == 3:
            o[r, x, z] = (up(b[r, f, x, z]) + up(self.c3[...])).astype(BF)

    def step(self, k):
        if k > 0:
            self.received(k - 1)
            self.add(k - 1)
        if k < 7:
            self.start(k)


def tile_at(q, t, half):
    p, mir = lax.rem(q, half // 2), lax.div(q, half // 2)
    b = lax.div(t + half - 1 - p, 2 * half)
    i = p + b * (half - 1 - 2 * p)
    j = t - b * (half + 1 + p)
    last = 2 * half - 1
    return b, i + mir * (last - 2 * i), j + mir * (last - 2 * j)


def rows_at(q, half):
    p, mir = lax.rem(q, half // 2), lax.div(q, half // 2)
    last = 2 * half - 1
    return [i + mir * (last - 2 * i) for i in (p, half - 1 - p)]


def in_parts(half, part):
    count = 3 * half + 1
    if count <= 13:
        part(0, count)
    else:
        size = max(d for d in range(1, 9) if count % d == 0)
        lax.fori_loop(0, count // size, lambda t, carry: (part(t * size, size), carry)[1], 0)


def forward_tiles(q, half, qt, ka, vt, acc):
    acc[...] = jnp.zeros_like(acc)
    def part(first, count):
        items = [(h,) + tile_at(q, first + t, half) for t in range(count) for h in range(3)]
        def front(it):
            h, _, i, j = it
            return mm(ka[h, j], qt[h, i])
        ready = [front(it) for it in items[:3]]
        for t, (h, b, i, j) in enumerate(items):
            if t + 3 < len(items):
                ready.append(front(items[t + 3]))
            e = jnp.exp(ready[t]).astype(BF)
            ready[t] = None
            acc[h, b] += mm(vt[h, j], e)
    in_parts(half, part)


def backward_tiles(q, half, qt, ka, kt, va, dnt, dq, dk, dv):
    dq[...] = jnp.zeros_like(dq)
    def part(first, count):
        items = [(h,) + tile_at(q, first + t, half) for t in range(count) for h in range(3)]
        def front(it):
            h, _, i, j = it
            return mm(ka[h, j], qt[h, i]), mm(va[h, j, :, 0:80], dnt[h, i])
        ready = [front(it) for it in items[:2]]
        for t, (h, b, i, j) in enumerate(items):
            if t + 2 < len(items):
                ready.append(front(items[t + 2]))
            s, dp = ready[t]
            ready[t] = None
            e = jnp.exp(s)
            eb = e.astype(BF)
            ds = (e * dp).astype(BF)
            dq[h, b] += mm(kt[h, j], ds)
            dk[h, j] += mm(qt[h, i, 0:64], ds, NT)
            dv[h, j] += mm(dnt[h, i, 0:64], eb, NT)
    in_parts(half, part)


def prep_block(i, xt, wa, wat, qt, ka, vt, kt, va):
    x = jnp.concatenate([xt[2 * i], xt[2 * i + 1]], axis=1)
    seg = x[GW:GW + 16].astype(F32)[0:1].astype(jnp.int32)
    r = iota((48, 256), 0)
    aug = jnp.where((r == seg) & (r < 32) | (r == 32), 1.0, 0.0).astype(BF)
    xa = jnp.concatenate([x[0:GW], aug], axis=0)
    xn = jnp.transpose(xa)
    q = mm(wat[0], xa).astype(BF)
    k = mm(wat[1], xa).astype(BF)
    v = mm(wat[2], xa).astype(BF)
    kn = mm(xn, wa[1]).astype(BF)
    vn = mm(xn, wa[2]).astype(BF)
    for h in range(3):
        o = h * 128
        qt[h, i] = q[o:o + 128]
        anchor = jnp.sum(q[o:o + 64].astype(F32) * k[o:o + 64].astype(F32), axis=0, keepdims=True)
        qt[h, i, 96:112] = jnp.where(iota((16, 256), 0) == 0, -anchor, 0.0).astype(BF)
        ka[h, i] = kn[:, o:o + 128]
        vt[h, i] = v[o:o + 80]
        kt[h, i] = k[o:o + 64]
        va[h, i] = vn[:, o:o + 128]


def mega(n, fast, x):
    f, c = lax.axis_index("fsdp"), lax.axis_index("ctx")
    g, m, mine = unit_of(c, n)
    u = m * 4 + g
    own = owners(n)
    sb, half = n // 2, n // 4
    r = lax.rem(c, 2)
    tok, dnt = x.tok, x.vt
    bar = pltpu.get_barrier_semaphore()
    for d in range(1, n):
        pl.semaphore_signal(bar, inc=1, device_id=(f, lax.rem(c + d, n)), device_id_type=MESH)
    greeted = n - 1
    if fast:
        for p in range(4):
            pl.semaphore_signal(bar, inc=1, device_id=(1 - f, g * 4 + p), device_id_type=MESH)
        greeted += 4
        fetch = [pltpu.make_async_copy(x.wo, x.wout.at[pl.ds(f * 384, 384)], x.lsem.at[0]),
                 pltpu.make_async_copy(x.wi, x.wint.at[pl.ds(f * 96, 96)], x.lsem.at[1]),
                 pltpu.make_async_copy(x.wf, x.wffo.at[pl.ds(f * 384, 384)], x.lsem.at[2]),
                 pltpu.make_async_copy(x.cot_in, x.cot, x.lsem.at[3])]
        for cp in fetch:
            cp.start()
    for k in range(MICRO):
        t = jnp.transpose(tok[k * 128:k * 128 + 128, :])
        sg = jnp.broadcast_to(x.seg[k:k + 1, :].astype(F32), (16, 128)).astype(BF)
        for j in range(4):
            x.tsend[k * 4 + j, 0:GW, :] = t[j * GW:j * GW + GW]
            x.tsend[k * 4 + j, GW:CH, :] = sg
    if fast:
        own_rows = [getattr(x, k)[...].astype(F32).reshape(1, 384) for k in VECTORS]
        inter = x.inter_bias[...].astype(F32).reshape(1, 1536)
        own_rows += [inter[:, k * 384:k * 384 + 384] for k in range(4)]
        x.vbuf[f] = jnp.concatenate(own_rows + [jnp.zeros((4, 384), F32)], axis=0).astype(BF)
    pl.semaphore_wait(bar, greeted)

    def spread(src, dst, ss, rs, start):
        for k in range(12):
            @pl.when(c != own[k])
            def _():
                cp = remote_copy(src.at[k], dst.at[c], ss.at[k], rs.at[c], f, own[k])
                cp.start() if start else cp.wait_send()
            if start:
                @pl.when(c == own[k])
                def _():
                    pltpu.make_async_copy(src.at[k], dst.at[c], rs.at[c]).start()
    def arrived(src, dst, rs, s):
        @pl.when(c != s)
        def _():
            remote_copy(src.at[0], dst.at[s], x.ls, rs.at[s], f, s).wait_recv()
        @pl.when(c == s)
        def _():
            pltpu.make_async_copy(src.at[0], dst.at[s], rs.at[s]).wait()
    def give(src, dst, ss, rs, t, start):
        @pl.when(c != t)
        def _():
            cp = remote_copy(src.at[t], dst.at[u], ss.at[t], rs.at[u], f, t)
            cp.start() if start else cp.wait_send()
        if start:
            @pl.when(c == t)
            def _():
                pltpu.make_async_copy(src.at[t], dst.at[u], rs.at[u]).start()
    def taken(src, dst, rs):
        for k in range(12):
            @pl.when(c != own[k])
            def _():
                remote_copy(src.at[0], dst.at[k], x.ls, rs.at[k], f, own[k]).wait_recv()
            @pl.when(c == own[k])
            def _():
                pltpu.make_async_copy(src.at[0], dst.at[k], rs.at[k]).wait()

    if fast:
        sib = c + 1 - 2 * r
        parts = ((x.wo, x.wout, 384), (x.wi, x.wint, 96), (x.wf, x.wffo, 384))
        def window(j, k):
            return remote_copy((x.wq, x.wk, x.wv)[j].at[:, WIN[k]:WIN[k] + 256], x.qrem.at[j], x.wss.at[6 + j], x.wrs.at[6 + j], 1 - f, c)
        def vectors():
            return remote_copy(x.vbuf.at[f], x.vbuf.at[f], x.wss.at[9], x.wrs.at[9], 1 - f, c)
        def half_over(j):
            src, dst, rows = parts[j]
            h = rows // 2
            return remote_copy(src.at[pl.ds(r * h, h)], dst.at[pl.ds(f * rows + r * h, h)], x.wss.at[j], x.wrs.at[j], 1 - f, c)
        def relay(j, back=False):
            _, dst, rows = parts[j]
            h = rows // 2
            at = pl.ds((1 - f) * rows + r * h, h)
            return remote_copy(dst.at[at], dst.at[at], x.wss.at[3 + j], x.wrs.at[3 + j], f, sib)
        @pl.when(mine)
        def _():
            for k in range(4):
                @pl.when(g == k)
                def _():
                    for j in range(3):
                        window(j, k).start()
        vectors().start()
    spread(x.tsend, x.xt, x.tss, x.trs, True)
    if fast:
        for j in range(3):
            half_over(j).start()
        def pass_on(j):
            half_over(j).wait_recv()
            relay(j).start()

    if fast:
        vectors().wait_recv()
        for k in range(2):
            for j in range(8):
                x.vec[j:j + 1, k * 384:k * 384 + 384] = x.vbuf[k, 0:16, :].astype(F32)[j:j + 1, :]
            for j in range(4):
                row, at = 8 + 2 * k + j // 2, (j % 2) * 384
                x.vec[row:row + 1, at:at + 384] = x.vbuf[k, 0:16, :].astype(F32)[8 + j:9 + j, :]

    @pl.when(mine)
    def _():
        for k in range(4):
            @pl.when(g == k)
            def _():
                lanes = slice(k * GW, k * GW + GW)
                if not fast:
                    x.w[...] = x.wqkv[:, :, lanes]
                else:
                    for j in range(3):
                        window(j, k).wait_recv()
                        for h in range(2):
                            @pl.when(f == h)
                            def _():
                                x.w[j, h * 96:h * 96 + 96, :] = (x.wq, x.wk, x.wv)[j][:, lanes]
                                x.w[j, 96 - h * 96:192 - h * 96, :] = x.qrem[j, :, OFF[k]:OFF[k] + GW]
                x.bias[0:2, :] = x.vec[6:8, lanes]
        build_weights(x.w, x.bias, x.wa, x.wat)
        def first(i, carry):
            arrived(x.tsend, x.xt, x.trs, 2 * i)
            arrived(x.tsend, x.xt, x.trs, 2 * i + 1)
            prep_block(i, x.xt, x.wa, x.wat, x.qt, x.ka, x.vt, x.kt, x.va)
            return carry
        lax.fori_loop(0, sb, first, 0)

    def forward_step(q, carry):
        @pl.when(mine)
        def _():
            forward_tiles(q, half, x.qt, x.ka, x.vt, x.acc)
            for b, i in enumerate(rows_at(q, half)):
                for h in range(3):
                    a = x.acc[h, b]
                    v = a[0:64] / a[64:65]
                    x.cf[i, h * 64:h * 64 + 64, :] = v
                    x.lsum[i, h:h + 1, :] = a[64:65]
                    vb = v.astype(BF)
                    x.csend[2 * i, h * 64:h * 64 + 64, :] = vb[:, 0:128]
                    x.csend[2 * i + 1, h * 64:h * 64 + 64, :] = vb[:, 128:256]
                give(x.csend, x.crecv, x.css, x.crs, 2 * i, True)
                give(x.csend, x.crecv, x.css, x.crs, 2 * i + 1, True)
        if fast:
            for j in range(3):
                @pl.when(q == j)
                def _():
                    pass_on(j)
        return carry
    lax.fori_loop(0, half, forward_step, 0)
    @pl.when(mine)
    def _():
        x.dk[...] = jnp.zeros_like(x.dk)
        x.dv[...] = jnp.zeros_like(x.dv)

    if fast:
        for cp in fetch:
            cp.wait()
        for j in range(3):
            relay(j).wait_recv()
        chains = {k: Chain(o, f, c, [getattr(x, k + s) for s in ("b", "1", "2", "3", "4", "o", "ss", "rs")])
                  for k, o in (("A", "yxz"), ("B", "zyx"), ("C", "yxz"))}
    pad_weights(x.wint, x.wffo, x.wip, x.wfp)
    taken(x.csend, x.crecv, x.crs)
    def send_dct():
        spread(x.dsend, x.dc, x.dss, x.drs, True)
    dense_body(MICRO * 128, x, send_dct, chains if fast else None)

    if fast:
        chains["A"].step(1)
        chains["B"].step(1)
    else:
        x.gw[...] = jnp.zeros_like(x.gw)
        x.gb[...] = jnp.zeros_like(x.gb)

    def backward_step(q, carry):
        @pl.when(mine)
        def _():
            for b, i in enumerate(rows_at(q, half)):
                arrived(x.dsend, x.dc, x.drs, 2 * i)
                arrived(x.dsend, x.dc, x.drs, 2 * i + 1)
                d = jnp.concatenate([x.dc[2 * i], x.dc[2 * i + 1]], axis=1).astype(F32)
                for h in range(3):
                    dh = d[h * 64:h * 64 + 64]
                    inv = 1.0 / x.lsum[i, h:h + 1, :]
                    delta = jnp.sum(dh * x.cf[i, h * 64:h * 64 + 64, :], axis=0, keepdims=True) * inv
                    dnt[h, i] = jnp.concatenate([dh * inv, jnp.where(iota((16, 256), 0) == 0, -delta, 0.0)], axis=0).astype(BF)
            backward_tiles(q, half, x.qt, x.ka, x.kt, x.va, dnt, x.dq, x.dk, x.dv)
            for b, i in enumerate(rows_at(q, half)):
                for h in range(3):
                    x.dqt[i, h * 64:h * 64 + 64, :] = (x.dq[h, b] * 0.125).astype(BF)
        if fast:
            for k in range(4):
                @pl.when(q == k)
                def _():
                    chains["A"].step(k + 2)
                    chains["B"].step(k + 2)
                    chains["C"].step(k + 1)
        return carry
    lax.fori_loop(0, half, backward_step, 0)

    xsend = x.csend
    @pl.when(mine)
    def _():
        for t in range(n):
            give(x.csend, x.crecv, x.css, x.crs, t, False)
        x.gacc[...] = jnp.zeros_like(x.gacc)
        x.gbacc[...] = jnp.zeros_like(x.gbacc)
        ones = jnp.ones((8, 256), BF)
        def post(i, carry):
            xb = jnp.concatenate([x.xt[2 * i, 0:GW, :], x.xt[2 * i + 1, 0:GW, :]], axis=1)
            q = x.dqt[i]
            k = jnp.concatenate([x.dk[h, i] for h in range(3)], axis=0).astype(BF)
            v = jnp.concatenate([x.dv[h, i] for h in range(3)], axis=0).astype(BF)
            x2 = (mm(x.w[0], q) + mm(x.w[1], k) + mm(x.w[2], v)).astype(BF)
            xsend[2 * i] = x2[:, 0:128]
            xsend[2 * i + 1] = x2[:, 128:256]
            give(xsend, x.xrecv, x.xss, x.xrs, 2 * i, True)
            give(xsend, x.xrecv, x.xss, x.xrs, 2 * i + 1, True)
            x.gacc[0] += mm(xb, q, NT)
            x.gacc[1] += mm(xb, k, NT)
            x.gacc[2] += mm(xb, v, NT)
            x.gbacc[0] += mm(ones, q, NT)
            x.gbacc[1] += mm(ones, v, NT)
            return carry
        lax.fori_loop(0, sb, post, 0)
        if fast:
            low = iota((96, 64), 0)
            bb = jnp.zeros((96, 64), F32)
            for k in range(2):
                for i in range(3):
                    bb = jnp.where(low == 3 * k + i, x.gbacc[k, 0:1, i * 64:i * 64 + 64], bb)
            for h in range(2):
                cat = jnp.concatenate([x.gacc[k, h * 96:h * 96 + 96, :] for k in range(3)] + [bb], axis=1).astype(BF)
                for s in range(5):
                    x.qs[h, s * 96:s * 96 + 96, :] = cat[:, s * 128:s * 128 + 128]
        else:
            for k in range(4):
                @pl.when(g == k)
                def _():
                    x.gw[:, :, k * GW:k * GW + GW] = x.gacc[...].astype(BF)
                    x.gb[0:1, k * GW:k * GW + GW] = x.gbacc[0, 0:1]
                    x.gb[1:2, k * GW:k * GW + GW] = x.gbacc[1, 0:1]

    if fast:
        def to_sum(h, t):
            return remote_copy(x.qs.at[h, pl.ds(t * 160, 160)], x.qr.at[f * 3 + m], x.qss.at[h * 3 + t], x.qrs.at[f * 3 + m], h, place_at(g, t))
        def stay():
            return pltpu.make_async_copy(x.qs.at[f, pl.ds(m * 160, 160)], x.qr.at[f * 3 + m], x.qrs.at[f * 3 + m])
        def place_at(g, t):
            return g * 4 + t + lax.rem(g, 2)
        def to_all(d):
            return remote_copy(x.qb.at[u], x.qb.at[u], x.qbs.at[d], x.qbr.at[u], f, lax.rem(c + d, n))
        def elsewhere(h, t):
            return (f != h) | (m != t)
        @pl.when(mine)
        def _():
            for h in range(2):
                for t in range(3):
                    @pl.when(elsewhere(h, t))
                    def _():
                        to_sum(h, t).start()
            stay().start()
        chains["A"].step(6)
        chains["B"].step(6)
        chains["C"].step(5)
        @pl.when(mine)
        def _():
            for h in range(2):
                for t in range(3):
                    @pl.when(elsewhere(h, t))
                    def _():
                        remote_copy(x.qs.at[0, pl.ds(0, 160)], x.qr.at[h * 3 + t], x.ls, x.qrs.at[h * 3 + t], h, place_at(g, t)).wait_recv()
            stay().wait()
            x.qb[u] = sum(x.qr[k].astype(F32) for k in range(6)).astype(BF)
            for d in range(1, n):
                to_all(d).start()
        chains["C"].step(6)
        for k in range(12):
            @pl.when(c != own[k])
            def _():
                remote_copy(x.qb.at[k], x.qb.at[k], x.ls, x.qbr.at[k], f, own[k]).wait_recv()

    taken(xsend, x.xrecv, x.xrs)
    if fast:
        for k in "ABC":
            chains[k].step(7)
            chains[k].sent()
        vectors().wait_send()
        for j in range(3):
            half_over(j).wait_send()
            relay(j).wait_send()
        @pl.when(mine)
        def _():
            for j in range(3):
                window(j, 0).wait_send()
            for h in range(2):
                for t in range(3):
                    @pl.when(elsewhere(h, t))
                    def _():
                        to_sum(h, t).wait_send()
            for d in range(1, n):
                to_all(d).wait_send()
    else:
        for k in range(MICRO):
            t = jnp.concatenate([x.xrecv[k * 4 + j] for j in range(4)], axis=0).astype(F32)
            s = slice(k * 128, k * 128 + 128)
            x.grad[s, :] = (jnp.transpose(t) + x.d1[s, :]).astype(BF)
    spread(x.tsend, x.xt, x.tss, x.trs, False)
    spread(x.dsend, x.dc, x.dss, x.drs, False)
    @pl.when(mine)
    def _():
        for t in range(n):
            give(xsend, x.xrecv, x.xss, x.xrs, t, False)


DMA = pltpu.SemaphoreType.DMA
S, V = jax.ShapeDtypeStruct, pltpu.VMEM


def common_scratch(n):
    rows, sb = MICRO * 128, n // 2
    return dict(
        tsend=V((12, CH, 128), BF), xt=V((n, CH, 128), BF), csend=V((n, GW, 128), BF), crecv=V((12, GW, 128), BF),
        dsend=V((12, GW, 128), BF), dc=V((n, GW, 128), BF),
        w=V((3, GW, GW), BF), bias=V((8, GW), F32), wa=V((3, XA, 384), BF), wat=V((3, 384, XA), BF),
        qt=V((3, sb, 128, 256), BF), ka=V((3, sb, 256, 128), BF), vt=V((3, sb, 80, 256), BF), kt=V((3, sb, 64, 256), BF), va=V((3, sb, 256, 128), BF),
        cf=V((sb, GW, 256), F32), lsum=V((sb, 8, 256), F32), acc=V((3, 2, 80, 256), F32), dq=V((3, 2, 64, 256), F32),
        dk=V((3, sb, 64, 256), F32), dv=V((3, sb, 64, 256), F32), dqt=V((sb, GW, 256), BF), gacc=V((3, GW, GW), F32), gbacc=V((2, 8, GW), F32),
        ctx=V((rows, D), BF), xh=V((rows, D), F32), n1b=V((rows, D), BF), wip=V((4, 256, D), BF), wfp=V((4, D, 256), BF), dpre=V((4, rows, D), BF),
        hid=V((4, rows, D), BF), br=V((rows, D), F32), dn=V((rows, D), F32), db=V((rows, D), BF), st=V((rows, 128), F32),
        tss=DMA((12,)), trs=DMA((n,)), css=DMA((n,)), crs=DMA((12,)), dss=DMA((12,)), drs=DMA((n,)), xss=DMA((n,)), xrs=DMA((12,)), ls=DMA)


class Refs:
    def __init__(self, **k):
        self.__dict__.update(k)


def call(n, fast, ins, outs, scratch, far):
    names, onames = list(ins), list(outs)
    def kernel(*a):
        refs = dict(zip(names, a[:len(names)]))
        refs.update(zip(onames, a[len(names):len(names) + len(onames)]))
        refs.update(a[-1])
        mega(n, fast, Refs(**refs))
    vm = pl.BlockSpec(memory_space=pltpu.VMEM)
    got = pl.pallas_call(
        kernel, out_shape=tuple(outs.values()),
        in_specs=[pl.BlockSpec(memory_space=pl.ANY) if k in far else vm for k in names], out_specs=(vm,) * len(onames),
        scratch_shapes=[scratch],
        compiler_params=pltpu.CompilerParams(collective_id=0, has_side_effects=True, vmem_limit_bytes=60 * 2**20))(*ins.values())
    return dict(zip(onames, got))


def run_whole(n, ins):
    rows = MICRO * 128
    outs = dict(out=S((rows, D), BF), grad=S((rows, D), BF), gw=S((3, GW, D), BF), gb=S((8, D), F32), ga=S((D, D), BF), gi=S((192, FF), BF),
                gf=S((D, D), BF), gv=S((16, D), F32))
    scratch = common_scratch(n)
    scratch.update(xrecv=V((12, GW, 128), BF), d1=V((rows, D), F32))
    return call(n, False, ins, outs, scratch, ())


def run_fast(n, ins):
    rows = MICRO * 128
    outs = dict(out=S((rows, D), BF), xrecv=S((12, GW, 128), BF), d1=S((rows, D), F32), qb=S((12, 160, 128), BF))
    for k in "ABC":
        outs[k + "o"] = S((2, 2, 4, LEN[k], 128), BF)
    scratch = common_scratch(n)
    scratch.update(cot=V((rows, D), BF), wout=V((D, D), BF), wint=V((192, FF), BF), wffo=V((D, D), BF), vec=V((16, D), F32), vbuf=V((2, 16, 384), BF),
                   qrem=V((3, 96, 256), BF), gv=V((16, D), F32), qs=V((2, 480, 128), BF), qr=V((6, 160, 128), BF),
                   lsem=DMA((4,)), wss=DMA((10,)), wrs=DMA((10,)), qss=DMA((6,)), qrs=DMA((6,)), qbs=DMA((n,)), qbr=DMA((12,)))
    for k in "ABC":
        l = LEN[k]
        scratch[k + "b"] = V((2, 2, 2, 4, l, 128), BF)
        scratch[k + "1"] = V((2, 2, 4, l, 128), BF)
        scratch[k + "2"] = V((2, l, 128) if k == "B" else (2, 4, l, 128), BF)
        scratch[k + "3"] = V((l, 128) if k == "B" else (4, l, 128), BF)
        scratch[k + "4"] = V((4, 2, 2, l, 128) if k == "B" else (4, l, 128), BF)
        scratch[k + "ss"] = DMA((11,))
        scratch[k + "rs"] = DMA((11,))
    return call(n, True, ins, outs, scratch, ("wo", "wi", "wf", "cot_in"))


def finish(out, xrecv, d1, qb, a, b, c, o_out, o_grad, o_q, o_k, o_v, o_qb, o_vb, o_w, o_b, o_g1, o_s1, o_i, o_ib, o_f, o_fb, o_g2, o_s2):
    f = lax.axis_index("fsdp")
    o_out[...] = out[...]
    for k in range(MICRO):
        t = jnp.concatenate([xrecv[k * 4 + j] for j in range(4)], axis=0).astype(F32)
        s = slice(k * 128, k * 128 + 128)
        o_grad[s, :] = (jnp.transpose(t) + d1[s, :]).astype(BF)
    def slab(ref, base, rows):
        got = [ref[b // 8, (b // 4) % 2, b % 4, w:w + size, :] for b, w, _, size in pieces(base, rows)]
        return jnp.concatenate(got, axis=0).astype(F32) if len(got) > 1 else got[0].astype(F32)
    for s in range(6):
        o_w[:, s * 128:s * 128 + 128] = slab(a, s * 384, 384)
    for s in range(24):
        o_i[:, s * 128:s * 128 + 128] = slab(b, s * 96, 96)
    for s in range(3):
        o_f[s * 128:s * 128 + 128, :] = jnp.transpose(slab(c, s * 768, 768))
    cats, qbs, vbs = [], [], []
    for g in range(4):
        rows = jnp.concatenate([qb[t * 4 + g] for t in range(3)], axis=0).astype(F32)
        cat = jnp.concatenate([rows[s * 96:s * 96 + 96] for s in range(5)], axis=1)
        cats.append(cat)
        qbs.append(jnp.concatenate([cat[i:i + 1, 576:640] for i in range(3)], axis=1))
        vbs.append(jnp.concatenate([cat[3 + i:4 + i, 576:640] for i in range(3)], axis=1))
    for k, o in enumerate((o_q, o_k, o_v)):
        o[...] = jnp.concatenate([cat[:, k * GW:k * GW + GW] for cat in cats], axis=1)
    pick = lambda v: jnp.where(f == 0, jnp.concatenate(v[0:2], axis=1), jnp.concatenate(v[2:4], axis=1))
    o_qb[...] = pick(qbs).reshape(384)
    o_vb[...] = pick(vbs).reshape(384)
    rows = []
    for k in range(30):
        b = k // 2
        rows.append(a[b // 8, (b // 4) % 2, b % 4, 144:160, :].astype(F32)[k % 2:k % 2 + 1, :])
    for i, o in enumerate((o_b, o_g1, o_s1, o_fb, o_g2, o_s2)):
        o[...] = jnp.concatenate(rows[3 * i:3 * i + 3], axis=1).reshape(384)
    o_ib[...] = jnp.concatenate(rows[18:30], axis=1).reshape(1536)


def local(tokens, cotangent, segment_ids, q_weight, key_weight, value_weight, q_bias, value_bias, out_weight, out_bias,
          norm1_gain, norm1_bias, inter_weight, inter_bias, ffo_weight, ffo_bias, norm2_gain, norm2_bias):
    n, nf = lax.axis_size("ctx"), lax.axis_size("fsdp")
    rows = MICRO * 128
    tok, cot, seg = tokens.reshape(rows, D), cotangent.reshape(rows, D), segment_ids.reshape(MICRO, 128)
    dl = q_bias.shape[0]
    if n == 16 and nf == 2:
        x = run_fast(n, dict(tok=tok, seg=seg, cot_in=cot, wq=q_weight, wk=key_weight, wv=value_weight, wo=out_weight, wi=inter_weight, wf=ffo_weight,
                             out_bias=out_bias, norm1_gain=norm1_gain, norm1_bias=norm1_bias, ffo_bias=ffo_bias, norm2_gain=norm2_gain,
                             norm2_bias=norm2_bias, q_bias=q_bias, value_bias=value_bias, inter_bias=inter_bias))
        vm = pl.BlockSpec(memory_space=pltpu.VMEM)
        row = S((dl,), F32)
        outs = (S((rows, D), BF), S((rows, D), BF)) + (S((96, D), F32),) * 3 + (row, row, S((384, D), F32), row, row, row, S((96, FF), F32), S((4 * dl,), F32),
                S((384, D), F32), row, row, row)
        got = pl.pallas_call(
            finish, out_shape=outs, in_specs=[vm] * 7, out_specs=(vm,) * 17,
            compiler_params=pltpu.CompilerParams(vmem_limit_bytes=60 * 2**20))(x["out"], x["xrecv"], x["d1"], x["qb"], x["Ao"], x["Bo"], x["Co"])
        return (got[0].reshape(tokens.shape), got[1].reshape(tokens.shape)) + tuple(got[2:])
    gather = lambda a, ax: lax.all_gather(a, "fsdp", axis=ax, tiled=True)
    pack = jnp.concatenate([out_bias, norm1_gain, norm1_bias, ffo_bias, norm2_gain, norm2_bias, q_bias, value_bias, inter_bias]).reshape(12, dl)
    wqkv = gather(jnp.stack([q_weight, key_weight, value_weight]), 1)
    allv = lax.all_gather(pack, "fsdp", axis=0)
    vec = jnp.concatenate([jnp.swapaxes(allv[:, 0:8], 0, 1).reshape(8, D), allv[:, 8:12].reshape(4, D), jnp.zeros((4, D), BF)], axis=0).astype(F32)
    x = run_whole(n, dict(tok=tok, seg=seg, cot=cot, wqkv=wqkv, wout=gather(out_weight, 0), wint=gather(inter_weight, 0), wffo=gather(ffo_weight, 0), vec=vec))
    gw, gv = x["gw"], x["gv"]
    scatter = lambda a: lax.psum(lax.psum_scatter(a, "fsdp", scatter_dimension=0, tiled=True), "ctx").astype(F32)
    gvec = lax.psum(jnp.concatenate([gv, x["gb"]], axis=0), ("fsdp", "ctx"))
    me = lax.axis_index("fsdp")
    part = lambda i: lax.dynamic_slice(gvec[i], (me * dl,), (dl,))
    gib = lax.dynamic_slice(gvec[8:12].reshape(4 * D), (me * 4 * dl,), (4 * dl,))
    return (x["out"].reshape(tokens.shape), x["grad"].reshape(tokens.shape), scatter(gw[0]), scatter(gw[1]), scatter(gw[2]), part(16), part(17),
            scatter(x["ga"]), part(0), part(1), part(2), scatter(x["gi"]), gib, scatter(x["gf"].T), part(3), part(4), part(5))


def solution(mesh):
    act, seg, mat, vec = P(None, "fsdp", "ctx", None), P(None, "fsdp", "ctx"), P("fsdp", None), P("fsdp")
    return jax.shard_map(
        local, mesh=mesh,
        in_specs=(act, act, seg, mat, mat, mat, vec, vec, mat, vec, vec, vec, mat, vec, mat, vec, vec, vec),
        out_specs=(act, act, mat, mat, mat, vec, vec, mat, vec, vec, vec, mat, vec, mat, vec, vec, vec),
        check_vma=False)
```

```python
import math

import jax
import jax.numpy as jnp
from jax import lax
from jax.experimental import pallas as pl
from jax.experimental.pallas import tpu as pltpu
from jax.sharding import PartitionSpec as P

MESH = pl.DeviceIdType.MESH
MICRO = 3


def place(n, g, m):
    return g * (n // 4) + m + (g % 2)


def owners(n):
    return [place(n, g, m) for m in range(MICRO) for g in range(4)]


def unit_of(c, n):
    g = c // (n // 4)
    m = c - g * (n // 4) - lax.rem(g, 2)
    return g, m, (m >= 0) & (m < MICRO)


BF, F32 = jnp.bfloat16, jnp.float32
HEAD, GW = 64, 192
CH = 208
XA = 240
BIG = 1e9
NN = (((1,), (0,)), ((), ()))
NT = (((1,), (1,)), ((), ()))
TN = (((0,), (0,)), ((), ()))

def mm(a, b, dims=NN):
    return lax.dot_general(a, b, dims, preferred_element_type=F32)

def iota(shape, axis):
    return lax.broadcasted_iota(jnp.int32, shape, axis)

def build_weights(w_ref, b_ref, wa_ref, wat_ref):
    for s in range(3):
        for h in range(3):
            w = w_ref[s, :, h * 64:h * 64 + 64].astype(F32)
            top = jnp.concatenate([w * (0.125 if s == 0 else 1.0), jnp.zeros((GW, 64), F32)], axis=1)
            r, c = iota((48, 128), 0), iota((48, 128), 1)
            same = (c - 64 == r)
            lanes = (c >= 64) & (c < 96) & (r < 32)
            one = (r == 32)
            zero = jnp.zeros((48, 128), F32)
            if s == 0:
                bias = jnp.concatenate([b_ref[0:1, h * 64:h * 64 + 64].astype(F32) * 0.125, jnp.zeros((1, 64), F32)], axis=1)
                low = jnp.where(lanes & same, 1.0, zero) + jnp.where(one, bias, zero)
            elif s == 1:
                low = jnp.where(lanes & ~same, -BIG, zero) + jnp.where(one & (c == 96), 1.0, zero)
            else:
                bias = jnp.concatenate([b_ref[1:2, h * 64:h * 64 + 64].astype(F32), jnp.zeros((1, 64), F32)], axis=1)
                low = jnp.where(one, bias, zero) + jnp.where(one & (c == 64), 1.0, zero)
            full = jnp.concatenate([top, low], axis=0)
            wa_ref[s, :, h * 128:h * 128 + 128] = full.astype(BF)
            wat_ref[s, h * 128:h * 128 + 128, :] = jnp.transpose(full).astype(BF)

D, FF = 768, 3072
EPS = 1e-12
WIN = (0, 128, 384, 512)
OFF = (0, 64, 0, 64)
RS2 = math.sqrt(0.5)
IPI = 1.0 / math.sqrt(2.0 * math.pi)
CK = 32

def rowmean(x):
    return jnp.sum(x, axis=-1, keepdims=True) * (1.0 / D)

def tall(ref, m):
    return jnp.concatenate([ref[m * 4 + g] for g in range(4)], axis=0)


def pad_weights(wint, wffo, wip, wfp):
    for j in range(4):
        o = OFF[j]
        wip[j] = jnp.zeros((256, D), BF)
        wip[j, o:o + 192, :] = wint[:, j * D:(j + 1) * D]
        lane = iota((D, 256), 1)
        w = wffo[:, WIN[j]:WIN[j] + 256]
        wfp[j] = jnp.where((lane >= o) & (lane < o + 192), w.astype(F32), 0.0).astype(BF)


def dense_body(rows, x, send, chains, slot):
    tok, cot, ctxt, wout, out, d1, dct, gv = x.tok, x.cot, x.crecv, x.wout, x.out, x.d1, x.dsend, x.gv
    ctx, attn, n1b, wip, wfp, dpre, hid, br, dn, db, st = x.ctx, x.xh, x.n1b, x.wip, x.wfp, x.dpre, x.hid, x.br, x.dn, x.db, x.st
    da = ctx
    nm = rows // 128
    v = lambda i: x.vec[i:i + 1, :]
    for m in range(nm):
        ctx[m * 128:(m + 1) * 128, :] = jnp.transpose(tall(ctxt, m))
    attn[...] = mm(ctx[...], wout[...])
    def ln1(t, c):
        s = pl.ds(pl.multiple_of(t * CK, CK), CK)
        r = attn[s, :] + v(0) + tok[s, :].astype(F32)
        cen = r - rowmean(r)
        rstd = lax.rsqrt(rowmean(cen * cen) + EPS)
        xh = cen * rstd
        attn[s, :] = xh
        st[s, :] = jnp.broadcast_to(rstd, (CK, 128))
        n = xh * v(1) + v(2)
        n1b[s, :] = n.astype(BF)
        br[s, :] = n + v(3)
        return c
    lax.fori_loop(0, rows // CK, ln1, 0)
    for j in range(4):
        for m in range(nm):
            s = slice(m * 128, (m + 1) * 128)
            u = mm(n1b[s, WIN[j]:WIN[j] + 256], wip[j]) + v(8 + j)
            half = 0.5 + 0.5 * lax.erf(u * RS2)
            hid[j, s, :] = (u * half).astype(BF)
            dpre[j, s, :] = (half + u * (jnp.exp(u * u * -0.5) * IPI)).astype(BF)
        br[:, WIN[j]:WIN[j] + 256] += mm(hid[j], wfp[j])
    gv[...] = jnp.zeros_like(gv)
    def ln2(t, c):
        s = pl.ds(pl.multiple_of(t * CK, CK), CK)
        r = br[s, :]
        cen = r - rowmean(r)
        rstd = lax.rsqrt(rowmean(cen * cen) + EPS)
        xh = cen * rstd
        out[s, :] = (xh * v(4) + v(5)).astype(BF)
        ct = cot[s, :].astype(F32)
        u = ct * v(4)
        dd = rstd * (u - rowmean(u) - xh * rowmean(u * xh))
        dn[s, :] = dd
        ddb = dd.astype(BF)
        db[s, :] = ddb
        gv[4:5, :] += jnp.sum(ct * xh, axis=0, keepdims=True)
        gv[5:6, :] += jnp.sum(ct, axis=0, keepdims=True)
        gv[3:4, :] += jnp.sum(ddb.astype(F32), axis=0, keepdims=True)
        return c
    lax.fori_loop(0, rows // CK, ln2, 0)
    dbt = jnp.transpose(db[...])
    for j in range(4):
        o = WIN[j] + OFF[j]
        val = mm(dbt[o:o + 192, :], hid[j])
        if chains is None:
            x.gf[j * 192:(j + 1) * 192, :] = val.astype(BF)
            continue
        for f in range(2):
            for s in range(3):
                at = f * 384 + s * 128
                put(x.Cb, f, s * 768 + j * 192, val[:, at:at + 128])
    if chains is not None:
        chains["C"].step(0)
    for j in range(4):
        for m in range(nm):
            s = slice(m * 128, (m + 1) * 128)
            dh = mm(db[s, WIN[j]:WIN[j] + 256], wfp[j], NT)
            dp = (dh * dpre[j, s, :].astype(F32)).astype(BF)
            dpre[j, s, :] = dp
            gv[8 + j:9 + j, :] += jnp.sum(dp.astype(F32), axis=0, keepdims=True)
        dn[:, WIN[j]:WIN[j] + 256] += mm(dpre[j], wip[j], NT)
    nt = jnp.transpose(n1b[...])
    for j in range(4):
        o = WIN[j] + OFF[j]
        val = mm(nt[o:o + 192, :], dpre[j])
        if chains is None:
            x.gi[:, j * D:(j + 1) * D] = val.astype(BF)
            continue
        for f in range(2):
            for s in range(6):
                put(x.Bb, f, (j * 6 + s) * 96, val[f * 96:f * 96 + 96, s * 128:s * 128 + 128])
    if chains is not None:
        chains["B"].step(0)
    slot(0)
    def lnb(t, c):
        s = pl.ds(pl.multiple_of(t * CK, CK), CK)
        g = dn[s, :]
        xh = attn[s, :]
        u = g * v(1)
        dd = st[s, 0:1] * (u - rowmean(u) - xh * rowmean(u * xh))
        d1[s, :] = dd
        ddb = dd.astype(BF)
        da[s, :] = ddb
        gv[1:2, :] += jnp.sum(g * xh, axis=0, keepdims=True)
        gv[2:3, :] += jnp.sum(g, axis=0, keepdims=True)
        gv[0:1, :] += jnp.sum(ddb.astype(F32), axis=0, keepdims=True)
        return c
    lax.fori_loop(0, rows // CK, lnb, 0)
    dc = mm(wout[...], da[...], NT).astype(BF)
    for m in range(nm):
        for g in range(4):
            dct[m * 4 + g] = dc[g * GW:g * GW + GW, m * 128:(m + 1) * 128]
    send()
    ct = jnp.concatenate([tall(ctxt, m) for m in range(nm)], axis=1)
    if chains is None:
        x.ga[...] = mm(ct, da[...]).astype(BF)
        return
    for s in range(3):
        val = mm(ct, da[:, s * 256:s * 256 + 256])
        for f in range(2):
            for k in range(2):
                put(x.Ab, f, (2 * s + k) * 384, val[f * 384:f * 384 + 384, k * 128:k * 128 + 128])
    low = iota((16, 128), 0)
    for f in range(2):
        for b in range(16):
            two = []
            for k in (2 * b, 2 * b + 1):
                if k < 18:
                    at = f * 384 + (k % 3) * 128
                    two.append(gv[k // 3:k // 3 + 1, at:at + 128])
                elif k < 30:
                    row, at = 8 + 2 * f + (k - 18) // 6, (k - 18) % 6 * 128
                    two.append(gv[row:row + 1, at:at + 128])
                else:
                    two.append(jnp.zeros((1, 128), F32))
            x.Ab[b // 8, f, (b // 4) % 2, b % 4, 144:160, :] = jnp.where(low == 0, two[0], jnp.where(low == 1, two[1], 0.0)).astype(BF)
    chains["A"].step(0)


def remote_copy(src, dst, ssem, rsem, f, c):
    return pltpu.make_async_remote_copy(src_ref=src, dst_ref=dst, send_sem=ssem, recv_sem=rsem, device_id=(f, c), device_id_type=MESH)


VECTORS = ("out_bias", "norm1_gain", "norm1_bias", "ffo_bias", "norm2_gain", "norm2_bias", "q_bias", "value_bias")
ORDER = {"A": "yxz", "B": "yxz", "C": "yxz"}
SCHEDULE = {"C": (0, 1, 3, 5, 7, 9, 10), "B": (1, 3, 5, 7, 9, 10, 11), "A": (1, 5, 7, 9, 10, 11, 12)}
LEN = {"A": 160, "B": 144, "C": 144}


def pieces(base, rows):
    out, at = [], 0
    while at < rows:
        b, w = divmod(base + at, 144)
        size = min(144 - w, rows - at)
        out.append((b, w, at, size))
        at += size
    return out


def put(ref, f, base, val):
    for b, w, at, size in pieces(base, val.shape[0]):
        ref[b // 8, f, (b // 4) % 2, b % 4, w:w + size, :] = val[at:at + size].astype(BF)


class Chain:
    def __init__(self, order, f, c, refs):
        self.order, self.f, self.c = order, f, c
        self.b, self.c1, self.c2, self.c3, self.c4, self.out, self.ss, self.rs = refs
        self.r, self.x, self.z = lax.rem(c, 2), lax.rem(lax.div(c, 2), 2), lax.div(c, 4)
        self.started = []

    def core(self):
        return self.f, self.c + 1 - 2 * self.r

    def along_x(self):
        return self.f, self.c + 2 - 4 * self.x

    def along_z(self, d):
        return self.f, lax.rem(self.c + 4 * d, 16)

    def copy(self, k, src, dst, to):
        return remote_copy(src, dst, self.ss.at[k], self.rs.at[k], *to)

    def moves(self, k):
        b, r, f, x, z, o = self.b, self.r, self.f, self.x, self.z, self.out
        zs = [(d, lax.rem(z + d, 4)) for d in (1, 2, 3)]
        y = (1 - f, self.c)
        if k == 0:
            return [(0, b.at[1 - r], self.c1, self.core())]
        if k == 6:
            return [(4, o.at[r], o.at[r], self.core())]
        if self.order == "yxz":
            return {1: [(1, b.at[r, 1 - f], self.c2, y)],
                    2: [(2, b.at[r, f, 1 - x], self.c3, self.along_x())],
                    3: [(4 + d, b.at[r, f, x, t], self.c4.at[z], self.along_z(d)) for d, t in zs],
                    4: [(7 + d, o.at[r, x, z], o.at[r, x, z], self.along_z(d)) for d, t in zs],
                    5: [(3, o.at[r, x], o.at[r, x], self.along_x())]}[k]
        return {1: [(4 + d, b.at[r, :, :, t], self.c4.at[z], self.along_z(d)) for d, t in zs],
                2: [(1, b.at[r, 1 - f, :, z], self.c2, y)],
                3: [(2, b.at[r, f, 1 - x, z], self.c3, self.along_x())],
                4: [(3, o.at[r, x, z], o.at[r, x, z], self.along_x())],
                5: [(7 + d, o.at[r, :, z], o.at[r, :, z], self.along_z(d)) for d, t in zs]}[k]

    def start(self, k):
        for mv in self.moves(k):
            self.copy(*mv).start()

    def received(self, k):
        for mv in self.moves(k):
            self.copy(*mv).wait_recv()

    def sent(self):
        for k in range(7):
            for mv in self.moves(k):
                self.copy(*mv).wait_send()

    def add(self, k):
        b, r, f, x, z, o = self.b, self.r, self.f, self.x, self.z, self.out
        up = lambda v: v.astype(F32)
        others = [lax.rem(z + 4 - d, 4) for d in (1, 2, 3)]
        if k == 0:
            def one(t, carry):
                i, j, l = t // 8, lax.rem(t // 4, 2), lax.rem(t, 4)
                b[r, i, j, l] = (up(b[r, i, j, l]) + up(self.c1[i, j, l])).astype(BF)
                return carry
            lax.fori_loop(0, 16, one, 0)
        elif self.order == "yxz" and k == 1:
            def one(t, carry):
                j, l = t // 4, lax.rem(t, 4)
                b[r, f, j, l] = (up(b[r, f, j, l]) + up(self.c2[j, l])).astype(BF)
                return carry
            lax.fori_loop(0, 8, one, 0)
        elif self.order == "yxz" and k == 2:
            for l in range(4):
                b[r, f, x, l] = (up(b[r, f, x, l]) + up(self.c3[l])).astype(BF)
        elif self.order == "yxz" and k == 3:
            o[r, x, z] = (up(b[r, f, x, z]) + sum(up(self.c4[t]) for t in others)).astype(BF)
        elif self.order == "zyx" and k == 1:
            for i in range(2):
                for j in range(2):
                    b[r, i, j, z] = (up(b[r, i, j, z]) + sum(up(self.c4[t, i, j]) for t in others)).astype(BF)
        elif self.order == "zyx" and k == 2:
            for j in range(2):
                b[r, f, j, z] = (up(b[r, f, j, z]) + up(self.c2[j])).astype(BF)
        elif self.order == "zyx" and k == 3:
            o[r, x, z] = (up(b[r, f, x, z]) + up(self.c3[...])).astype(BF)

    def step(self, k):
        if k > 0:
            self.received(k - 1)
            self.add(k - 1)
        if k < 7:
            self.start(k)


def tile_at(q, t, half):
    p, mir = lax.rem(q, half // 2), lax.div(q, half // 2)
    b = lax.div(t + half - 1 - p, 2 * half)
    i = p + b * (half - 1 - 2 * p)
    j = t - b * (half + 1 + p)
    last = 2 * half - 1
    return b, i + mir * (last - 2 * i), j + mir * (last - 2 * j)


def rows_at(q, half):
    p, mir = lax.rem(q, half // 2), lax.div(q, half // 2)
    last = 2 * half - 1
    return [i + mir * (last - 2 * i) for i in (p, half - 1 - p)]


def in_parts(half, part):
    count = 3 * half + 1
    if count <= 13:
        part(0, count)
    else:
        size = max(d for d in range(1, 9) if count % d == 0)
        lax.fori_loop(0, count // size, lambda t, carry: (part(t * size, size), carry)[1], 0)


def forward_tiles(q, half, qt, ka, vt, acc):
    acc[...] = jnp.zeros_like(acc)
    def part(first, count):
        items = [(h,) + tile_at(q, first + t, half) for t in range(count) for h in range(3)]
        def front(it):
            h, _, i, j = it
            return mm(ka[h, j], qt[h, i])
        ready = [front(it) for it in items[:3]]
        for t, (h, b, i, j) in enumerate(items):
            if t + 3 < len(items):
                ready.append(front(items[t + 3]))
            e = jnp.exp(ready[t]).astype(BF)
            ready[t] = None
            acc[h, b] += mm(vt[h, j], e)
    in_parts(half, part)


def backward_tiles(q, half, qt, ka, kt, va, dnt, dq, dk, dv):
    dq[...] = jnp.zeros_like(dq)
    def part(first, count):
        items = [(h,) + tile_at(q, first + t, half) for t in range(count) for h in range(3)]
        def front(it):
            h, _, i, j = it
            return mm(ka[h, j], qt[h, i]), mm(va[h, j, :, 0:80], dnt[h, i])
        ready = [front(it) for it in items[:2]]
        for t, (h, b, i, j) in enumerate(items):
            if t + 2 < len(items):
                ready.append(front(items[t + 2]))
            s, dp = ready[t]
            ready[t] = None
            e = jnp.exp(s)
            eb = e.astype(BF)
            ds = (e * dp).astype(BF)
            dq[h, b] += mm(kt[h, j], ds)
            dk[h, j] += mm(qt[h, i, 0:64], ds, NT)
            dv[h, j] += mm(dnt[h, i, 0:64], eb, NT)
    in_parts(half, part)


def prep_block(i, xt, wa, wat, qt, ka, vt, kt, va):
    x = jnp.concatenate([xt[2 * i], xt[2 * i + 1]], axis=1)
    seg = x[GW:GW + 16].astype(F32)[0:1].astype(jnp.int32)
    r = iota((48, 256), 0)
    aug = jnp.where((r == seg) & (r < 32) | (r == 32), 1.0, 0.0).astype(BF)
    xa = jnp.concatenate([x[0:GW], aug], axis=0)
    xn = jnp.transpose(xa)
    q = mm(wat[0], xa).astype(BF)
    k = mm(wat[1], xa).astype(BF)
    v = mm(wat[2], xa).astype(BF)
    kn = mm(xn, wa[1]).astype(BF)
    vn = mm(xn, wa[2]).astype(BF)
    for h in range(3):
        o = h * 128
        qt[h, i] = q[o:o + 128]
        anchor = jnp.sum(q[o:o + 64].astype(F32) * k[o:o + 64].astype(F32), axis=0, keepdims=True)
        qt[h, i, 96:112] = jnp.where(iota((16, 256), 0) == 0, -anchor, 0.0).astype(BF)
        ka[h, i] = kn[:, o:o + 128]
        vt[h, i] = v[o:o + 80]
        kt[h, i] = k[o:o + 64]
        va[h, i] = vn[:, o:o + 128]


def mega(n, fast, x):
    f, c = lax.axis_index("fsdp"), lax.axis_index("ctx")
    g, m, mine = unit_of(c, n)
    u = m * 4 + g
    own = owners(n)
    sb, half = n // 2, n // 4
    r = lax.rem(c, 2)
    tok, dnt = x.tok, x.vt
    bar = pltpu.get_barrier_semaphore()
    for d in range(1, n):
        pl.semaphore_signal(bar, inc=1, device_id=(f, lax.rem(c + d, n)), device_id_type=MESH)
    greeted = n - 1
    if fast:
        for p in range(4):
            pl.semaphore_signal(bar, inc=1, device_id=(1 - f, g * 4 + p), device_id_type=MESH)
        greeted += 4
        fetch = [pltpu.make_async_copy(x.wo, x.wout.at[pl.ds(f * 384, 384)], x.lsem.at[0]),
                 pltpu.make_async_copy(x.wi, x.wint.at[pl.ds(f * 96, 96)], x.lsem.at[1]),
                 pltpu.make_async_copy(x.wf, x.wffo.at[pl.ds(f * 384, 384)], x.lsem.at[2]),
                 pltpu.make_async_copy(x.cot_in, x.cot, x.lsem.at[3])]
        for cp in fetch:
            cp.start()
    for k in range(MICRO):
        t = jnp.transpose(tok[k * 128:k * 128 + 128, :])
        sg = jnp.broadcast_to(x.seg[k].astype(F32), (16, 128)).astype(BF)
        for j in range(4):
            x.tsend[k * 4 + j, 0:GW, :] = t[j * GW:j * GW + GW]
            x.tsend[k * 4 + j, GW:CH, :] = sg
    if fast:
        own_rows = [getattr(x, k)[...].astype(F32).reshape(1, 384) for k in VECTORS]
        inter = x.inter_bias[...].astype(F32).reshape(1, 1536)
        own_rows += [inter[:, k * 384:k * 384 + 384] for k in range(4)]
        x.vbuf[f] = jnp.concatenate(own_rows + [jnp.zeros((4, 384), F32)], axis=0).astype(BF)
    pl.semaphore_wait(bar, greeted)

    def spread(src, dst, ss, rs, start):
        for k in range(12):
            @pl.when(c != own[k])
            def _():
                cp = remote_copy(src.at[k], dst.at[c], ss.at[k], rs.at[c], f, own[k])
                cp.start() if start else cp.wait_send()
            if start:
                @pl.when(c == own[k])
                def _():
                    pltpu.make_async_copy(src.at[k], dst.at[c], rs.at[c]).start()
    def arrived(src, dst, rs, s):
        @pl.when(c != s)
        def _():
            remote_copy(src.at[0], dst.at[s], x.ls, rs.at[s], f, s).wait_recv()
        @pl.when(c == s)
        def _():
            pltpu.make_async_copy(src.at[0], dst.at[s], rs.at[s]).wait()
    def give(src, dst, ss, rs, t, start):
        @pl.when(c != t)
        def _():
            cp = remote_copy(src.at[t], dst.at[u], ss.at[t], rs.at[u], f, t)
            cp.start() if start else cp.wait_send()
        if start:
            @pl.when(c == t)
            def _():
                pltpu.make_async_copy(src.at[t], dst.at[u], rs.at[u]).start()
    def taken(src, dst, rs):
        for k in range(12):
            @pl.when(c != own[k])
            def _():
                remote_copy(src.at[0], dst.at[k], x.ls, rs.at[k], f, own[k]).wait_recv()
            @pl.when(c == own[k])
            def _():
                pltpu.make_async_copy(src.at[0], dst.at[k], rs.at[k]).wait()

    if fast:
        sib = c + 1 - 2 * r
        parts = ((x.wo, x.wout, 384), (x.wi, x.wint, 96), (x.wf, x.wffo, 384))
        def window(j, k):
            return remote_copy((x.wq, x.wk, x.wv)[j].at[:, WIN[k]:WIN[k] + 256], x.qrem.at[j], x.wss.at[6 + j], x.wrs.at[6 + j], 1 - f, c)
        def vectors():
            return remote_copy(x.vbuf.at[f], x.vbuf.at[f], x.wss.at[9], x.wrs.at[9], 1 - f, c)
        def half_over(j):
            src, dst, rows = parts[j]
            h = rows // 2
            return remote_copy(src.at[pl.ds(r * h, h)], dst.at[pl.ds(f * rows + r * h, h)], x.wss.at[j], x.wrs.at[j], 1 - f, c)
        def relay(j, back=False):
            _, dst, rows = parts[j]
            h = rows // 2
            at = pl.ds((1 - f) * rows + r * h, h)
            return remote_copy(dst.at[at], dst.at[at], x.wss.at[3 + j], x.wrs.at[3 + j], f, sib)
        @pl.when(mine)
        def _():
            for k in range(4):
                @pl.when(g == k)
                def _():
                    for j in range(3):
                        window(j, k).start()
        vectors().start()
    spread(x.tsend, x.xt, x.tss, x.trs, True)
    if fast:
        for j in range(3):
            half_over(j).start()
        def pass_on(j):
            half_over(j).wait_recv()
            relay(j).start()

    if fast:
        vectors().wait_recv()
        for k in range(2):
            for j in range(8):
                x.vec[j:j + 1, k * 384:k * 384 + 384] = x.vbuf[k, 0:16, :].astype(F32)[j:j + 1, :]
            for j in range(4):
                row, at = 8 + 2 * k + j // 2, (j % 2) * 384
                x.vec[row:row + 1, at:at + 384] = x.vbuf[k, 0:16, :].astype(F32)[8 + j:9 + j, :]

    @pl.when(mine)
    def _():
        for k in range(4):
            @pl.when(g == k)
            def _():
                lanes = slice(k * GW, k * GW + GW)
                if not fast:
                    x.w[...] = x.wqkv[:, :, lanes]
                else:
                    for j in range(3):
                        window(j, k).wait_recv()
                        for h in range(2):
                            @pl.when(f == h)
                            def _():
                                x.w[j, h * 96:h * 96 + 96, :] = (x.wq, x.wk, x.wv)[j][:, lanes]
                                x.w[j, 96 - h * 96:192 - h * 96, :] = x.qrem[j, :, OFF[k]:OFF[k] + GW]
                x.bias[0:2, :] = x.vec[6:8, lanes]
        build_weights(x.w, x.bias, x.wa, x.wat)
        def first(i, carry):
            arrived(x.tsend, x.xt, x.trs, 2 * i)
            arrived(x.tsend, x.xt, x.trs, 2 * i + 1)
            prep_block(i, x.xt, x.wa, x.wat, x.qt, x.ka, x.vt, x.kt, x.va)
            return carry
        lax.fori_loop(0, sb, first, 0)

    def forward_step(q, carry):
        @pl.when(mine)
        def _():
            forward_tiles(q, half, x.qt, x.ka, x.vt, x.acc)
            for b, i in enumerate(rows_at(q, half)):
                for h in range(3):
                    a = x.acc[h, b]
                    v = a[0:64] / a[64:65]
                    x.cf[i, h * 64:h * 64 + 64, :] = v
                    x.lsum[i, h:h + 1, :] = a[64:65]
                    vb = v.astype(BF)
                    x.csend[2 * i, h * 64:h * 64 + 64, :] = vb[:, 0:128]
                    x.csend[2 * i + 1, h * 64:h * 64 + 64, :] = vb[:, 128:256]
                give(x.csend, x.crecv, x.css, x.crs, 2 * i, True)
                give(x.csend, x.crecv, x.css, x.crs, 2 * i + 1, True)
        if fast:
            for j in range(3):
                @pl.when(q == j)
                def _():
                    pass_on(j)
        return carry
    lax.fori_loop(0, half, forward_step, 0)
    @pl.when(mine)
    def _():
        x.dk[...] = jnp.zeros_like(x.dk)
        x.dv[...] = jnp.zeros_like(x.dv)

    if fast:
        for cp in fetch:
            cp.wait()
        for j in range(3):
            relay(j).wait_recv()
        chains = {k: Chain(o, f, c, [getattr(x, k + s) for s in ("b", "1", "2", "3", "4", "o", "ss", "rs")]) for k, o in ORDER.items()}
    def slot(s):
        for k, at in SCHEDULE.items():
            for i in range(7):
                if fast and at[i] == s:
                    chains[k].step(i + 1)
    pad_weights(x.wint, x.wffo, x.wip, x.wfp)
    taken(x.csend, x.crecv, x.crs)
    def send_dct():
        spread(x.dsend, x.dc, x.dss, x.drs, True)
    dense_body(MICRO * 128, x, send_dct, chains if fast else None, slot)

    if fast:
        slot(1)
    else:
        x.gw[...] = jnp.zeros_like(x.gw)
        x.gb[...] = jnp.zeros_like(x.gb)

    def backward_step(q, carry):
        @pl.when(mine)
        def _():
            for b, i in enumerate(rows_at(q, half)):
                arrived(x.dsend, x.dc, x.drs, 2 * i)
                arrived(x.dsend, x.dc, x.drs, 2 * i + 1)
                d = jnp.concatenate([x.dc[2 * i], x.dc[2 * i + 1]], axis=1).astype(F32)
                for h in range(3):
                    dh = d[h * 64:h * 64 + 64]
                    inv = 1.0 / x.lsum[i, h:h + 1, :]
                    delta = jnp.sum(dh * x.cf[i, h * 64:h * 64 + 64, :], axis=0, keepdims=True) * inv
                    dnt[h, i] = jnp.concatenate([dh * inv, jnp.where(iota((16, 256), 0) == 0, -delta, 0.0)], axis=0).astype(BF)
            backward_tiles(q, half, x.qt, x.ka, x.kt, x.va, dnt, x.dq, x.dk, x.dv)
            for b, i in enumerate(rows_at(q, half)):
                for h in range(3):
                    x.dqt[i, h * 64:h * 64 + 64, :] = (x.dq[h, b] * 0.125).astype(BF)
        if fast:
            for k in range(4):
                @pl.when(q == k)
                def _():
                    slot(2 * k + 3)
        return carry
    lax.fori_loop(0, half, backward_step, 0)

    xsend = x.csend
    def grads_at(i):
        k = jnp.concatenate([x.dk[h, i] for h in range(3)], axis=0).astype(BF)
        v = jnp.concatenate([x.dv[h, i] for h in range(3)], axis=0).astype(BF)
        return x.dqt[i], k, v
    @pl.when(mine)
    def _():
        for t in range(n):
            give(x.csend, x.crecv, x.css, x.crs, t, False)
        x.gacc[...] = jnp.zeros_like(x.gacc)
        x.gbacc[...] = jnp.zeros_like(x.gbacc)
        ones = jnp.ones((8, 256), BF)
        def weigh(i, carry):
            xb = jnp.concatenate([x.xt[2 * i, 0:GW, :], x.xt[2 * i + 1, 0:GW, :]], axis=1)
            q, k, v = grads_at(i)
            x.gacc[0] += mm(xb, q, NT)
            x.gacc[1] += mm(xb, k, NT)
            x.gacc[2] += mm(xb, v, NT)
            x.gbacc[0] += mm(ones, q, NT)
            x.gbacc[1] += mm(ones, v, NT)
            return carry
        lax.fori_loop(0, sb, weigh, 0)
        if fast:
            low = iota((96, 64), 0)
            bb = jnp.zeros((96, 64), F32)
            for k in range(2):
                for i in range(3):
                    bb = jnp.where(low == 3 * k + i, x.gbacc[k, 0:1, i * 64:i * 64 + 64], bb)
            for h in range(2):
                cat = jnp.concatenate([x.gacc[k, h * 96:h * 96 + 96, :] for k in range(3)] + [bb], axis=1).astype(BF)
                for s in range(5):
                    x.qs[h, s * 96:s * 96 + 96, :] = cat[:, s * 128:s * 128 + 128]
        else:
            for k in range(4):
                @pl.when(g == k)
                def _():
                    x.gw[:, :, k * GW:k * GW + GW] = x.gacc[...].astype(BF)
                    x.gb[0:1, k * GW:k * GW + GW] = x.gbacc[0, 0:1]
                    x.gb[1:2, k * GW:k * GW + GW] = x.gbacc[1, 0:1]

    if fast:
        def to_sum(h, t):
            return remote_copy(x.qs.at[h, pl.ds(t * 160, 160)], x.qr.at[f * 3 + m], x.qss.at[h * 3 + t], x.qrs.at[f * 3 + m], h, place_at(g, t))
        def stay():
            return pltpu.make_async_copy(x.qs.at[f, pl.ds(m * 160, 160)], x.qr.at[f * 3 + m], x.qrs.at[f * 3 + m])
        def place_at(g, t):
            return g * 4 + t + lax.rem(g, 2)
        def to_all(d):
            return remote_copy(x.qb.at[u], x.qb.at[u], x.qbs.at[d], x.qbr.at[u], f, lax.rem(c + 2 * d, n))
        def hand_over(k):
            return remote_copy(x.qb.at[k], x.qb.at[k], x.qbx.at[k], x.qbr.at[k], f, sib)
        def elsewhere(h, t):
            return (f != h) | (m != t)
        @pl.when(mine)
        def _():
            for h in range(2):
                for t in range(3):
                    @pl.when(elsewhere(h, t))
                    def _():
                        to_sum(h, t).start()
            stay().start()
    @pl.when(mine)
    def _():
        def post(i, carry):
            q, k, v = grads_at(i)
            x2 = (mm(x.w[0], q) + mm(x.w[1], k) + mm(x.w[2], v)).astype(BF)
            xsend[2 * i] = x2[:, 0:128]
            xsend[2 * i + 1] = x2[:, 128:256]
            give(xsend, x.xrecv, x.xss, x.xrs, 2 * i, True)
            give(xsend, x.xrecv, x.xss, x.xrs, 2 * i + 1, True)
            return carry
        lax.fori_loop(0, sb, post, 0)
    if fast:
        slot(10)
        @pl.when(mine)
        def _():
            for h in range(2):
                for t in range(3):
                    @pl.when(elsewhere(h, t))
                    def _():
                        remote_copy(x.qs.at[0, pl.ds(0, 160)], x.qr.at[h * 3 + t], x.ls, x.qrs.at[h * 3 + t], h, place_at(g, t)).wait_recv()
            stay().wait()
            x.qb[u] = sum(x.qr[k].astype(F32) for k in range(6)).astype(BF)
            for d in range(1, n // 2):
                to_all(d).start()
        slot(11)
        for k in range(12):
            @pl.when((r == own[k] % 2) & (c != own[k]))
            def _():
                remote_copy(x.qb.at[k], x.qb.at[k], x.ls, x.qbr.at[k], f, own[k]).wait_recv()
            @pl.when(r == own[k] % 2)
            def _():
                hand_over(k).start()

    taken(xsend, x.xrecv, x.xrs)
    if fast:
        for k in range(12):
            @pl.when(r != own[k] % 2)
            def _():
                hand_over(k).wait_recv()
        for s in range(12, 16):
            slot(s)
        for k in "ABC":
            chains[k].sent()
        vectors().wait_send()
        for j in range(3):
            half_over(j).wait_send()
            relay(j).wait_send()
        @pl.when(mine)
        def _():
            for j in range(3):
                window(j, 0).wait_send()
            for h in range(2):
                for t in range(3):
                    @pl.when(elsewhere(h, t))
                    def _():
                        to_sum(h, t).wait_send()
            for d in range(1, n // 2):
                to_all(d).wait_send()
        for k in range(12):
            @pl.when(r == own[k] % 2)
            def _():
                hand_over(k).wait_send()
    else:
        for k in range(MICRO):
            t = jnp.concatenate([x.xrecv[k * 4 + j] for j in range(4)], axis=0).astype(F32)
            s = slice(k * 128, k * 128 + 128)
            x.grad[s, :] = (jnp.transpose(t) + x.d1[s, :]).astype(BF)
    spread(x.tsend, x.xt, x.tss, x.trs, False)
    spread(x.dsend, x.dc, x.dss, x.drs, False)
    @pl.when(mine)
    def _():
        for t in range(n):
            give(xsend, x.xrecv, x.xss, x.xrs, t, False)


DMA = pltpu.SemaphoreType.DMA
S, V = jax.ShapeDtypeStruct, pltpu.VMEM


def common_scratch(n):
    rows, sb = MICRO * 128, n // 2
    return dict(
        tsend=V((12, CH, 128), BF), xt=V((n, CH, 128), BF), csend=V((n, GW, 128), BF), crecv=V((12, GW, 128), BF),
        dsend=V((12, GW, 128), BF), dc=V((n, GW, 128), BF),
        w=V((3, GW, GW), BF), bias=V((8, GW), F32), wa=V((3, XA, 384), BF), wat=V((3, 384, XA), BF),
        qt=V((3, sb, 128, 256), BF), ka=V((3, sb, 256, 128), BF), vt=V((3, sb, 80, 256), BF), kt=V((3, sb, 64, 256), BF), va=V((3, sb, 256, 128), BF),
        cf=V((sb, GW, 256), F32), lsum=V((sb, 8, 256), F32), acc=V((3, 2, 80, 256), F32), dq=V((3, 2, 64, 256), F32),
        dk=V((3, sb, 64, 256), F32), dv=V((3, sb, 64, 256), F32), dqt=V((sb, GW, 256), BF), gacc=V((3, GW, GW), F32), gbacc=V((2, 8, GW), F32),
        ctx=V((rows, D), BF), xh=V((rows, D), F32), n1b=V((rows, D), BF), wip=V((4, 256, D), BF), wfp=V((4, D, 256), BF), dpre=V((4, rows, D), BF),
        hid=V((4, rows, D), BF), br=V((rows, D), F32), dn=V((rows, D), F32), db=V((rows, D), BF), st=V((rows, 128), F32),
        tss=DMA((12,)), trs=DMA((n,)), css=DMA((n,)), crs=DMA((12,)), dss=DMA((12,)), drs=DMA((n,)), xss=DMA((n,)), xrs=DMA((12,)), ls=DMA)


class Refs:
    def __init__(self, **k):
        self.__dict__.update(k)


def call(n, fast, ins, outs, scratch, far):
    names, onames = list(ins), list(outs)
    def kernel(*a):
        refs = dict(zip(names, a[:len(names)]))
        refs.update(zip(onames, a[len(names):len(names) + len(onames)]))
        refs.update(a[-1])
        mega(n, fast, Refs(**refs))
    vm = pl.BlockSpec(memory_space=pltpu.VMEM)
    got = pl.pallas_call(
        kernel, out_shape=tuple(outs.values()),
        in_specs=[pl.BlockSpec(memory_space=pl.ANY) if k in far else vm for k in names], out_specs=(vm,) * len(onames),
        scratch_shapes=[scratch],
        compiler_params=pltpu.CompilerParams(collective_id=0, has_side_effects=True, vmem_limit_bytes=60 * 2**20))(*ins.values())
    return dict(zip(onames, got))


def run_whole(n, ins):
    rows = MICRO * 128
    outs = dict(out=S((rows, D), BF), grad=S((rows, D), BF), gw=S((3, GW, D), BF), gb=S((8, D), F32), ga=S((D, D), BF), gi=S((192, FF), BF),
                gf=S((D, D), BF), gv=S((16, D), F32))
    scratch = common_scratch(n)
    scratch.update(xrecv=V((12, GW, 128), BF), d1=V((rows, D), F32))
    return call(n, False, ins, outs, scratch, ())


def run_fast(n, ins):
    rows = MICRO * 128
    outs = dict(out=S((rows, D), BF), xrecv=S((12, GW, 128), BF), d1=S((rows, D), F32), qb=S((12, 160, 128), BF))
    for k in "ABC":
        outs[k + "o"] = S((2, 2, 4, LEN[k], 128), BF)
    scratch = common_scratch(n)
    scratch.update(cot=V((rows, D), BF), wout=V((D, D), BF), wint=V((192, FF), BF), wffo=V((D, D), BF), vec=V((16, D), F32), vbuf=V((2, 16, 384), BF),
                   qrem=V((3, 96, 256), BF), gv=V((16, D), F32), qs=V((2, 480, 128), BF), qr=V((6, 160, 128), BF),
                   lsem=DMA((4,)), wss=DMA((10,)), wrs=DMA((10,)), qss=DMA((6,)), qrs=DMA((6,)), qbs=DMA((n,)), qbr=DMA((12,)), qbx=DMA((12,)))
    for k in "ABC":
        l = LEN[k]
        scratch[k + "b"] = V((2, 2, 2, 4, l, 128), BF)
        scratch[k + "1"] = V((2, 2, 4, l, 128), BF)
        scratch[k + "2"] = V((2, l, 128) if ORDER[k] == "zyx" else (2, 4, l, 128), BF)
        scratch[k + "3"] = V((l, 128) if ORDER[k] == "zyx" else (4, l, 128), BF)
        scratch[k + "4"] = V((4, 2, 2, l, 128) if ORDER[k] == "zyx" else (4, l, 128), BF)
        scratch[k + "ss"] = DMA((11,))
        scratch[k + "rs"] = DMA((11,))
    return call(n, True, ins, outs, scratch, ("wo", "wi", "wf", "cot_in"))


def finish(out, xrecv, d1, qb, a, b, c, o_out, o_grad, o_q, o_k, o_v, o_qb, o_vb, o_w, o_b, o_g1, o_s1, o_i, o_ib, o_f, o_fb, o_g2, o_s2):
    f = lax.axis_index("fsdp")
    o_out[...] = out[...]
    for k in range(MICRO):
        t = jnp.concatenate([xrecv[k * 4 + j] for j in range(4)], axis=0).astype(F32)
        s = slice(k * 128, k * 128 + 128)
        o_grad[s, :] = (jnp.transpose(t) + d1[s, :]).astype(BF)
    def slab(ref, base, rows):
        got = [ref[b // 8, (b // 4) % 2, b % 4, w:w + size, :] for b, w, _, size in pieces(base, rows)]
        return jnp.concatenate(got, axis=0).astype(F32) if len(got) > 1 else got[0].astype(F32)
    for s in range(6):
        o_w[:, s * 128:s * 128 + 128] = slab(a, s * 384, 384)
    for s in range(24):
        o_i[:, s * 128:s * 128 + 128] = slab(b, s * 96, 96)
    for s in range(3):
        o_f[s * 128:s * 128 + 128, :] = jnp.transpose(slab(c, s * 768, 768))
    cats, qbs, vbs = [], [], []
    for g in range(4):
        rows = jnp.concatenate([qb[t * 4 + g] for t in range(3)], axis=0).astype(F32)
        cat = jnp.concatenate([rows[s * 96:s * 96 + 96] for s in range(5)], axis=1)
        cats.append(cat)
        qbs.append(jnp.concatenate([cat[i:i + 1, 576:640] for i in range(3)], axis=1))
        vbs.append(jnp.concatenate([cat[3 + i:4 + i, 576:640] for i in range(3)], axis=1))
    for k, o in enumerate((o_q, o_k, o_v)):
        o[...] = jnp.concatenate([cat[:, k * GW:k * GW + GW] for cat in cats], axis=1)
    pick = lambda v: jnp.where(f == 0, jnp.concatenate(v[0:2], axis=1), jnp.concatenate(v[2:4], axis=1))
    o_qb[...] = pick(qbs).reshape(384)
    o_vb[...] = pick(vbs).reshape(384)
    rows = []
    for k in range(30):
        b = k // 2
        rows.append(a[b // 8, (b // 4) % 2, b % 4, 144:160, :].astype(F32)[k % 2:k % 2 + 1, :])
    for i, o in enumerate((o_b, o_g1, o_s1, o_fb, o_g2, o_s2)):
        o[...] = jnp.concatenate(rows[3 * i:3 * i + 3], axis=1).reshape(384)
    o_ib[...] = jnp.concatenate(rows[18:30], axis=1).reshape(1536)


def local(tokens, cotangent, segment_ids, q_weight, key_weight, value_weight, q_bias, value_bias, out_weight, out_bias,
          norm1_gain, norm1_bias, inter_weight, inter_bias, ffo_weight, ffo_bias, norm2_gain, norm2_bias):
    n, nf = lax.axis_size("ctx"), lax.axis_size("fsdp")
    rows = MICRO * 128
    tok, cot, seg = tokens.reshape(rows, D), cotangent.reshape(rows, D), segment_ids
    dl = q_bias.shape[0]
    if n == 16 and nf == 2:
        x = run_fast(n, dict(tok=tok, seg=seg, cot_in=cot, wq=q_weight, wk=key_weight, wv=value_weight, wo=out_weight, wi=inter_weight, wf=ffo_weight,
                             out_bias=out_bias, norm1_gain=norm1_gain, norm1_bias=norm1_bias, ffo_bias=ffo_bias, norm2_gain=norm2_gain,
                             norm2_bias=norm2_bias, q_bias=q_bias, value_bias=value_bias, inter_bias=inter_bias))
        vm = pl.BlockSpec(memory_space=pltpu.VMEM)
        row = S((dl,), F32)
        outs = (S((rows, D), BF), S((rows, D), BF)) + (S((96, D), F32),) * 3 + (row, row, S((384, D), F32), row, row, row, S((96, FF), F32), S((4 * dl,), F32),
                S((384, D), F32), row, row, row)
        got = pl.pallas_call(
            finish, out_shape=outs, in_specs=[vm] * 7, out_specs=(vm,) * 17,
            compiler_params=pltpu.CompilerParams(vmem_limit_bytes=60 * 2**20))(x["out"], x["xrecv"], x["d1"], x["qb"], x["Ao"], x["Bo"], x["Co"])
        return (got[0].reshape(tokens.shape), got[1].reshape(tokens.shape)) + tuple(got[2:])
    gather = lambda a, ax: lax.all_gather(a, "fsdp", axis=ax, tiled=True)
    pack = jnp.concatenate([out_bias, norm1_gain, norm1_bias, ffo_bias, norm2_gain, norm2_bias, q_bias, value_bias, inter_bias]).reshape(12, dl)
    wqkv = gather(jnp.stack([q_weight, key_weight, value_weight]), 1)
    allv = lax.all_gather(pack, "fsdp", axis=0)
    vec = jnp.concatenate([jnp.swapaxes(allv[:, 0:8], 0, 1).reshape(8, D), allv[:, 8:12].reshape(4, D), jnp.zeros((4, D), BF)], axis=0).astype(F32)
    x = run_whole(n, dict(tok=tok, seg=seg, cot=cot, wqkv=wqkv, wout=gather(out_weight, 0), wint=gather(inter_weight, 0), wffo=gather(ffo_weight, 0), vec=vec))
    gw, gv = x["gw"], x["gv"]
    scatter = lambda a: lax.psum(lax.psum_scatter(a, "fsdp", scatter_dimension=0, tiled=True), "ctx").astype(F32)
    gvec = lax.psum(jnp.concatenate([gv, x["gb"]], axis=0), ("fsdp", "ctx"))
    me = lax.axis_index("fsdp")
    part = lambda i: lax.dynamic_slice(gvec[i], (me * dl,), (dl,))
    gib = lax.dynamic_slice(gvec[8:12].reshape(4 * D), (me * 4 * dl,), (4 * dl,))
    return (x["out"].reshape(tokens.shape), x["grad"].reshape(tokens.shape), scatter(gw[0]), scatter(gw[1]), scatter(gw[2]), part(16), part(17),
            scatter(x["ga"]), part(0), part(1), part(2), scatter(x["gi"]), gib, scatter(x["gf"].T), part(3), part(4), part(5))


def solution(mesh):
    act, seg, mat, vec = P(None, "fsdp", "ctx", None), P(None, "fsdp", "ctx"), P("fsdp", None), P("fsdp")
    return jax.shard_map(
        local, mesh=mesh,
        in_specs=(act, act, seg, mat, mat, mat, vec, vec, mat, vec, vec, vec, mat, vec, mat, vec, vec, vec),
        out_specs=(act, act, mat, mat, mat, vec, vec, mat, vec, vec, vec, mat, vec, mat, vec, vec, vec),
        check_vma=False)
```

```python
import math

import jax
import jax.numpy as jnp
from jax import lax
from jax.experimental import pallas as pl
from jax.experimental.pallas import tpu as pltpu
from jax.sharding import PartitionSpec as P

MESH = pl.DeviceIdType.MESH
MICRO = 3


def place(n, g, m):
    return g * (n // 4) + m + (g % 2)


def owners(n):
    return [place(n, g, m) for m in range(MICRO) for g in range(4)]


def unit_of(c, n):
    g = c // (n // 4)
    m = c - g * (n // 4) - lax.rem(g, 2)
    return g, m, (m >= 0) & (m < MICRO)


BF, F32 = jnp.bfloat16, jnp.float32
HEAD, GW = 64, 192
CH = 208
XA = 240
BIG = 1e9
NN = (((1,), (0,)), ((), ()))
NT = (((1,), (1,)), ((), ()))
TN = (((0,), (0,)), ((), ()))

def mm(a, b, dims=NN):
    return lax.dot_general(a, b, dims, preferred_element_type=F32)

def iota(shape, axis):
    return lax.broadcasted_iota(jnp.int32, shape, axis)

def build_weights(w_ref, b_ref, wa_ref, wat_ref):
    for s in range(3):
        for h in range(3):
            w = w_ref[s, :, h * 64:h * 64 + 64].astype(F32)
            top = jnp.concatenate([w * (0.125 if s == 0 else 1.0), jnp.zeros((GW, 64), F32)], axis=1)
            r, c = iota((48, 128), 0), iota((48, 128), 1)
            same = (c - 64 == r)
            lanes = (c >= 64) & (c < 96) & (r < 32)
            one = (r == 32)
            zero = jnp.zeros((48, 128), F32)
            if s == 0:
                bias = jnp.concatenate([b_ref[0:1, h * 64:h * 64 + 64].astype(F32) * 0.125, jnp.zeros((1, 64), F32)], axis=1)
                low = jnp.where(lanes & same, 1.0, zero) + jnp.where(one, bias, zero)
            elif s == 1:
                low = jnp.where(lanes & ~same, -BIG, zero) + jnp.where(one & (c == 96), 1.0, zero)
            else:
                bias = jnp.concatenate([b_ref[1:2, h * 64:h * 64 + 64].astype(F32), jnp.zeros((1, 64), F32)], axis=1)
                low = jnp.where(one, bias, zero) + jnp.where(one & (c == 64), 1.0, zero)
            full = jnp.concatenate([top, low], axis=0)
            wa_ref[s, :, h * 128:h * 128 + 128] = full.astype(BF)
            wat_ref[s, h * 128:h * 128 + 128, :] = jnp.transpose(full).astype(BF)

D, FF = 768, 3072
EPS = 1e-12
WIN = (0, 128, 384, 512)
OFF = (0, 64, 0, 64)
RS2 = math.sqrt(0.5)
IPI = 1.0 / math.sqrt(2.0 * math.pi)
CK = 128

def rowmean(x):
    return jnp.sum(x, axis=-1, keepdims=True) * (1.0 / D)

def tall(ref, m):
    return jnp.concatenate([ref[m * 4 + g] for g in range(4)], axis=0)


def pad_weights(wint, wffo, wip, wfp):
    for j in range(4):
        o = OFF[j]
        wip[j] = jnp.zeros((256, D), BF)
        wip[j, o:o + 192, :] = wint[:, j * D:(j + 1) * D]
        lane = iota((D, 256), 1)
        w = wffo[:, WIN[j]:WIN[j] + 256]
        wfp[j] = jnp.where((lane >= o) & (lane < o + 192), w.astype(F32), 0.0).astype(BF)


def dense_body(rows, x, send, chains, slot):
    tok, cot, ctxt, wout, out, d1, dct, gv = x.tok, x.cot, x.crecv, x.wout, x.out, x.d1, x.dsend, x.gv
    ctx, attn, n1b, wip, wfp, dpre, hid, br, dn, db, st = x.ctx, x.xh, x.n1b, x.wip, x.wfp, x.dpre, x.hid, x.br, x.dn, x.db, x.st
    da = ctx
    nm = rows // 128
    v = lambda i: x.vec[i:i + 1, :]
    for m in range(nm):
        ctx[m * 128:(m + 1) * 128, :] = jnp.transpose(tall(ctxt, m))
    attn[...] = mm(ctx[...], wout[...])
    def ln1(t, c):
        s = pl.ds(pl.multiple_of(t * CK, CK), CK)
        r = attn[s, :] + v(0) + tok[s, :].astype(F32)
        cen = r - rowmean(r)
        rstd = lax.rsqrt(rowmean(cen * cen) + EPS)
        xh = cen * rstd
        attn[s, :] = xh
        st[s, :] = jnp.broadcast_to(rstd, (CK, 128))
        n = xh * v(1) + v(2)
        n1b[s, :] = n.astype(BF)
        br[s, :] = n + v(3)
        return c
    lax.fori_loop(0, rows // CK, ln1, 0)
    for j in range(4):
        for m in range(nm):
            s = slice(m * 128, (m + 1) * 128)
            u = mm(n1b[s, WIN[j]:WIN[j] + 256], wip[j]) + v(8 + j)
            half = 0.5 + 0.5 * lax.erf(u * RS2)
            hid[j, s, :] = (u * half).astype(BF)
            dpre[j, s, :] = (half + u * (jnp.exp(u * u * -0.5) * IPI)).astype(BF)
        br[:, WIN[j]:WIN[j] + 256] += mm(hid[j], wfp[j])
    gv[...] = jnp.zeros_like(gv)
    def ln2(t, c):
        s = pl.ds(pl.multiple_of(t * CK, CK), CK)
        r = br[s, :]
        cen = r - rowmean(r)
        rstd = lax.rsqrt(rowmean(cen * cen) + EPS)
        xh = cen * rstd
        out[s, :] = (xh * v(4) + v(5)).astype(BF)
        ct = cot[s, :].astype(F32)
        u = ct * v(4)
        dd = rstd * (u - rowmean(u) - xh * rowmean(u * xh))
        dn[s, :] = dd
        ddb = dd.astype(BF)
        db[s, :] = ddb
        gv[4:5, :] += jnp.sum(ct * xh, axis=0, keepdims=True)
        gv[5:6, :] += jnp.sum(ct, axis=0, keepdims=True)
        gv[3:4, :] += jnp.sum(ddb.astype(F32), axis=0, keepdims=True)
        return c
    lax.fori_loop(0, rows // CK, ln2, 0)
    dbt = jnp.transpose(db[...])
    for j in range(4):
        o = WIN[j] + OFF[j]
        val = mm(dbt[o:o + 192, :], hid[j])
        if chains is None:
            x.gf[j * 192:(j + 1) * 192, :] = val.astype(BF)
            continue
        for f in range(2):
            for s in range(3):
                at = f * 384 + s * 128
                put(x.Cb, f, s * 768 + j * 192, val[:, at:at + 128])
    if chains is not None:
        chains["C"].step(0)
    for j in range(4):
        for m in range(nm):
            s = slice(m * 128, (m + 1) * 128)
            dh = mm(db[s, WIN[j]:WIN[j] + 256], wfp[j], NT)
            dp = (dh * dpre[j, s, :].astype(F32)).astype(BF)
            dpre[j, s, :] = dp
            gv[8 + j:9 + j, :] += jnp.sum(dp.astype(F32), axis=0, keepdims=True)
        dn[:, WIN[j]:WIN[j] + 256] += mm(dpre[j], wip[j], NT)
    nt = jnp.transpose(n1b[...])
    for j in range(4):
        o = WIN[j] + OFF[j]
        val = mm(nt[o:o + 192, :], dpre[j])
        if chains is None:
            x.gi[:, j * D:(j + 1) * D] = val.astype(BF)
            continue
        for f in range(2):
            for s in range(6):
                put(x.Bb, f, (j * 6 + s) * 96, val[f * 96:f * 96 + 96, s * 128:s * 128 + 128])
    if chains is not None:
        chains["B"].step(0)
    slot(0)
    def lnb(t, c):
        s = pl.ds(pl.multiple_of(t * CK, CK), CK)
        g = dn[s, :]
        xh = attn[s, :]
        u = g * v(1)
        dd = st[s, 0:1] * (u - rowmean(u) - xh * rowmean(u * xh))
        d1[s, :] = dd
        ddb = dd.astype(BF)
        da[s, :] = ddb
        gv[1:2, :] += jnp.sum(g * xh, axis=0, keepdims=True)
        gv[2:3, :] += jnp.sum(g, axis=0, keepdims=True)
        gv[0:1, :] += jnp.sum(ddb.astype(F32), axis=0, keepdims=True)
        return c
    lax.fori_loop(0, rows // CK, lnb, 0)
    dc = mm(wout[...], da[...], NT).astype(BF)
    for m in range(nm):
        for g in range(4):
            dct[m * 4 + g] = dc[g * GW:g * GW + GW, m * 128:(m + 1) * 128]
    send()
    ct = jnp.concatenate([tall(ctxt, m) for m in range(nm)], axis=1)
    if chains is None:
        x.ga[...] = mm(ct, da[...]).astype(BF)
        return
    for s in range(3):
        val = mm(ct, da[:, s * 256:s * 256 + 256])
        for f in range(2):
            for k in range(2):
                put(x.Ab, f, (2 * s + k) * 384, val[f * 384:f * 384 + 384, k * 128:k * 128 + 128])
    low = iota((16, 128), 0)
    for f in range(2):
        for b in range(16):
            two = []
            for k in (2 * b, 2 * b + 1):
                if k < 18:
                    at = f * 384 + (k % 3) * 128
                    two.append(gv[k // 3:k // 3 + 1, at:at + 128])
                elif k < 30:
                    row, at = 8 + 2 * f + (k - 18) // 6, (k - 18) % 6 * 128
                    two.append(gv[row:row + 1, at:at + 128])
                else:
                    two.append(jnp.zeros((1, 128), F32))
            x.Ab[b // 8, f, (b // 4) % 2, b % 4, 144:160, :] = jnp.where(low == 0, two[0], jnp.where(low == 1, two[1], 0.0)).astype(BF)
    chains["A"].step(0)


def remote_copy(src, dst, ssem, rsem, f, c):
    return pltpu.make_async_remote_copy(src_ref=src, dst_ref=dst, send_sem=ssem, recv_sem=rsem, device_id=(f, c), device_id_type=MESH)


VECTORS = ("out_bias", "norm1_gain", "norm1_bias", "ffo_bias", "norm2_gain", "norm2_bias", "q_bias", "value_bias")
ORDER = {"A": "yxz", "B": "yxz", "C": "yxz"}
SCHEDULE = {"C": (0, 1, 3, 5, 7, 9, 10), "B": (1, 3, 5, 7, 9, 10, 11), "A": (1, 5, 7, 9, 10, 11, 12)}
LEN = {"A": 160, "B": 144, "C": 144}


def pieces(base, rows):
    out, at = [], 0
    while at < rows:
        b, w = divmod(base + at, 144)
        size = min(144 - w, rows - at)
        out.append((b, w, at, size))
        at += size
    return out


def put(ref, f, base, val):
    for b, w, at, size in pieces(base, val.shape[0]):
        ref[b // 8, f, (b // 4) % 2, b % 4, w:w + size, :] = val[at:at + size].astype(BF)


class Chain:
    def __init__(self, order, f, c, refs):
        self.order, self.f, self.c = order, f, c
        self.b, self.c1, self.c2, self.c3, self.c4, self.out, self.ss, self.rs = refs
        self.r, self.x, self.z = lax.rem(c, 2), lax.rem(lax.div(c, 2), 2), lax.div(c, 4)
        self.started = []

    def core(self):
        return self.f, self.c + 1 - 2 * self.r

    def along_x(self):
        return self.f, self.c + 2 - 4 * self.x

    def along_z(self, d):
        return self.f, lax.rem(self.c + 4 * d, 16)

    def copy(self, k, src, dst, to):
        return remote_copy(src, dst, self.ss.at[k], self.rs.at[k], *to)

    def moves(self, k):
        b, r, f, x, z, o = self.b, self.r, self.f, self.x, self.z, self.out
        zs = [(d, lax.rem(z + d, 4)) for d in (1, 2, 3)]
        y = (1 - f, self.c)
        if k == 0:
            return [(0, b.at[1 - r], self.c1, self.core())]
        if k == 6:
            return [(4, o.at[r], o.at[r], self.core())]
        if self.order == "yxz":
            return {1: [(1, b.at[r, 1 - f], self.c2, y)],
                    2: [(2, b.at[r, f, 1 - x], self.c3, self.along_x())],
                    3: [(4 + d, b.at[r, f, x, t], self.c4.at[z], self.along_z(d)) for d, t in zs],
                    4: [(7 + d, o.at[r, x, z], o.at[r, x, z], self.along_z(d)) for d, t in zs],
                    5: [(3, o.at[r, x], o.at[r, x], self.along_x())]}[k]
        return {1: [(4 + d, b.at[r, :, :, t], self.c4.at[z], self.along_z(d)) for d, t in zs],
                2: [(1, b.at[r, 1 - f, :, z], self.c2, y)],
                3: [(2, b.at[r, f, 1 - x, z], self.c3, self.along_x())],
                4: [(3, o.at[r, x, z], o.at[r, x, z], self.along_x())],
                5: [(7 + d, o.at[r, :, z], o.at[r, :, z], self.along_z(d)) for d, t in zs]}[k]

    def start(self, k):
        for mv in self.moves(k):
            self.copy(*mv).start()

    def received(self, k):
        for mv in self.moves(k):
            self.copy(*mv).wait_recv()

    def sent(self):
        for k in range(7):
            for mv in self.moves(k):
                self.copy(*mv).wait_send()

    def add(self, k):
        b, r, f, x, z, o = self.b, self.r, self.f, self.x, self.z, self.out
        up = lambda v: v.astype(F32)
        others = [lax.rem(z + 4 - d, 4) for d in (1, 2, 3)]
        if k == 0:
            def one(t, carry):
                i, j, l = t // 8, lax.rem(t // 4, 2), lax.rem(t, 4)
                b[r, i, j, l] = (up(b[r, i, j, l]) + up(self.c1[i, j, l])).astype(BF)
                return carry
            lax.fori_loop(0, 16, one, 0)
        elif self.order == "yxz" and k == 1:
            def one(t, carry):
                j, l = t // 4, lax.rem(t, 4)
                b[r, f, j, l] = (up(b[r, f, j, l]) + up(self.c2[j, l])).astype(BF)
                return carry
            lax.fori_loop(0, 8, one, 0)
        elif self.order == "yxz" and k == 2:
            for l in range(4):
                b[r, f, x, l] = (up(b[r, f, x, l]) + up(self.c3[l])).astype(BF)
        elif self.order == "yxz" and k == 3:
            o[r, x, z] = (up(b[r, f, x, z]) + sum(up(self.c4[t]) for t in others)).astype(BF)
        elif self.order == "zyx" and k == 1:
            for i in range(2):
                for j in range(2):
                    b[r, i, j, z] = (up(b[r, i, j, z]) + sum(up(self.c4[t, i, j]) for t in others)).astype(BF)
        elif self.order == "zyx" and k == 2:
            for j in range(2):
                b[r, f, j, z] = (up(b[r, f, j, z]) + up(self.c2[j])).astype(BF)
        elif self.order == "zyx" and k == 3:
            o[r, x, z] = (up(b[r, f, x, z]) + up(self.c3[...])).astype(BF)

    def step(self, k):
        if k > 0:
            self.received(k - 1)
            self.add(k - 1)
        if k < 7:
            self.start(k)


def tile_at(q, t, half):
    p, mir = lax.rem(q, half // 2), lax.div(q, half // 2)
    b = lax.div(t + half - 1 - p, 2 * half)
    i = p + b * (half - 1 - 2 * p)
    j = t - b * (half + 1 + p)
    last = 2 * half - 1
    return b, i + mir * (last - 2 * i), j + mir * (last - 2 * j)


def rows_at(q, half):
    p, mir = lax.rem(q, half // 2), lax.div(q, half // 2)
    last = 2 * half - 1
    return [i + mir * (last - 2 * i) for i in (p, half - 1 - p)]


def in_parts(half, part):
    count = 3 * half + 1
    if count <= 13:
        part(0, count)
    else:
        size = max(d for d in range(1, 9) if count % d == 0)
        lax.fori_loop(0, count // size, lambda t, carry: (part(t * size, size), carry)[1], 0)


def forward_tiles(q, half, qt, ka, vt, acc):
    acc[...] = jnp.zeros_like(acc)
    def part(first, count):
        items = [(h,) + tile_at(q, first + t, half) for t in range(count) for h in range(3)]
        def front(it):
            h, _, i, j = it
            return mm(ka[h, j], qt[h, i])
        ready = [front(it) for it in items[:3]]
        for t, (h, b, i, j) in enumerate(items):
            if t + 3 < len(items):
                ready.append(front(items[t + 3]))
            e = jnp.exp(ready[t]).astype(BF)
            ready[t] = None
            acc[h, b] += mm(vt[h, j], e)
    in_parts(half, part)


def backward_tiles(q, half, qt, ka, kt, va, dnt, dq, dk, dv):
    dq[...] = jnp.zeros_like(dq)
    def part(first, count):
        items = [(h,) + tile_at(q, first + t, half) for t in range(count) for h in range(3)]
        def front(it):
            h, _, i, j = it
            return mm(ka[h, j], qt[h, i]), mm(va[h, j, :, 0:80], dnt[h, i])
        ready = [front(it) for it in items[:2]]
        for t, (h, b, i, j) in enumerate(items):
            if t + 2 < len(items):
                ready.append(front(items[t + 2]))
            s, dp = ready[t]
            ready[t] = None
            e = jnp.exp(s)
            eb = e.astype(BF)
            ds = (e * dp).astype(BF)
            dq[h, b] += mm(kt[h, j], ds)
            dk[h, j] += mm(qt[h, i, 0:64], ds, NT)
            dv[h, j] += mm(dnt[h, i, 0:64], eb, NT)
    in_parts(half, part)


def prep_block(i, xt, wa, wat, qt, ka, vt, kt, va):
    x = jnp.concatenate([xt[2 * i], xt[2 * i + 1]], axis=1)
    seg = x[GW:GW + 16].astype(F32)[0:1].astype(jnp.int32)
    r = iota((48, 256), 0)
    aug = jnp.where((r == seg) & (r < 32) | (r == 32), 1.0, 0.0).astype(BF)
    xa = jnp.concatenate([x[0:GW], aug], axis=0)
    xn = jnp.transpose(xa)
    q = mm(wat[0], xa).astype(BF)
    k = mm(wat[1], xa).astype(BF)
    v = mm(wat[2], xa).astype(BF)
    kn = mm(xn, wa[1]).astype(BF)
    vn = mm(xn, wa[2]).astype(BF)
    for h in range(3):
        o = h * 128
        qt[h, i] = q[o:o + 128]
        anchor = jnp.sum(q[o:o + 64].astype(F32) * k[o:o + 64].astype(F32), axis=0, keepdims=True)
        qt[h, i, 96:112] = jnp.where(iota((16, 256), 0) == 0, -anchor, 0.0).astype(BF)
        ka[h, i] = kn[:, o:o + 128]
        vt[h, i] = v[o:o + 80]
        kt[h, i] = k[o:o + 64]
        va[h, i] = vn[:, o:o + 128]


def mega(n, fast, x):
    f, c = lax.axis_index("fsdp"), lax.axis_index("ctx")
    g, m, mine = unit_of(c, n)
    u = m * 4 + g
    own = owners(n)
    sb, half = n // 2, n // 4
    r = lax.rem(c, 2)
    tok, dnt = x.tok, x.vt
    bar = pltpu.get_barrier_semaphore()
    for d in range(1, n):
        pl.semaphore_signal(bar, inc=1, device_id=(f, lax.rem(c + d, n)), device_id_type=MESH)
    greeted = n - 1
    if fast:
        for p in range(4):
            pl.semaphore_signal(bar, inc=1, device_id=(1 - f, g * 4 + p), device_id_type=MESH)
        greeted += 4
        fetch = [pltpu.make_async_copy(x.wo, x.wout.at[pl.ds(f * 384, 384)], x.lsem.at[0]),
                 pltpu.make_async_copy(x.wi, x.wint.at[pl.ds(f * 96, 96)], x.lsem.at[1]),
                 pltpu.make_async_copy(x.wf, x.wffo.at[pl.ds(f * 384, 384)], x.lsem.at[2]),
                 pltpu.make_async_copy(x.cot_in, x.cot, x.lsem.at[3])]
        for cp in fetch:
            cp.start()
    for k in range(MICRO):
        t = jnp.transpose(tok[k * 128:k * 128 + 128, :])
        sg = jnp.broadcast_to(x.seg[k].astype(F32), (16, 128)).astype(BF)
        for j in range(4):
            x.tsend[k * 4 + j, 0:GW, :] = t[j * GW:j * GW + GW]
            x.tsend[k * 4 + j, GW:CH, :] = sg
    if fast:
        own_rows = [getattr(x, k)[...].astype(F32).reshape(1, 384) for k in VECTORS]
        inter = x.inter_bias[...].astype(F32).reshape(1, 1536)
        own_rows += [inter[:, k * 384:k * 384 + 384] for k in range(4)]
        x.vbuf[f] = jnp.concatenate(own_rows + [jnp.zeros((4, 384), F32)], axis=0).astype(BF)
    pl.semaphore_wait(bar, greeted)

    def spread(src, dst, ss, rs, start):
        for k in range(12):
            @pl.when(c != own[k])
            def _():
                cp = remote_copy(src.at[k], dst.at[c], ss.at[k], rs.at[c], f, own[k])
                cp.start() if start else cp.wait_send()
            if start:
                @pl.when(c == own[k])
                def _():
                    pltpu.make_async_copy(src.at[k], dst.at[c], rs.at[c]).start()
    def arrived(src, dst, rs, s):
        @pl.when(c != s)
        def _():
            remote_copy(src.at[0], dst.at[s], x.ls, rs.at[s], f, s).wait_recv()
        @pl.when(c == s)
        def _():
            pltpu.make_async_copy(src.at[0], dst.at[s], rs.at[s]).wait()
    def give(src, dst, ss, rs, t, start):
        @pl.when(c != t)
        def _():
            cp = remote_copy(src.at[t], dst.at[u], ss.at[t], rs.at[u], f, t)
            cp.start() if start else cp.wait_send()
        if start:
            @pl.when(c == t)
            def _():
                pltpu.make_async_copy(src.at[t], dst.at[u], rs.at[u]).start()
    def taken(src, dst, rs):
        for k in range(12):
            @pl.when(c != own[k])
            def _():
                remote_copy(src.at[0], dst.at[k], x.ls, rs.at[k], f, own[k]).wait_recv()
            @pl.when(c == own[k])
            def _():
                pltpu.make_async_copy(src.at[0], dst.at[k], rs.at[k]).wait()

    if fast:
        sib = c + 1 - 2 * r
        parts = ((x.wo, x.wout, 384), (x.wi, x.wint, 96), (x.wf, x.wffo, 384))
        def window(j, k):
            return remote_copy((x.wq, x.wk, x.wv)[j].at[:, WIN[k]:WIN[k] + 256], x.qrem.at[j], x.wss.at[6 + j], x.wrs.at[6 + j], 1 - f, c)
        def vectors():
            return remote_copy(x.vbuf.at[f], x.vbuf.at[f], x.wss.at[9], x.wrs.at[9], 1 - f, c)
        def half_over(j):
            src, dst, rows = parts[j]
            h = rows // 2
            return remote_copy(src.at[pl.ds(r * h, h)], dst.at[pl.ds(f * rows + r * h, h)], x.wss.at[j], x.wrs.at[j], 1 - f, c)
        def relay(j, back=False):
            _, dst, rows = parts[j]
            h = rows // 2
            at = pl.ds((1 - f) * rows + r * h, h)
            return remote_copy(dst.at[at], dst.at[at], x.wss.at[3 + j], x.wrs.at[3 + j], f, sib)
        @pl.when(mine)
        def _():
            for k in range(4):
                @pl.when(g == k)
                def _():
                    for j in range(3):
                        window(j, k).start()
        vectors().start()
    spread(x.tsend, x.xt, x.tss, x.trs, True)
    if fast:
        for j in range(3):
            half_over(j).start()
        def pass_on(j):
            half_over(j).wait_recv()
            relay(j).start()

    if fast:
        vectors().wait_recv()
        for k in range(2):
            for j in range(8):
                x.vec[j:j + 1, k * 384:k * 384 + 384] = x.vbuf[k, 0:16, :].astype(F32)[j:j + 1, :]
            for j in range(4):
                row, at = 8 + 2 * k + j // 2, (j % 2) * 384
                x.vec[row:row + 1, at:at + 384] = x.vbuf[k, 0:16, :].astype(F32)[8 + j:9 + j, :]

    @pl.when(mine)
    def _():
        for k in range(4):
            @pl.when(g == k)
            def _():
                lanes = slice(k * GW, k * GW + GW)
                if not fast:
                    x.w[...] = x.wqkv[:, :, lanes]
                else:
                    for j in range(3):
                        window(j, k).wait_recv()
                        for h in range(2):
                            @pl.when(f == h)
                            def _():
                                x.w[j, h * 96:h * 96 + 96, :] = (x.wq, x.wk, x.wv)[j][:, lanes]
                                x.w[j, 96 - h * 96:192 - h * 96, :] = x.qrem[j, :, OFF[k]:OFF[k] + GW]
                x.bias[0:2, :] = x.vec[6:8, lanes]
        build_weights(x.w, x.bias, x.wa, x.wat)
        def first(i, carry):
            arrived(x.tsend, x.xt, x.trs, 2 * i)
            arrived(x.tsend, x.xt, x.trs, 2 * i + 1)
            prep_block(i, x.xt, x.wa, x.wat, x.qt, x.ka, x.vt, x.kt, x.va)
            return carry
        lax.fori_loop(0, sb, first, 0)

    def forward_step(q, carry):
        @pl.when(mine)
        def _():
            forward_tiles(q, half, x.qt, x.ka, x.vt, x.acc)
            for b, i in enumerate(rows_at(q, half)):
                for h in range(3):
                    a = x.acc[h, b]
                    v = a[0:64] / a[64:65]
                    x.cf[i, h * 64:h * 64 + 64, :] = v
                    x.lsum[i, h:h + 1, :] = a[64:65]
                    vb = v.astype(BF)
                    x.csend[2 * i, h * 64:h * 64 + 64, :] = vb[:, 0:128]
                    x.csend[2 * i + 1, h * 64:h * 64 + 64, :] = vb[:, 128:256]
                give(x.csend, x.crecv, x.css, x.crs, 2 * i, True)
                give(x.csend, x.crecv, x.css, x.crs, 2 * i + 1, True)
        if fast:
            for j in range(3):
                @pl.when(q == j)
                def _():
                    pass_on(j)
        return carry
    lax.fori_loop(0, half, forward_step, 0)
    @pl.when(mine)
    def _():
        x.dk[...] = jnp.zeros_like(x.dk)
        x.dv[...] = jnp.zeros_like(x.dv)

    if fast:
        for cp in fetch:
            cp.wait()
        for j in range(3):
            relay(j).wait_recv()
        chains = {k: Chain(o, f, c, [getattr(x, k + s) for s in ("b", "1", "2", "3", "4", "o", "ss", "rs")]) for k, o in ORDER.items()}
    def slot(s):
        for k, at in SCHEDULE.items():
            for i in range(7):
                if fast and at[i] == s:
                    chains[k].step(i + 1)
    pad_weights(x.wint, x.wffo, x.wip, x.wfp)
    taken(x.csend, x.crecv, x.crs)
    def send_dct():
        spread(x.dsend, x.dc, x.dss, x.drs, True)
    dense_body(MICRO * 128, x, send_dct, chains if fast else None, slot)

    if fast:
        slot(1)
    else:
        x.gw[...] = jnp.zeros_like(x.gw)
        x.gb[...] = jnp.zeros_like(x.gb)

    def backward_step(q, carry):
        @pl.when(mine)
        def _():
            for b, i in enumerate(rows_at(q, half)):
                arrived(x.dsend, x.dc, x.drs, 2 * i)
                arrived(x.dsend, x.dc, x.drs, 2 * i + 1)
                d = jnp.concatenate([x.dc[2 * i], x.dc[2 * i + 1]], axis=1).astype(F32)
                for h in range(3):
                    dh = d[h * 64:h * 64 + 64]
                    inv = 1.0 / x.lsum[i, h:h + 1, :]
                    delta = jnp.sum(dh * x.cf[i, h * 64:h * 64 + 64, :], axis=0, keepdims=True) * inv
                    dnt[h, i] = jnp.concatenate([dh * inv, jnp.where(iota((16, 256), 0) == 0, -delta, 0.0)], axis=0).astype(BF)
            backward_tiles(q, half, x.qt, x.ka, x.kt, x.va, dnt, x.dq, x.dk, x.dv)
            for b, i in enumerate(rows_at(q, half)):
                for h in range(3):
                    x.dqt[i, h * 64:h * 64 + 64, :] = (x.dq[h, b] * 0.125).astype(BF)
        if fast:
            for k in range(4):
                @pl.when(q == k)
                def _():
                    slot(2 * k + 3)
        return carry
    lax.fori_loop(0, half, backward_step, 0)

    xsend = x.csend
    def grads_at(i):
        k = jnp.concatenate([x.dk[h, i] for h in range(3)], axis=0).astype(BF)
        v = jnp.concatenate([x.dv[h, i] for h in range(3)], axis=0).astype(BF)
        return x.dqt[i], k, v
    @pl.when(mine)
    def _():
        for t in range(n):
            give(x.csend, x.crecv, x.css, x.crs, t, False)
        def post(i, carry):
            q, k, v = grads_at(i)
            x2 = (mm(x.w[0], q) + mm(x.w[1], k) + mm(x.w[2], v)).astype(BF)
            xsend[2 * i] = x2[:, 0:128]
            xsend[2 * i + 1] = x2[:, 128:256]
            give(xsend, x.xrecv, x.xss, x.xrs, 2 * i, True)
            give(xsend, x.xrecv, x.xss, x.xrs, 2 * i + 1, True)
            return carry
        lax.fori_loop(0, sb, post, 0)
    @pl.when(mine)
    def _():
        x.gacc[...] = jnp.zeros_like(x.gacc)
        x.gbacc[...] = jnp.zeros_like(x.gbacc)
        ones = jnp.ones((8, 256), BF)
        def weigh(i, carry):
            xb = jnp.concatenate([x.xt[2 * i, 0:GW, :], x.xt[2 * i + 1, 0:GW, :]], axis=1)
            q, k, v = grads_at(i)
            x.gacc[0] += mm(xb, q, NT)
            x.gacc[1] += mm(xb, k, NT)
            x.gacc[2] += mm(xb, v, NT)
            x.gbacc[0] += mm(ones, q, NT)
            x.gbacc[1] += mm(ones, v, NT)
            return carry
        lax.fori_loop(0, sb, weigh, 0)
        if fast:
            low = iota((96, 64), 0)
            bb = jnp.zeros((96, 64), F32)
            for k in range(2):
                for i in range(3):
                    bb = jnp.where(low == 3 * k + i, x.gbacc[k, 0:1, i * 64:i * 64 + 64], bb)
            for h in range(2):
                cat = jnp.concatenate([x.gacc[k, h * 96:h * 96 + 96, :] for k in range(3)] + [bb], axis=1).astype(BF)
                for s in range(5):
                    x.qs[h, s * 96:s * 96 + 96, :] = cat[:, s * 128:s * 128 + 128]
        else:
            for k in range(4):
                @pl.when(g == k)
                def _():
                    x.gw[:, :, k * GW:k * GW + GW] = x.gacc[...].astype(BF)
                    x.gb[0:1, k * GW:k * GW + GW] = x.gbacc[0, 0:1]
                    x.gb[1:2, k * GW:k * GW + GW] = x.gbacc[1, 0:1]

    if fast:
        def to_sum(h, t):
            return remote_copy(x.qs.at[h, pl.ds(t * 160, 160)], x.qr.at[f * 3 + m], x.qss.at[h * 3 + t], x.qrs.at[f * 3 + m], h, place_at(g, t))
        def stay():
            return pltpu.make_async_copy(x.qs.at[f, pl.ds(m * 160, 160)], x.qr.at[f * 3 + m], x.qrs.at[f * 3 + m])
        def place_at(g, t):
            return g * 4 + t + lax.rem(g, 2)
        def to_all(d):
            return remote_copy(x.qb.at[u], x.qb.at[u], x.qbs.at[d], x.qbr.at[u], f, lax.rem(c + 2 * d, n))
        def hand_over(k):
            return remote_copy(x.qb.at[k], x.qb.at[k], x.qbx.at[k], x.qbr.at[k], f, sib)
        def elsewhere(h, t):
            return (f != h) | (m != t)
        @pl.when(mine)
        def _():
            for h in range(2):
                for t in range(3):
                    @pl.when(elsewhere(h, t))
                    def _():
                        to_sum(h, t).start()
            stay().start()
    if fast:
        slot(10)
        @pl.when(mine)
        def _():
            for h in range(2):
                for t in range(3):
                    @pl.when(elsewhere(h, t))
                    def _():
                        remote_copy(x.qs.at[0, pl.ds(0, 160)], x.qr.at[h * 3 + t], x.ls, x.qrs.at[h * 3 + t], h, place_at(g, t)).wait_recv()
            stay().wait()
            x.qb[u] = sum(x.qr[k].astype(F32) for k in range(6)).astype(BF)
            for d in range(1, n // 2):
                to_all(d).start()
        slot(11)
        for k in range(12):
            @pl.when((r == own[k] % 2) & (c != own[k]))
            def _():
                remote_copy(x.qb.at[k], x.qb.at[k], x.ls, x.qbr.at[k], f, own[k]).wait_recv()
            @pl.when(r == own[k] % 2)
            def _():
                hand_over(k).start()

    taken(xsend, x.xrecv, x.xrs)
    if fast:
        for k in range(12):
            @pl.when(r != own[k] % 2)
            def _():
                hand_over(k).wait_recv()
        for s in range(12, 16):
            slot(s)
        for k in "ABC":
            chains[k].sent()
        vectors().wait_send()
        for j in range(3):
            half_over(j).wait_send()
            relay(j).wait_send()
        @pl.when(mine)
        def _():
            for j in range(3):
                window(j, 0).wait_send()
            for h in range(2):
                for t in range(3):
                    @pl.when(elsewhere(h, t))
                    def _():
                        to_sum(h, t).wait_send()
            for d in range(1, n // 2):
                to_all(d).wait_send()
        for k in range(12):
            @pl.when(r == own[k] % 2)
            def _():
                hand_over(k).wait_send()
    else:
        for k in range(MICRO):
            t = jnp.concatenate([x.xrecv[k * 4 + j] for j in range(4)], axis=0).astype(F32)
            s = slice(k * 128, k * 128 + 128)
            x.grad[s, :] = (jnp.transpose(t) + x.d1[s, :]).astype(BF)
    spread(x.tsend, x.xt, x.tss, x.trs, False)
    spread(x.dsend, x.dc, x.dss, x.drs, False)
    @pl.when(mine)
    def _():
        for t in range(n):
            give(xsend, x.xrecv, x.xss, x.xrs, t, False)


DMA = pltpu.SemaphoreType.DMA
S, V = jax.ShapeDtypeStruct, pltpu.VMEM


def common_scratch(n):
    rows, sb = MICRO * 128, n // 2
    return dict(
        tsend=V((12, CH, 128), BF), xt=V((n, CH, 128), BF), csend=V((n, GW, 128), BF), crecv=V((12, GW, 128), BF),
        dsend=V((12, GW, 128), BF), dc=V((n, GW, 128), BF),
        w=V((3, GW, GW), BF), bias=V((8, GW), F32), wa=V((3, XA, 384), BF), wat=V((3, 384, XA), BF),
        qt=V((3, sb, 128, 256), BF), ka=V((3, sb, 256, 128), BF), vt=V((3, sb, 80, 256), BF), kt=V((3, sb, 64, 256), BF), va=V((3, sb, 256, 128), BF),
        cf=V((sb, GW, 256), F32), lsum=V((sb, 8, 256), F32), acc=V((3, 2, 80, 256), F32), dq=V((3, 2, 64, 256), F32),
        dk=V((3, sb, 64, 256), F32), dv=V((3, sb, 64, 256), F32), dqt=V((sb, GW, 256), BF), gacc=V((3, GW, GW), F32), gbacc=V((2, 8, GW), F32),
        ctx=V((rows, D), BF), xh=V((rows, D), F32), n1b=V((rows, D), BF), wip=V((4, 256, D), BF), wfp=V((4, D, 256), BF), dpre=V((4, rows, D), BF),
        hid=V((4, rows, D), BF), br=V((rows, D), F32), dn=V((rows, D), F32), db=V((rows, D), BF), st=V((rows, 128), F32),
        tss=DMA((12,)), trs=DMA((n,)), css=DMA((n,)), crs=DMA((12,)), dss=DMA((12,)), drs=DMA((n,)), xss=DMA((n,)), xrs=DMA((12,)), ls=DMA)


class Refs:
    def __init__(self, **k):
        self.__dict__.update(k)


def call(n, fast, ins, outs, scratch, far):
    names, onames = list(ins), list(outs)
    def kernel(*a):
        refs = dict(zip(names, a[:len(names)]))
        refs.update(zip(onames, a[len(names):len(names) + len(onames)]))
        refs.update(a[-1])
        mega(n, fast, Refs(**refs))
    vm = pl.BlockSpec(memory_space=pltpu.VMEM)
    got = pl.pallas_call(
        kernel, out_shape=tuple(outs.values()),
        in_specs=[pl.BlockSpec(memory_space=pl.ANY) if k in far else vm for k in names], out_specs=(vm,) * len(onames),
        scratch_shapes=[scratch],
        compiler_params=pltpu.CompilerParams(collective_id=0, has_side_effects=True, vmem_limit_bytes=60 * 2**20))(*ins.values())
    return dict(zip(onames, got))


def run_whole(n, ins):
    rows = MICRO * 128
    outs = dict(out=S((rows, D), BF), grad=S((rows, D), BF), gw=S((3, GW, D), BF), gb=S((8, D), F32), ga=S((D, D), BF), gi=S((192, FF), BF),
                gf=S((D, D), BF), gv=S((16, D), F32))
    scratch = common_scratch(n)
    scratch.update(xrecv=V((12, GW, 128), BF), d1=V((rows, D), F32))
    return call(n, False, ins, outs, scratch, ())


def run_fast(n, ins):
    rows = MICRO * 128
    outs = dict(out=S((rows, D), BF), xrecv=S((12, GW, 128), BF), d1=S((rows, D), F32), qb=S((12, 160, 128), BF))
    for k in "ABC":
        outs[k + "o"] = S((2, 2, 4, LEN[k], 128), BF)
    scratch = common_scratch(n)
    scratch.update(cot=V((rows, D), BF), wout=V((D, D), BF), wint=V((192, FF), BF), wffo=V((D, D), BF), vec=V((16, D), F32), vbuf=V((2, 16, 384), BF),
                   qrem=V((3, 96, 256), BF), gv=V((16, D), F32), qs=V((2, 480, 128), BF), qr=V((6, 160, 128), BF),
                   lsem=DMA((4,)), wss=DMA((10,)), wrs=DMA((10,)), qss=DMA((6,)), qrs=DMA((6,)), qbs=DMA((n,)), qbr=DMA((12,)), qbx=DMA((12,)))
    for k in "ABC":
        l = LEN[k]
        scratch[k + "b"] = V((2, 2, 2, 4, l, 128), BF)
        scratch[k + "1"] = V((2, 2, 4, l, 128), BF)
        scratch[k + "2"] = V((2, l, 128) if ORDER[k] == "zyx" else (2, 4, l, 128), BF)
        scratch[k + "3"] = V((l, 128) if ORDER[k] == "zyx" else (4, l, 128), BF)
        scratch[k + "4"] = V((4, 2, 2, l, 128) if ORDER[k] == "zyx" else (4, l, 128), BF)
        scratch[k + "ss"] = DMA((11,))
        scratch[k + "rs"] = DMA((11,))
    return call(n, True, ins, outs, scratch, ("wo", "wi", "wf", "cot_in"))


def finish(out, xrecv, d1, qb, a, b, c, o_out, o_grad, o_q, o_k, o_v, o_qb, o_vb, o_w, o_b, o_g1, o_s1, o_i, o_ib, o_f, o_fb, o_g2, o_s2):
    f = lax.axis_index("fsdp")
    o_out[...] = out[...]
    for k in range(MICRO):
        t = jnp.concatenate([xrecv[k * 4 + j] for j in range(4)], axis=0).astype(F32)
        s = slice(k * 128, k * 128 + 128)
        o_grad[s, :] = (jnp.transpose(t) + d1[s, :]).astype(BF)
    def slab(ref, base, rows):
        got = [ref[b // 8, (b // 4) % 2, b % 4, w:w + size, :] for b, w, _, size in pieces(base, rows)]
        return jnp.concatenate(got, axis=0).astype(F32) if len(got) > 1 else got[0].astype(F32)
    for s in range(6):
        o_w[:, s * 128:s * 128 + 128] = slab(a, s * 384, 384)
    for s in range(24):
        o_i[:, s * 128:s * 128 + 128] = slab(b, s * 96, 96)
    for s in range(3):
        o_f[s * 128:s * 128 + 128, :] = jnp.transpose(slab(c, s * 768, 768))
    cats, qbs, vbs = [], [], []
    for g in range(4):
        rows = jnp.concatenate([qb[t * 4 + g] for t in range(3)], axis=0).astype(F32)
        cat = jnp.concatenate([rows[s * 96:s * 96 + 96] for s in range(5)], axis=1)
        cats.append(cat)
        qbs.append(jnp.concatenate([cat[i:i + 1, 576:640] for i in range(3)], axis=1))
        vbs.append(jnp.concatenate([cat[3 + i:4 + i, 576:640] for i in range(3)], axis=1))
    for k, o in enumerate((o_q, o_k, o_v)):
        o[...] = jnp.concatenate([cat[:, k * GW:k * GW + GW] for cat in cats], axis=1)
    pick = lambda v: jnp.where(f == 0, jnp.concatenate(v[0:2], axis=1), jnp.concatenate(v[2:4], axis=1))
    o_qb[...] = pick(qbs).reshape(384)
    o_vb[...] = pick(vbs).reshape(384)
    rows = []
    for k in range(30):
        b = k // 2
        rows.append(a[b // 8, (b // 4) % 2, b % 4, 144:160, :].astype(F32)[k % 2:k % 2 + 1, :])
    for i, o in enumerate((o_b, o_g1, o_s1, o_fb, o_g2, o_s2)):
        o[...] = jnp.concatenate(rows[3 * i:3 * i + 3], axis=1).reshape(384)
    o_ib[...] = jnp.concatenate(rows[18:30], axis=1).reshape(1536)


def local(tokens, cotangent, segment_ids, q_weight, key_weight, value_weight, q_bias, value_bias, out_weight, out_bias,
          norm1_gain, norm1_bias, inter_weight, inter_bias, ffo_weight, ffo_bias, norm2_gain, norm2_bias):
    n, nf = lax.axis_size("ctx"), lax.axis_size("fsdp")
    rows = MICRO * 128
    tok, cot, seg = tokens.reshape(rows, D), cotangent.reshape(rows, D), segment_ids
    dl = q_bias.shape[0]
    if n == 16 and nf == 2:
        x = run_fast(n, dict(tok=tok, seg=seg, cot_in=cot, wq=q_weight, wk=key_weight, wv=value_weight, wo=out_weight, wi=inter_weight, wf=ffo_weight,
                             out_bias=out_bias, norm1_gain=norm1_gain, norm1_bias=norm1_bias, ffo_bias=ffo_bias, norm2_gain=norm2_gain,
                             norm2_bias=norm2_bias, q_bias=q_bias, value_bias=value_bias, inter_bias=inter_bias))
        vm = pl.BlockSpec(memory_space=pltpu.VMEM)
        row = S((dl,), F32)
        outs = (S((rows, D), BF), S((rows, D), BF)) + (S((96, D), F32),) * 3 + (row, row, S((384, D), F32), row, row, row, S((96, FF), F32), S((4 * dl,), F32),
                S((384, D), F32), row, row, row)
        got = pl.pallas_call(
            finish, out_shape=outs, in_specs=[vm] * 7, out_specs=(vm,) * 17,
            compiler_params=pltpu.CompilerParams(vmem_limit_bytes=60 * 2**20))(x["out"], x["xrecv"], x["d1"], x["qb"], x["Ao"], x["Bo"], x["Co"])
        return (got[0].reshape(tokens.shape), got[1].reshape(tokens.shape)) + tuple(got[2:])
    gather = lambda a, ax: lax.all_gather(a, "fsdp", axis=ax, tiled=True)
    pack = jnp.concatenate([out_bias, norm1_gain, norm1_bias, ffo_bias, norm2_gain, norm2_bias, q_bias, value_bias, inter_bias]).reshape(12, dl)
    wqkv = gather(jnp.stack([q_weight, key_weight, value_weight]), 1)
    allv = lax.all_gather(pack, "fsdp", axis=0)
    vec = jnp.concatenate([jnp.swapaxes(allv[:, 0:8], 0, 1).reshape(8, D), allv[:, 8:12].reshape(4, D), jnp.zeros((4, D), BF)], axis=0).astype(F32)
    x = run_whole(n, dict(tok=tok, seg=seg, cot=cot, wqkv=wqkv, wout=gather(out_weight, 0), wint=gather(inter_weight, 0), wffo=gather(ffo_weight, 0), vec=vec))
    gw, gv = x["gw"], x["gv"]
    scatter = lambda a: lax.psum(lax.psum_scatter(a, "fsdp", scatter_dimension=0, tiled=True), "ctx").astype(F32)
    gvec = lax.psum(jnp.concatenate([gv, x["gb"]], axis=0), ("fsdp", "ctx"))
    me = lax.axis_index("fsdp")
    part = lambda i: lax.dynamic_slice(gvec[i], (me * dl,), (dl,))
    gib = lax.dynamic_slice(gvec[8:12].reshape(4 * D), (me * 4 * dl,), (4 * dl,))
    return (x["out"].reshape(tokens.shape), x["grad"].reshape(tokens.shape), scatter(gw[0]), scatter(gw[1]), scatter(gw[2]), part(16), part(17),
            scatter(x["ga"]), part(0), part(1), part(2), scatter(x["gi"]), gib, scatter(x["gf"].T), part(3), part(4), part(5))


def solution(mesh):
    act, seg, mat, vec = P(None, "fsdp", "ctx", None), P(None, "fsdp", "ctx"), P("fsdp", None), P("fsdp")
    return jax.shard_map(
        local, mesh=mesh,
        in_specs=(act, act, seg, mat, mat, mat, vec, vec, mat, vec, vec, vec, mat, vec, mat, vec, vec, vec),
        out_specs=(act, act, mat, mat, mat, vec, vec, mat, vec, vec, vec, mat, vec, mat, vec, vec, vec),
        check_vma=False)
```

```python
import math

import jax
import jax.numpy as jnp
from jax import lax
from jax.experimental import pallas as pl
from jax.experimental.pallas import tpu as pltpu
from jax.sharding import PartitionSpec as P

MESH = pl.DeviceIdType.MESH
MICRO = 3


def place(n, g, m):
    return g * (n // 4) + m + (g % 2)


def owners(n):
    return [place(n, g, m) for m in range(MICRO) for g in range(4)]


def unit_of(c, n):
    g = c // (n // 4)
    m = c - g * (n // 4) - lax.rem(g, 2)
    return g, m, (m >= 0) & (m < MICRO)


BF, F32 = jnp.bfloat16, jnp.float32
HEAD, GW = 64, 192
CH = 208
XA = 240
BIG = 1e9
NN = (((1,), (0,)), ((), ()))
NT = (((1,), (1,)), ((), ()))
TN = (((0,), (0,)), ((), ()))

def mm(a, b, dims=NN):
    return lax.dot_general(a, b, dims, preferred_element_type=F32)

def iota(shape, axis):
    return lax.broadcasted_iota(jnp.int32, shape, axis)

def build_weights(w_ref, b_ref, wa_ref, wat_ref):
    for s in range(3):
        for h in range(3):
            w = w_ref[s, :, h * 64:h * 64 + 64].astype(F32)
            top = jnp.concatenate([w * (0.125 if s == 0 else 1.0), jnp.zeros((GW, 64), F32)], axis=1)
            r, c = iota((48, 128), 0), iota((48, 128), 1)
            same = (c - 64 == r)
            lanes = (c >= 64) & (c < 96) & (r < 32)
            one = (r == 32)
            zero = jnp.zeros((48, 128), F32)
            if s == 0:
                bias = jnp.concatenate([b_ref[0:1, h * 64:h * 64 + 64].astype(F32) * 0.125, jnp.zeros((1, 64), F32)], axis=1)
                low = jnp.where(lanes & same, 1.0, zero) + jnp.where(one, bias, zero)
            elif s == 1:
                low = jnp.where(lanes & ~same, -BIG, zero) + jnp.where(one & (c == 96), 1.0, zero)
            else:
                bias = jnp.concatenate([b_ref[1:2, h * 64:h * 64 + 64].astype(F32), jnp.zeros((1, 64), F32)], axis=1)
                low = jnp.where(one, bias, zero) + jnp.where(one & (c == 64), 1.0, zero)
            full = jnp.concatenate([top, low], axis=0)
            wa_ref[s, :, h * 128:h * 128 + 128] = full.astype(BF)
            wat_ref[s, h * 128:h * 128 + 128, :] = jnp.transpose(full).astype(BF)

D, FF = 768, 3072
EPS = 1e-12
WIN = (0, 128, 384, 512)
OFF = (0, 64, 0, 64)
RS2 = math.sqrt(0.5)
IPI = 1.0 / math.sqrt(2.0 * math.pi)
CK = 128

def rowmean(x):
    return jnp.sum(x, axis=-1, keepdims=True) * (1.0 / D)

def tall(ref, m):
    return jnp.concatenate([ref[m * 4 + g] for g in range(4)], axis=0)


def pad_weights(wint, wffo, wip, wfp):
    for j in range(4):
        o = OFF[j]
        wip[j] = jnp.zeros((256, D), BF)
        wip[j, o:o + 192, :] = wint[:, j * D:(j + 1) * D]
        lane = iota((D, 256), 1)
        w = wffo[:, WIN[j]:WIN[j] + 256]
        wfp[j] = jnp.where((lane >= o) & (lane < o + 192), w.astype(F32), 0.0).astype(BF)


def dense_body(rows, x, send, chains, slot):
    tok, cot, ctxt, wout, out, d1, dct, gv = x.tok, x.cot, x.crecv, x.wout, x.out, x.d1, x.dsend, x.gv
    ctx, attn, n1b, wip, wfp, dpre, hid, br, dn, db, st = x.ctx, x.xh, x.n1b, x.wip, x.wfp, x.dpre, x.hid, x.br, x.dn, x.db, x.st
    da = ctx
    nm = rows // 128
    v = lambda i: x.vec[i:i + 1, :]
    for m in range(nm):
        ctx[m * 128:(m + 1) * 128, :] = jnp.transpose(tall(ctxt, m))
    attn[...] = mm(ctx[...], wout[...])
    def ln1(t, c):
        s = pl.ds(pl.multiple_of(t * CK, CK), CK)
        r = attn[s, :] + v(0) + tok[s, :].astype(F32)
        cen = r - rowmean(r)
        rstd = lax.rsqrt(rowmean(cen * cen) + EPS)
        xh = cen * rstd
        attn[s, :] = xh
        st[s, :] = jnp.broadcast_to(rstd, (CK, 128))
        n = xh * v(1) + v(2)
        n1b[s, :] = n.astype(BF)
        br[s, :] = n + v(3)
        return c
    lax.fori_loop(0, rows // CK, ln1, 0)
    for j in range(4):
        for s in (slice(0, rows),):
            u = mm(n1b[s, WIN[j]:WIN[j] + 256], wip[j]) + v(8 + j)
            half = 0.5 + 0.5 * lax.erf(u * RS2)
            hid[j, s, :] = (u * half).astype(BF)
            dpre[j, s, :] = (half + u * (jnp.exp(u * u * -0.5) * IPI)).astype(BF)
        br[:, WIN[j]:WIN[j] + 256] += mm(hid[j], wfp[j])
    gv[...] = jnp.zeros_like(gv)
    def ln2(t, c):
        s = pl.ds(pl.multiple_of(t * CK, CK), CK)
        r = br[s, :]
        cen = r - rowmean(r)
        rstd = lax.rsqrt(rowmean(cen * cen) + EPS)
        xh = cen * rstd
        out[s, :] = (xh * v(4) + v(5)).astype(BF)
        ct = cot[s, :].astype(F32)
        u = ct * v(4)
        dd = rstd * (u - rowmean(u) - xh * rowmean(u * xh))
        dn[s, :] = dd
        ddb = dd.astype(BF)
        db[s, :] = ddb
        gv[4:5, :] += jnp.sum(ct * xh, axis=0, keepdims=True)
        gv[5:6, :] += jnp.sum(ct, axis=0, keepdims=True)
        gv[3:4, :] += jnp.sum(ddb.astype(F32), axis=0, keepdims=True)
        return c
    lax.fori_loop(0, rows // CK, ln2, 0)
    dbt = jnp.transpose(db[...])
    for j in range(4):
        o = WIN[j] + OFF[j]
        val = mm(dbt[o:o + 192, :], hid[j])
        if chains is None:
            x.gf[j * 192:(j + 1) * 192, :] = val.astype(BF)
            continue
        for f in range(2):
            for s in range(3):
                at = f * 384 + s * 128
                put(x.Cb, f, s * 768 + j * 192, val[:, at:at + 128])
    if chains is not None:
        chains["C"].step(0)
    for j in range(4):
        for s in (slice(0, rows),):
            dh = mm(db[s, WIN[j]:WIN[j] + 256], wfp[j], NT)
            dp = (dh * dpre[j, s, :].astype(F32)).astype(BF)
            dpre[j, s, :] = dp
            gv[8 + j:9 + j, :] += jnp.sum(dp.astype(F32), axis=0, keepdims=True)
        dn[:, WIN[j]:WIN[j] + 256] += mm(dpre[j], wip[j], NT)
    nt = jnp.transpose(n1b[...])
    for j in range(4):
        o = WIN[j] + OFF[j]
        val = mm(nt[o:o + 192, :], dpre[j])
        if chains is None:
            x.gi[:, j * D:(j + 1) * D] = val.astype(BF)
            continue
        for f in range(2):
            for s in range(6):
                put(x.Bb, f, (j * 6 + s) * 96, val[f * 96:f * 96 + 96, s * 128:s * 128 + 128])
    if chains is not None:
        chains["B"].step(0)
    slot(0)
    def lnb(t, c):
        s = pl.ds(pl.multiple_of(t * CK, CK), CK)
        g = dn[s, :]
        xh = attn[s, :]
        u = g * v(1)
        dd = st[s, 0:1] * (u - rowmean(u) - xh * rowmean(u * xh))
        d1[s, :] = dd
        ddb = dd.astype(BF)
        da[s, :] = ddb
        gv[1:2, :] += jnp.sum(g * xh, axis=0, keepdims=True)
        gv[2:3, :] += jnp.sum(g, axis=0, keepdims=True)
        gv[0:1, :] += jnp.sum(ddb.astype(F32), axis=0, keepdims=True)
        return c
    lax.fori_loop(0, rows // CK, lnb, 0)
    dc = mm(wout[...], da[...], NT).astype(BF)
    for m in range(nm):
        for g in range(4):
            dct[m * 4 + g] = dc[g * GW:g * GW + GW, m * 128:(m + 1) * 128]
    send()
    ct = jnp.concatenate([tall(ctxt, m) for m in range(nm)], axis=1)
    if chains is None:
        x.ga[...] = mm(ct, da[...]).astype(BF)
        return
    for s in range(3):
        val = mm(ct, da[:, s * 256:s * 256 + 256])
        for f in range(2):
            for k in range(2):
                put(x.Ab, f, (2 * s + k) * 384, val[f * 384:f * 384 + 384, k * 128:k * 128 + 128])
    low = iota((16, 128), 0)
    for f in range(2):
        for b in range(16):
            two = []
            for k in (2 * b, 2 * b + 1):
                if k < 18:
                    at = f * 384 + (k % 3) * 128
                    two.append(gv[k // 3:k // 3 + 1, at:at + 128])
                elif k < 30:
                    row, at = 8 + 2 * f + (k - 18) // 6, (k - 18) % 6 * 128
                    two.append(gv[row:row + 1, at:at + 128])
                else:
                    two.append(jnp.zeros((1, 128), F32))
            x.Ab[b // 8, f, (b // 4) % 2, b % 4, 144:160, :] = jnp.where(low == 0, two[0], jnp.where(low == 1, two[1], 0.0)).astype(BF)
    chains["A"].step(0)


def remote_copy(src, dst, ssem, rsem, f, c):
    return pltpu.make_async_remote_copy(src_ref=src, dst_ref=dst, send_sem=ssem, recv_sem=rsem, device_id=(f, c), device_id_type=MESH)


VECTORS = ("out_bias", "norm1_gain", "norm1_bias", "ffo_bias", "norm2_gain", "norm2_bias", "q_bias", "value_bias")
ORDER = {"A": "yxz", "B": "yxz", "C": "yxz"}
SCHEDULE = {"C": (0, 1, 3, 5, 7, 9, 10), "B": (1, 3, 5, 7, 9, 10, 11), "A": (1, 5, 7, 9, 10, 11, 12)}
LEN = {"A": 160, "B": 144, "C": 144}


def pieces(base, rows):
    out, at = [], 0
    while at < rows:
        b, w = divmod(base + at, 144)
        size = min(144 - w, rows - at)
        out.append((b, w, at, size))
        at += size
    return out


def put(ref, f, base, val):
    for b, w, at, size in pieces(base, val.shape[0]):
        ref[b // 8, f, (b // 4) % 2, b % 4, w:w + size, :] = val[at:at + size].astype(BF)


class Chain:
    def __init__(self, order, f, c, refs):
        self.order, self.f, self.c = order, f, c
        self.b, self.c1, self.c2, self.c3, self.c4, self.out, self.ss, self.rs = refs
        self.r, self.x, self.z = lax.rem(c, 2), lax.rem(lax.div(c, 2), 2), lax.div(c, 4)
        self.started = []

    def core(self):
        return self.f, self.c + 1 - 2 * self.r

    def along_x(self):
        return self.f, self.c + 2 - 4 * self.x

    def along_z(self, d):
        return self.f, lax.rem(self.c + 4 * d, 16)

    def copy(self, k, src, dst, to):
        return remote_copy(src, dst, self.ss.at[k], self.rs.at[k], *to)

    def moves(self, k):
        b, r, f, x, z, o = self.b, self.r, self.f, self.x, self.z, self.out
        zs = [(d, lax.rem(z + d, 4)) for d in (1, 2, 3)]
        y = (1 - f, self.c)
        if k == 0:
            return [(0, b.at[1 - r], self.c1, self.core())]
        if k == 6:
            return [(4, o.at[r], o.at[r], self.core())]
        if self.order == "yxz":
            return {1: [(1, b.at[r, 1 - f], self.c2, y)],
                    2: [(2, b.at[r, f, 1 - x], self.c3, self.along_x())],
                    3: [(4 + d, b.at[r, f, x, t], self.c4.at[z], self.along_z(d)) for d, t in zs],
                    4: [(7 + d, o.at[r, x, z], o.at[r, x, z], self.along_z(d)) for d, t in zs],
                    5: [(3, o.at[r, x], o.at[r, x], self.along_x())]}[k]
        return {1: [(4 + d, b.at[r, :, :, t], self.c4.at[z], self.along_z(d)) for d, t in zs],
                2: [(1, b.at[r, 1 - f, :, z], self.c2, y)],
                3: [(2, b.at[r, f, 1 - x, z], self.c3, self.along_x())],
                4: [(3, o.at[r, x, z], o.at[r, x, z], self.along_x())],
                5: [(7 + d, o.at[r, :, z], o.at[r, :, z], self.along_z(d)) for d, t in zs]}[k]

    def start(self, k):
        for mv in self.moves(k):
            self.copy(*mv).start()

    def received(self, k):
        for mv in self.moves(k):
            self.copy(*mv).wait_recv()

    def sent(self):
        for k in range(7):
            for mv in self.moves(k):
                self.copy(*mv).wait_send()

    def add(self, k):
        b, r, f, x, z, o = self.b, self.r, self.f, self.x, self.z, self.out
        up = lambda v: v.astype(F32)
        others = [lax.rem(z + 4 - d, 4) for d in (1, 2, 3)]
        if k == 0:
            def one(t, carry):
                i, j, l = t // 8, lax.rem(t // 4, 2), lax.rem(t, 4)
                b[r, i, j, l] = (up(b[r, i, j, l]) + up(self.c1[i, j, l])).astype(BF)
                return carry
            lax.fori_loop(0, 16, one, 0)
        elif self.order == "yxz" and k == 1:
            def one(t, carry):
                j, l = t // 4, lax.rem(t, 4)
                b[r, f, j, l] = (up(b[r, f, j, l]) + up(self.c2[j, l])).astype(BF)
                return carry
            lax.fori_loop(0, 8, one, 0)
        elif self.order == "yxz" and k == 2:
            for l in range(4):
                b[r, f, x, l] = (up(b[r, f, x, l]) + up(self.c3[l])).astype(BF)
        elif self.order == "yxz" and k == 3:
            o[r, x, z] = (up(b[r, f, x, z]) + sum(up(self.c4[t]) for t in others)).astype(BF)
        elif self.order == "zyx" and k == 1:
            for i in range(2):
                for j in range(2):
                    b[r, i, j, z] = (up(b[r, i, j, z]) + sum(up(self.c4[t, i, j]) for t in others)).astype(BF)
        elif self.order == "zyx" and k == 2:
            for j in range(2):
                b[r, f, j, z] = (up(b[r, f, j, z]) + up(self.c2[j])).astype(BF)
        elif self.order == "zyx" and k == 3:
            o[r, x, z] = (up(b[r, f, x, z]) + up(self.c3[...])).astype(BF)

    def step(self, k):
        if k > 0:
            self.received(k - 1)
            self.add(k - 1)
        if k < 7:
            self.start(k)


def tile_at(q, t, half):
    p, mir = lax.rem(q, half // 2), lax.div(q, half // 2)
    b = lax.div(t + half - 1 - p, 2 * half)
    i = p + b * (half - 1 - 2 * p)
    j = t - b * (half + 1 + p)
    last = 2 * half - 1
    return b, i + mir * (last - 2 * i), j + mir * (last - 2 * j)


def rows_at(q, half):
    p, mir = lax.rem(q, half // 2), lax.div(q, half // 2)
    last = 2 * half - 1
    return [i + mir * (last - 2 * i) for i in (p, half - 1 - p)]


def in_parts(half, part):
    count = 3 * half + 1
    if count <= 13:
        part(0, count)
    else:
        size = max(d for d in range(1, 9) if count % d == 0)
        lax.fori_loop(0, count // size, lambda t, carry: (part(t * size, size), carry)[1], 0)


def forward_tiles(q, half, qt, ka, vt, acc):
    acc[...] = jnp.zeros_like(acc)
    def part(first, count):
        items = [(h,) + tile_at(q, first + t, half) for t in range(count) for h in range(3)]
        def front(it):
            h, _, i, j = it
            return mm(ka[h, j], qt[h, i])
        ready = [front(it) for it in items[:3]]
        for t, (h, b, i, j) in enumerate(items):
            if t + 3 < len(items):
                ready.append(front(items[t + 3]))
            e = jnp.exp(ready[t]).astype(BF)
            ready[t] = None
            acc[h, b] += mm(vt[h, j], e)
    in_parts(half, part)


def backward_tiles(q, half, qt, ka, kt, va, dnt, dq, dk, dv):
    dq[...] = jnp.zeros_like(dq)
    def part(first, count):
        items = [(h,) + tile_at(q, first + t, half) for t in range(count) for h in range(3)]
        def front(it):
            h, _, i, j = it
            return mm(ka[h, j], qt[h, i]), mm(va[h, j, :, 0:80], dnt[h, i])
        ready = [front(it) for it in items[:2]]
        for t, (h, b, i, j) in enumerate(items):
            if t + 2 < len(items):
                ready.append(front(items[t + 2]))
            s, dp = ready[t]
            ready[t] = None
            e = jnp.exp(s)
            eb = e.astype(BF)
            ds = (e * dp).astype(BF)
            dq[h, b] += mm(kt[h, j], ds)
            dk[h, j] += mm(qt[h, i, 0:64], ds, NT)
            dv[h, j] += mm(dnt[h, i, 0:64], eb, NT)
    in_parts(half, part)


def prep_block(i, xt, wa, wat, qt, ka, vt, kt, va):
    x = jnp.concatenate([xt[2 * i], xt[2 * i + 1]], axis=1)
    seg = x[GW:GW + 16].astype(F32)[0:1].astype(jnp.int32)
    r = iota((48, 256), 0)
    aug = jnp.where((r == seg) & (r < 32) | (r == 32), 1.0, 0.0).astype(BF)
    xa = jnp.concatenate([x[0:GW], aug], axis=0)
    xn = jnp.transpose(xa)
    q = mm(wat[0], xa).astype(BF)
    k = mm(wat[1], xa).astype(BF)
    v = mm(wat[2], xa).astype(BF)
    kn = mm(xn, wa[1]).astype(BF)
    vn = mm(xn, wa[2]).astype(BF)
    for h in range(3):
        o = h * 128
        qt[h, i] = q[o:o + 128]
        anchor = jnp.sum(q[o:o + 64].astype(F32) * k[o:o + 64].astype(F32), axis=0, keepdims=True)
        qt[h, i, 96:112] = jnp.where(iota((16, 256), 0) == 0, -anchor, 0.0).astype(BF)
        ka[h, i] = kn[:, o:o + 128]
        vt[h, i] = v[o:o + 80]
        kt[h, i] = k[o:o + 64]
        va[h, i] = vn[:, o:o + 128]


def mega(n, fast, x):
    f, c = lax.axis_index("fsdp"), lax.axis_index("ctx")
    g, m, mine = unit_of(c, n)
    u = m * 4 + g
    own = owners(n)
    sb, half = n // 2, n // 4
    r = lax.rem(c, 2)
    tok, dnt = x.tok, x.vt
    bar = pltpu.get_barrier_semaphore()
    for d in range(1, n):
        pl.semaphore_signal(bar, inc=1, device_id=(f, lax.rem(c + d, n)), device_id_type=MESH)
    greeted = n - 1
    if fast:
        for p in range(4):
            pl.semaphore_signal(bar, inc=1, device_id=(1 - f, g * 4 + p), device_id_type=MESH)
        greeted += 4
        fetch = [pltpu.make_async_copy(x.wo, x.wout.at[pl.ds(f * 384, 384)], x.lsem.at[0]),
                 pltpu.make_async_copy(x.wi, x.wint.at[pl.ds(f * 96, 96)], x.lsem.at[1]),
                 pltpu.make_async_copy(x.wf, x.wffo.at[pl.ds(f * 384, 384)], x.lsem.at[2]),
                 pltpu.make_async_copy(x.cot_in, x.cot, x.lsem.at[3])]
        for cp in fetch:
            cp.start()
    for k in range(MICRO):
        t = jnp.transpose(tok[k * 128:k * 128 + 128, :])
        sg = jnp.broadcast_to(x.seg[k].astype(F32), (16, 128)).astype(BF)
        for j in range(4):
            x.tsend[k * 4 + j, 0:GW, :] = t[j * GW:j * GW + GW]
            x.tsend[k * 4 + j, GW:CH, :] = sg
    if fast:
        own_rows = [getattr(x, k)[...].astype(F32).reshape(1, 384) for k in VECTORS]
        inter = x.inter_bias[...].astype(F32).reshape(1, 1536)
        own_rows += [inter[:, k * 384:k * 384 + 384] for k in range(4)]
        x.vbuf[f] = jnp.concatenate(own_rows + [jnp.zeros((4, 384), F32)], axis=0).astype(BF)
    pl.semaphore_wait(bar, greeted)

    def spread(src, dst, ss, rs, start):
        for k in range(12):
            @pl.when(c != own[k])
            def _():
                cp = remote_copy(src.at[k], dst.at[c], ss.at[k], rs.at[c], f, own[k])
                cp.start() if start else cp.wait_send()
            if start:
                @pl.when(c == own[k])
                def _():
                    pltpu.make_async_copy(src.at[k], dst.at[c], rs.at[c]).start()
    def arrived(src, dst, rs, s):
        @pl.when(c != s)
        def _():
            remote_copy(src.at[0], dst.at[s], x.ls, rs.at[s], f, s).wait_recv()
        @pl.when(c == s)
        def _():
            pltpu.make_async_copy(src.at[0], dst.at[s], rs.at[s]).wait()
    def give(src, dst, ss, rs, t, start):
        @pl.when(c != t)
        def _():
            cp = remote_copy(src.at[t], dst.at[u], ss.at[t], rs.at[u], f, t)
            cp.start() if start else cp.wait_send()
        if start:
            @pl.when(c == t)
            def _():
                pltpu.make_async_copy(src.at[t], dst.at[u], rs.at[u]).start()
    def taken(src, dst, rs):
        for k in range(12):
            @pl.when(c != own[k])
            def _():
                remote_copy(src.at[0], dst.at[k], x.ls, rs.at[k], f, own[k]).wait_recv()
            @pl.when(c == own[k])
            def _():
                pltpu.make_async_copy(src.at[0], dst.at[k], rs.at[k]).wait()

    if fast:
        sib = c + 1 - 2 * r
        parts = ((x.wo, x.wout, 384), (x.wi, x.wint, 96), (x.wf, x.wffo, 384))
        def window(j, k):
            return remote_copy((x.wq, x.wk, x.wv)[j].at[:, WIN[k]:WIN[k] + 256], x.qrem.at[j], x.wss.at[6 + j], x.wrs.at[6 + j], 1 - f, c)
        def vectors():
            return remote_copy(x.vbuf.at[f], x.vbuf.at[f], x.wss.at[9], x.wrs.at[9], 1 - f, c)
        def half_over(j):
            src, dst, rows = parts[j]
            h = rows // 2
            return remote_copy(src.at[pl.ds(r * h, h)], dst.at[pl.ds(f * rows + r * h, h)], x.wss.at[j], x.wrs.at[j], 1 - f, c)
        def relay(j, back=False):
            _, dst, rows = parts[j]
            h = rows // 2
            at = pl.ds((1 - f) * rows + r * h, h)
            return remote_copy(dst.at[at], dst.at[at], x.wss.at[3 + j], x.wrs.at[3 + j], f, sib)
        @pl.when(mine)
        def _():
            for k in range(4):
                @pl.when(g == k)
                def _():
                    for j in range(3):
                        window(j, k).start()
        vectors().start()
    spread(x.tsend, x.xt, x.tss, x.trs, True)
    if fast:
        for j in range(3):
            half_over(j).start()
        def pass_on(j):
            half_over(j).wait_recv()
            relay(j).start()

    if fast:
        vectors().wait_recv()
        for k in range(2):
            for j in range(8):
                x.vec[j:j + 1, k * 384:k * 384 + 384] = x.vbuf[k, 0:16, :].astype(F32)[j:j + 1, :]
            for j in range(4):
                row, at = 8 + 2 * k + j // 2, (j % 2) * 384
                x.vec[row:row + 1, at:at + 384] = x.vbuf[k, 0:16, :].astype(F32)[8 + j:9 + j, :]

    @pl.when(mine)
    def _():
        for k in range(4):
            @pl.when(g == k)
            def _():
                lanes = slice(k * GW, k * GW + GW)
                if not fast:
                    x.w[...] = x.wqkv[:, :, lanes]
                else:
                    for j in range(3):
                        window(j, k).wait_recv()
                        for h in range(2):
                            @pl.when(f == h)
                            def _():
                                x.w[j, h * 96:h * 96 + 96, :] = (x.wq, x.wk, x.wv)[j][:, lanes]
                                x.w[j, 96 - h * 96:192 - h * 96, :] = x.qrem[j, :, OFF[k]:OFF[k] + GW]
                x.bias[0:2, :] = x.vec[6:8, lanes]
        build_weights(x.w, x.bias, x.wa, x.wat)
        def first(i, carry):
            arrived(x.tsend, x.xt, x.trs, 2 * i)
            arrived(x.tsend, x.xt, x.trs, 2 * i + 1)
            prep_block(i, x.xt, x.wa, x.wat, x.qt, x.ka, x.vt, x.kt, x.va)
            return carry
        lax.fori_loop(0, sb, first, 0)

    def forward_step(q, carry):
        @pl.when(mine)
        def _():
            forward_tiles(q, half, x.qt, x.ka, x.vt, x.acc)
            for b, i in enumerate(rows_at(q, half)):
                for h in range(3):
                    a = x.acc[h, b]
                    v = a[0:64] / a[64:65]
                    x.cf[i, h * 64:h * 64 + 64, :] = v
                    x.lsum[i, h:h + 1, :] = a[64:65]
                    vb = v.astype(BF)
                    x.csend[2 * i, h * 64:h * 64 + 64, :] = vb[:, 0:128]
                    x.csend[2 * i + 1, h * 64:h * 64 + 64, :] = vb[:, 128:256]
                give(x.csend, x.crecv, x.css, x.crs, 2 * i, True)
                give(x.csend, x.crecv, x.css, x.crs, 2 * i + 1, True)
        if fast:
            for j in range(3):
                @pl.when(q == j)
                def _():
                    pass_on(j)
        return carry
    lax.fori_loop(0, half, forward_step, 0)
    @pl.when(mine)
    def _():
        x.dk[...] = jnp.zeros_like(x.dk)
        x.dv[...] = jnp.zeros_like(x.dv)

    if fast:
        for cp in fetch:
            cp.wait()
        for j in range(3):
            relay(j).wait_recv()
        chains = {k: Chain(o, f, c, [getattr(x, k + s) for s in ("b", "1", "2", "3", "4", "o", "ss", "rs")]) for k, o in ORDER.items()}
    def slot(s):
        for k, at in SCHEDULE.items():
            for i in range(7):
                if fast and at[i] == s:
                    chains[k].step(i + 1)
    pad_weights(x.wint, x.wffo, x.wip, x.wfp)
    taken(x.csend, x.crecv, x.crs)
    def send_dct():
        spread(x.dsend, x.dc, x.dss, x.drs, True)
    dense_body(MICRO * 128, x, send_dct, chains if fast else None, slot)

    if fast:
        slot(1)
    else:
        x.gw[...] = jnp.zeros_like(x.gw)
        x.gb[...] = jnp.zeros_like(x.gb)

    def backward_step(q, carry):
        @pl.when(mine)
        def _():
            for b, i in enumerate(rows_at(q, half)):
                arrived(x.dsend, x.dc, x.drs, 2 * i)
                arrived(x.dsend, x.dc, x.drs, 2 * i + 1)
                d = jnp.concatenate([x.dc[2 * i], x.dc[2 * i + 1]], axis=1).astype(F32)
                for h in range(3):
                    dh = d[h * 64:h * 64 + 64]
                    inv = 1.0 / x.lsum[i, h:h + 1, :]
                    delta = jnp.sum(dh * x.cf[i, h * 64:h * 64 + 64, :], axis=0, keepdims=True) * inv
                    dnt[h, i] = jnp.concatenate([dh * inv, jnp.where(iota((16, 256), 0) == 0, -delta, 0.0)], axis=0).astype(BF)
            backward_tiles(q, half, x.qt, x.ka, x.kt, x.va, dnt, x.dq, x.dk, x.dv)
            for b, i in enumerate(rows_at(q, half)):
                for h in range(3):
                    x.dqt[i, h * 64:h * 64 + 64, :] = (x.dq[h, b] * 0.125).astype(BF)
        if fast:
            for k in range(4):
                @pl.when(q == k)
                def _():
                    slot(2 * k + 3)
        return carry
    lax.fori_loop(0, half, backward_step, 0)

    xsend = x.csend
    def grads_at(i):
        k = jnp.concatenate([x.dk[h, i] for h in range(3)], axis=0).astype(BF)
        v = jnp.concatenate([x.dv[h, i] for h in range(3)], axis=0).astype(BF)
        return x.dqt[i], k, v
    @pl.when(mine)
    def _():
        for t in range(n):
            give(x.csend, x.crecv, x.css, x.crs, t, False)
        def post(i, carry):
            q, k, v = grads_at(i)
            x2 = (mm(x.w[0], q) + mm(x.w[1], k) + mm(x.w[2], v)).astype(BF)
            xsend[2 * i] = x2[:, 0:128]
            xsend[2 * i + 1] = x2[:, 128:256]
            give(xsend, x.xrecv, x.xss, x.xrs, 2 * i, True)
            give(xsend, x.xrecv, x.xss, x.xrs, 2 * i + 1, True)
            return carry
        lax.fori_loop(0, sb, post, 0)
    @pl.when(mine)
    def _():
        x.gacc[...] = jnp.zeros_like(x.gacc)
        x.gbacc[...] = jnp.zeros_like(x.gbacc)
        ones = jnp.ones((8, 256), BF)
        def weigh(i, carry):
            xb = jnp.concatenate([x.xt[2 * i, 0:GW, :], x.xt[2 * i + 1, 0:GW, :]], axis=1)
            q, k, v = grads_at(i)
            x.gacc[0] += mm(xb, q, NT)
            x.gacc[1] += mm(xb, k, NT)
            x.gacc[2] += mm(xb, v, NT)
            x.gbacc[0] += mm(ones, q, NT)
            x.gbacc[1] += mm(ones, v, NT)
            return carry
        lax.fori_loop(0, sb, weigh, 0)
        if fast:
            low = iota((96, 64), 0)
            bb = jnp.zeros((96, 64), F32)
            for k in range(2):
                for i in range(3):
                    bb = jnp.where(low == 3 * k + i, x.gbacc[k, 0:1, i * 64:i * 64 + 64], bb)
            for h in range(2):
                cat = jnp.concatenate([x.gacc[k, h * 96:h * 96 + 96, :] for k in range(3)] + [bb], axis=1).astype(BF)
                for s in range(5):
                    x.qs[h, s * 96:s * 96 + 96, :] = cat[:, s * 128:s * 128 + 128]
        else:
            for k in range(4):
                @pl.when(g == k)
                def _():
                    x.gw[:, :, k * GW:k * GW + GW] = x.gacc[...].astype(BF)
                    x.gb[0:1, k * GW:k * GW + GW] = x.gbacc[0, 0:1]
                    x.gb[1:2, k * GW:k * GW + GW] = x.gbacc[1, 0:1]

    if fast:
        def to_sum(h, t):
            return remote_copy(x.qs.at[h, pl.ds(t * 160, 160)], x.qr.at[f * 3 + m], x.qss.at[h * 3 + t], x.qrs.at[f * 3 + m], h, place_at(g, t))
        def stay():
            return pltpu.make_async_copy(x.qs.at[f, pl.ds(m * 160, 160)], x.qr.at[f * 3 + m], x.qrs.at[f * 3 + m])
        def place_at(g, t):
            return g * 4 + t + lax.rem(g, 2)
        def to_all(d):
            return remote_copy(x.qb.at[u], x.qb.at[u], x.qbs.at[d], x.qbr.at[u], f, lax.rem(c + 2 * d, n))
        def hand_over(k):
            return remote_copy(x.qb.at[k], x.qb.at[k], x.qbx.at[k], x.qbr.at[k], f, sib)
        def elsewhere(h, t):
            return (f != h) | (m != t)
        @pl.when(mine)
        def _():
            for h in range(2):
                for t in range(3):
                    @pl.when(elsewhere(h, t))
                    def _():
                        to_sum(h, t).start()
            stay().start()
    if fast:
        slot(10)
        @pl.when(mine)
        def _():
            for h in range(2):
                for t in range(3):
                    @pl.when(elsewhere(h, t))
                    def _():
                        remote_copy(x.qs.at[0, pl.ds(0, 160)], x.qr.at[h * 3 + t], x.ls, x.qrs.at[h * 3 + t], h, place_at(g, t)).wait_recv()
            stay().wait()
            x.qb[u] = sum(x.qr[k].astype(F32) for k in range(6)).astype(BF)
            for d in range(1, n // 2):
                to_all(d).start()
        slot(11)
        for k in range(12):
            @pl.when((r == own[k] % 2) & (c != own[k]))
            def _():
                remote_copy(x.qb.at[k], x.qb.at[k], x.ls, x.qbr.at[k], f, own[k]).wait_recv()
            @pl.when(r == own[k] % 2)
            def _():
                hand_over(k).start()

    taken(xsend, x.xrecv, x.xrs)
    if fast:
        for k in range(12):
            @pl.when(r != own[k] % 2)
            def _():
                hand_over(k).wait_recv()
        for s in range(12, 16):
            slot(s)
        for k in "ABC":
            chains[k].sent()
        vectors().wait_send()
        for j in range(3):
            half_over(j).wait_send()
            relay(j).wait_send()
        @pl.when(mine)
        def _():
            for j in range(3):
                window(j, 0).wait_send()
            for h in range(2):
                for t in range(3):
                    @pl.when(elsewhere(h, t))
                    def _():
                        to_sum(h, t).wait_send()
            for d in range(1, n // 2):
                to_all(d).wait_send()
        for k in range(12):
            @pl.when(r == own[k] % 2)
            def _():
                hand_over(k).wait_send()
    else:
        for k in range(MICRO):
            t = jnp.concatenate([x.xrecv[k * 4 + j] for j in range(4)], axis=0).astype(F32)
            s = slice(k * 128, k * 128 + 128)
            x.grad[s, :] = (jnp.transpose(t) + x.d1[s, :]).astype(BF)
    spread(x.tsend, x.xt, x.tss, x.trs, False)
    spread(x.dsend, x.dc, x.dss, x.drs, False)
    @pl.when(mine)
    def _():
        for t in range(n):
            give(xsend, x.xrecv, x.xss, x.xrs, t, False)


DMA = pltpu.SemaphoreType.DMA
S, V = jax.ShapeDtypeStruct, pltpu.VMEM


def common_scratch(n):
    rows, sb = MICRO * 128, n // 2
    return dict(
        tsend=V((12, CH, 128), BF), xt=V((n, CH, 128), BF), csend=V((n, GW, 128), BF), crecv=V((12, GW, 128), BF),
        dsend=V((12, GW, 128), BF), dc=V((n, GW, 128), BF),
        w=V((3, GW, GW), BF), bias=V((8, GW), F32), wa=V((3, XA, 384), BF), wat=V((3, 384, XA), BF),
        qt=V((3, sb, 128, 256), BF), ka=V((3, sb, 256, 128), BF), vt=V((3, sb, 80, 256), BF), kt=V((3, sb, 64, 256), BF), va=V((3, sb, 256, 128), BF),
        cf=V((sb, GW, 256), F32), lsum=V((sb, 8, 256), F32), acc=V((3, 2, 80, 256), F32), dq=V((3, 2, 64, 256), F32),
        dk=V((3, sb, 64, 256), F32), dv=V((3, sb, 64, 256), F32), dqt=V((sb, GW, 256), BF), gacc=V((3, GW, GW), F32), gbacc=V((2, 8, GW), F32),
        ctx=V((rows, D), BF), xh=V((rows, D), F32), n1b=V((rows, D), BF), wip=V((4, 256, D), BF), wfp=V((4, D, 256), BF), dpre=V((4, rows, D), BF),
        hid=V((4, rows, D), BF), br=V((rows, D), F32), dn=V((rows, D), F32), db=V((rows, D), BF), st=V((rows, 128), F32),
        tss=DMA((12,)), trs=DMA((n,)), css=DMA((n,)), crs=DMA((12,)), dss=DMA((12,)), drs=DMA((n,)), xss=DMA((n,)), xrs=DMA((12,)), ls=DMA)


class Refs:
    def __init__(self, **k):
        self.__dict__.update(k)


def call(n, fast, ins, outs, scratch, far):
    names, onames = list(ins), list(outs)
    def kernel(*a):
        refs = dict(zip(names, a[:len(names)]))
        refs.update(zip(onames, a[len(names):len(names) + len(onames)]))
        refs.update(a[-1])
        mega(n, fast, Refs(**refs))
    vm = pl.BlockSpec(memory_space=pltpu.VMEM)
    got = pl.pallas_call(
        kernel, out_shape=tuple(outs.values()),
        in_specs=[pl.BlockSpec(memory_space=pl.ANY) if k in far else vm for k in names], out_specs=(vm,) * len(onames),
        scratch_shapes=[scratch],
        compiler_params=pltpu.CompilerParams(collective_id=0, has_side_effects=True, vmem_limit_bytes=60 * 2**20))(*ins.values())
    return dict(zip(onames, got))


def run_whole(n, ins):
    rows = MICRO * 128
    outs = dict(out=S((rows, D), BF), grad=S((rows, D), BF), gw=S((3, GW, D), BF), gb=S((8, D), F32), ga=S((D, D), BF), gi=S((192, FF), BF),
                gf=S((D, D), BF), gv=S((16, D), F32))
    scratch = common_scratch(n)
    scratch.update(xrecv=V((12, GW, 128), BF), d1=V((rows, D), F32))
    return call(n, False, ins, outs, scratch, ())


def run_fast(n, ins):
    rows = MICRO * 128
    outs = dict(out=S((rows, D), BF), xrecv=S((12, GW, 128), BF), d1=S((rows, D), F32), qb=S((12, 160, 128), BF))
    for k in "ABC":
        outs[k + "o"] = S((2, 2, 4, LEN[k], 128), BF)
    scratch = common_scratch(n)
    scratch.update(cot=V((rows, D), BF), wout=V((D, D), BF), wint=V((192, FF), BF), wffo=V((D, D), BF), vec=V((16, D), F32), vbuf=V((2, 16, 384), BF),
                   qrem=V((3, 96, 256), BF), gv=V((16, D), F32), qs=V((2, 480, 128), BF), qr=V((6, 160, 128), BF),
                   lsem=DMA((4,)), wss=DMA((10,)), wrs=DMA((10,)), qss=DMA((6,)), qrs=DMA((6,)), qbs=DMA((n,)), qbr=DMA((12,)), qbx=DMA((12,)))
    for k in "ABC":
        l = LEN[k]
        scratch[k + "b"] = V((2, 2, 2, 4, l, 128), BF)
        scratch[k + "1"] = V((2, 2, 4, l, 128), BF)
        scratch[k + "2"] = V((2, l, 128) if ORDER[k] == "zyx" else (2, 4, l, 128), BF)
        scratch[k + "3"] = V((l, 128) if ORDER[k] == "zyx" else (4, l, 128), BF)
        scratch[k + "4"] = V((4, 2, 2, l, 128) if ORDER[k] == "zyx" else (4, l, 128), BF)
        scratch[k + "ss"] = DMA((11,))
        scratch[k + "rs"] = DMA((11,))
    return call(n, True, ins, outs, scratch, ("wo", "wi", "wf", "cot_in"))


def finish(out, xrecv, d1, qb, a, b, c, o_out, o_grad, o_q, o_k, o_v, o_qb, o_vb, o_w, o_b, o_g1, o_s1, o_i, o_ib, o_f, o_fb, o_g2, o_s2):
    f = lax.axis_index("fsdp")
    o_out[...] = out[...]
    for k in range(MICRO):
        t = jnp.concatenate([xrecv[k * 4 + j] for j in range(4)], axis=0).astype(F32)
        s = slice(k * 128, k * 128 + 128)
        o_grad[s, :] = (jnp.transpose(t) + d1[s, :]).astype(BF)
    def slab(ref, base, rows):
        got = [ref[b // 8, (b // 4) % 2, b % 4, w:w + size, :] for b, w, _, size in pieces(base, rows)]
        return jnp.concatenate(got, axis=0).astype(F32) if len(got) > 1 else got[0].astype(F32)
    for s in range(6):
        o_w[:, s * 128:s * 128 + 128] = slab(a, s * 384, 384)
    for s in range(24):
        o_i[:, s * 128:s * 128 + 128] = slab(b, s * 96, 96)
    for s in range(3):
        o_f[s * 128:s * 128 + 128, :] = jnp.transpose(slab(c, s * 768, 768))
    cats, qbs, vbs = [], [], []
    for g in range(4):
        rows = jnp.concatenate([qb[t * 4 + g] for t in range(3)], axis=0).astype(F32)
        cat = jnp.concatenate([rows[s * 96:s * 96 + 96] for s in range(5)], axis=1)
        cats.append(cat)
        qbs.append(jnp.concatenate([cat[i:i + 1, 576:640] for i in range(3)], axis=1))
        vbs.append(jnp.concatenate([cat[3 + i:4 + i, 576:640] for i in range(3)], axis=1))
    for k, o in enumerate((o_q, o_k, o_v)):
        o[...] = jnp.concatenate([cat[:, k * GW:k * GW + GW] for cat in cats], axis=1)
    pick = lambda v: jnp.where(f == 0, jnp.concatenate(v[0:2], axis=1), jnp.concatenate(v[2:4], axis=1))
    o_qb[...] = pick(qbs).reshape(384)
    o_vb[...] = pick(vbs).reshape(384)
    rows = []
    for k in range(30):
        b = k // 2
        rows.append(a[b // 8, (b // 4) % 2, b % 4, 144:160, :].astype(F32)[k % 2:k % 2 + 1, :])
    for i, o in enumerate((o_b, o_g1, o_s1, o_fb, o_g2, o_s2)):
        o[...] = jnp.concatenate(rows[3 * i:3 * i + 3], axis=1).reshape(384)
    o_ib[...] = jnp.concatenate(rows[18:30], axis=1).reshape(1536)


def local(tokens, cotangent, segment_ids, q_weight, key_weight, value_weight, q_bias, value_bias, out_weight, out_bias,
          norm1_gain, norm1_bias, inter_weight, inter_bias, ffo_weight, ffo_bias, norm2_gain, norm2_bias):
    n, nf = lax.axis_size("ctx"), lax.axis_size("fsdp")
    rows = MICRO * 128
    tok, cot, seg = tokens.reshape(rows, D), cotangent.reshape(rows, D), segment_ids
    dl = q_bias.shape[0]
    if n == 16 and nf == 2:
        x = run_fast(n, dict(tok=tok, seg=seg, cot_in=cot, wq=q_weight, wk=key_weight, wv=value_weight, wo=out_weight, wi=inter_weight, wf=ffo_weight,
                             out_bias=out_bias, norm1_gain=norm1_gain, norm1_bias=norm1_bias, ffo_bias=ffo_bias, norm2_gain=norm2_gain,
                             norm2_bias=norm2_bias, q_bias=q_bias, value_bias=value_bias, inter_bias=inter_bias))
        vm = pl.BlockSpec(memory_space=pltpu.VMEM)
        row = S((dl,), F32)
        outs = (S((rows, D), BF), S((rows, D), BF)) + (S((96, D), F32),) * 3 + (row, row, S((384, D), F32), row, row, row, S((96, FF), F32), S((4 * dl,), F32),
                S((384, D), F32), row, row, row)
        got = pl.pallas_call(
            finish, out_shape=outs, in_specs=[vm] * 7, out_specs=(vm,) * 17,
            compiler_params=pltpu.CompilerParams(vmem_limit_bytes=60 * 2**20))(x["out"], x["xrecv"], x["d1"], x["qb"], x["Ao"], x["Bo"], x["Co"])
        return (got[0].reshape(tokens.shape), got[1].reshape(tokens.shape)) + tuple(got[2:])
    gather = lambda a, ax: lax.all_gather(a, "fsdp", axis=ax, tiled=True)
    pack = jnp.concatenate([out_bias, norm1_gain, norm1_bias, ffo_bias, norm2_gain, norm2_bias, q_bias, value_bias, inter_bias]).reshape(12, dl)
    wqkv = gather(jnp.stack([q_weight, key_weight, value_weight]), 1)
    allv = lax.all_gather(pack, "fsdp", axis=0)
    vec = jnp.concatenate([jnp.swapaxes(allv[:, 0:8], 0, 1).reshape(8, D), allv[:, 8:12].reshape(4, D), jnp.zeros((4, D), BF)], axis=0).astype(F32)
    x = run_whole(n, dict(tok=tok, seg=seg, cot=cot, wqkv=wqkv, wout=gather(out_weight, 0), wint=gather(inter_weight, 0), wffo=gather(ffo_weight, 0), vec=vec))
    gw, gv = x["gw"], x["gv"]
    scatter = lambda a: lax.psum(lax.psum_scatter(a, "fsdp", scatter_dimension=0, tiled=True), "ctx").astype(F32)
    gvec = lax.psum(jnp.concatenate([gv, x["gb"]], axis=0), ("fsdp", "ctx"))
    me = lax.axis_index("fsdp")
    part = lambda i: lax.dynamic_slice(gvec[i], (me * dl,), (dl,))
    gib = lax.dynamic_slice(gvec[8:12].reshape(4 * D), (me * 4 * dl,), (4 * dl,))
    return (x["out"].reshape(tokens.shape), x["grad"].reshape(tokens.shape), scatter(gw[0]), scatter(gw[1]), scatter(gw[2]), part(16), part(17),
            scatter(x["ga"]), part(0), part(1), part(2), scatter(x["gi"]), gib, scatter(x["gf"].T), part(3), part(4), part(5))


def solution(mesh):
    act, seg, mat, vec = P(None, "fsdp", "ctx", None), P(None, "fsdp", "ctx"), P("fsdp", None), P("fsdp")
    return jax.shard_map(
        local, mesh=mesh,
        in_specs=(act, act, seg, mat, mat, mat, vec, vec, mat, vec, vec, vec, mat, vec, mat, vec, vec, vec),
        out_specs=(act, act, mat, mat, mat, vec, vec, mat, vec, vec, vec, mat, vec, mat, vec, vec, vec),
        check_vma=False)
```
